32 devices in a mesh: sector: 16 (over z, x, core), harm: 2 (over y).
Axes of the slice: x: 2, y: 2, z: 4, core: 2. Of those that a mesh axis runs over, the one named last changes fastest.
Arguments:
- disp: float32 [16, 3, 64, 1024], P('sector', None, 'harm'), may hold values from -0.6 to 0.6
- direction: float32 [16, 3, 64, 1024], P('sector', None, 'harm'), may hold values from -0.6 to 0.6
- stick_state: int32 [16, 128, 1024], P('sector'), may hold values from 0 to 2
- contact_params: float32 [16, 4, 1024], P('sector'), may hold values from 0.3 to 3
- mistuning: float32 [16], replicated, may hold values from 1 to 4
- group_ids: int32 [16], replicated, may hold values from 0 to 3, never falling along the last dimension, each value on 1 to 8 neighbouring positions
- diag_stiff: float32 [64, 16], P('harm'), may hold values from 1 to 10
- cross_stiff: float32 [64, 16], P('harm'), may hold values from -3 to 3
- excitation: float32 [3, 64, 1024, 16], P(None, 'harm', 'sector'), may hold values from -1.8 to 1.8
Outputs:
- residual: float32 [3, 64, 1024, 16], P(None, 'harm', 'sector')
- jvp: float32 [3, 64, 1024, 16], P(None, 'harm', 'sector')
The draws below stay inside these ranges and needn't reach their ends.
Inputs may be any that keep to these rules, and one draw needn't show every extreme that they name: `group_ids`: the sectors of one group are consecutive and ids never fall; each of the 4 groups holds 1 to 8 sectors.
All inputs are finite; a program needn't handle non-finite values.
Results may differ from the reference program's by a relative error of at most 0.0003.
Values sent between devices are 32-bit elements; how exact they have to be, the bound alone decides.
A program may use at most 64 MiB of HBM per device.

```python
import math
import jax
import jax.numpy as jnp
import numpy as np
from jax import lax

COEF = 64
SAMPLES = 128
CH = 3
NODES = 1024
SECTORS = 16
GROUPS = 4


def plant(result, key, smallest, high):
    longest = result.shape.index(max(result.shape))
    spots = []
    for shift in (0, 1):
        where = [jax.random.randint(jax.random.fold_in(key, axis), (), 0, length) for axis, length in enumerate(result.shape)]
        where[longest] = (where[longest] + shift) % result.shape[longest]
        spots.append(tuple(where))
    return result.at[spots[0]].set(smallest).at[spots[1]].set(high)


def block_levels(own_key, extent, split, smallest, high):
    factor_of = 1.0
    for position, parts in split:
        heights = jax.random.uniform(jax.random.fold_in(jax.random.fold_in(own_key, 6), position), (parts,), jnp.float32, smallest / len(split), high / len(split))
        factor_of = factor_of * jnp.repeat(jnp.exp(heights), extent[position] // parts).reshape((-1,) + (1,) * (len(extent) - 1 - position))
    return factor_of


def profile(amount, total, limit, skew):
    weights = [(1 << 20) // math.isqrt(standing ** skew) + 1 for standing in range(2, amount + 1)]
    surplus, given = total - limit - (amount - 1), [1] * (amount - 1)
    while surplus > 0:
        movable = [i for i in range(amount - 1) if given[i] < limit]
        whole, remaining = sum([weights[i] for i in movable]), surplus
        for i in movable:
            more = min(limit - given[i], max(1, remaining * weights[i] // whole), surplus)
            given[i] = given[i] + more
            surplus = surplus - more
    return np.array([limit] + given)


def uneven_parts(key, number_of, total, bound, skew):
    if number_of == 2:
        one = jax.random.randint(key, (), max(1, total - bound), min(bound, total - 1) + 1)
        return jnp.stack([one, total - one])
    sizes = jnp.asarray(profile(number_of, total, bound, skew), jnp.int32)
    pairs = (number_of - 1) // 2
    source_of, sink = sizes[1:1 + 2 * pairs:2], sizes[2:2 + 2 * pairs:2]
    slack = jnp.minimum(source_of - 1, bound - sink)
    passed = jax.random.randint(jax.random.fold_in(key, 1), (pairs,), 0, 1 << 20) % (slack + 1)
    sizes = sizes.at[1:1 + 2 * pairs:2].set(source_of - passed).at[2:2 + 2 * pairs:2].set(sink + passed)
    return sizes[jax.random.permutation(jax.random.fold_in(key, 2), number_of)]


def scatter_about(key, shape, spread, most, shards=(), kind=jnp.bfloat16):
    result = spread * jax.random.normal(key, shape, jnp.float32)
    if shards:
        result = result * block_levels(key, shape, shards, -0.22, 0.18)
    return jnp.clip(result, -most, most).astype(kind)


def setup_inputs(seed: int = 0) -> dict:
    seeds = jax.random.split(jax.random.key(seed), 10)
    disp = scatter_about(seeds[0], (SECTORS, CH, COEF, NODES), 0.1, 0.6, ((0, 16), (2, 2)), jnp.float32)
    direction = scatter_about(seeds[1], (SECTORS, CH, COEF, NODES), 0.1, 0.6, ((0, 16), (2, 2)), jnp.float32)
    stick_state = plant(jax.random.randint(seeds[2], (SECTORS, SAMPLES, NODES), 0, 3), jax.random.fold_in(seeds[2], 1), 0, 2).astype(jnp.int32)
    contact_params = jnp.clip(jnp.exp(math.log(3.0) - 2.3025851 * jax.random.uniform(seeds[3], (SECTORS, 4, NODES), jnp.float32) ** block_levels(seeds[3], (SECTORS, 4, NODES), ((0, 16),), -0.2, 0.2)), 0.3, 3.0)
    mistuning = jnp.clip(jnp.exp(jax.random.uniform(seeds[4], (SECTORS,), jnp.float32, math.log(1.0), math.log(4.0))), 1.0, 4.0)
    group_ids = jnp.searchsorted(jnp.cumsum(uneven_parts(seeds[5], GROUPS, SECTORS, 8, 2)), jnp.arange(SECTORS), side="right").astype(jnp.int32)
    diag_stiff = jnp.clip(jnp.exp(math.log(10.0) - 2.3025851 * jax.random.uniform(seeds[6], (COEF, SECTORS), jnp.float32) ** block_levels(seeds[6], (COEF, SECTORS), ((0, 2),), -0.2, 0.2)), 1.0, 10.0)
    cross_stiff = jnp.clip(jax.random.uniform(seeds[7], (COEF, SECTORS), jnp.float32, -3.0, 3.0) * block_levels(seeds[7], (COEF, SECTORS), ((0, 2),), -0.4, 0.0), -3.0, 3.0)
    excitation = scatter_about(seeds[8], (CH, COEF, NODES, SECTORS), 0.3, 1.8, ((1, 2), (2, 16)), jnp.float32)
    return dict(disp=disp, direction=direction, stick_state=stick_state, contact_params=contact_params, mistuning=mistuning, group_ids=group_ids, diag_stiff=diag_stiff, cross_stiff=cross_stiff, excitation=excitation)


exact_mode = lax.Precision.HIGHEST

def basis_table(coefs, samples):
    coef_index = lax.broadcasted_iota(jnp.int32, (coefs, samples), 0)
    time_index = lax.broadcasted_iota(jnp.int32, (coefs, samples), 1)
    harmonic = coef_index // 2 + 1
    phase = harmonic * time_index % samples
    angle = phase.astype(jnp.float32) * (2.0 * math.pi / samples)
    return jnp.where(coef_index % 2 == 0, jnp.cos(angle), jnp.sin(angle))

def contact_law(gaps, dgaps, states_here, params):
    preload = params[0]
    normal_stiff = params[1]
    tangent_stiff = params[2]
    friction_coef = params[3]
    touching = (states_here != 2).astype(jnp.float32)
    sliding = states_here == 1
    normal = (preload + normal_stiff * gaps[0]) * touching
    dnormal = normal_stiff * dgaps[0] * touching
    radius = jnp.sqrt(gaps[1] * gaps[1] + gaps[2] * gaps[2] + 1.0)
    projected = (gaps[1] * dgaps[1] + gaps[2] * dgaps[2]) / (radius * radius * radius)
    tractions = [normal]
    dtractions = [dnormal]
    for channel in (1, 2):
        stuck = tangent_stiff * gaps[channel]
        dstuck = tangent_stiff * dgaps[channel]
        slipped = friction_coef * normal * gaps[channel] / radius
        dslipped = friction_coef * (dnormal * gaps[channel] / radius + normal * (dgaps[channel] / radius - gaps[channel] * projected))
        tractions.append(jnp.where(sliding, slipped, stuck) * touching)
        dtractions.append(jnp.where(sliding, dslipped, dstuck) * touching)
    return (jnp.stack(tractions), jnp.stack(dtractions))

def hartley(field):

    def per_channel(block):
        spectrum = jnp.fft.fft(block, axis=0)
        return jnp.transpose((spectrum.real - spectrum.imag) / math.sqrt(SECTORS), (1, 2, 0))
    return lax.map(per_channel, jnp.moveaxis(field, 1, 0))

def mirror(field):
    return jnp.roll(jnp.flip(field, -1), 1, -1)

def group_mean(field, group_ids):
    counts = jax.ops.segment_sum(jnp.ones((SECTORS,), jnp.float32), group_ids, num_segments=GROUPS)
    sums = jax.ops.segment_sum(field, group_ids, num_segments=GROUPS)
    return sums[group_ids] / counts[group_ids][:, None, None, None]

def reference(disp, direction, stick_state, contact_params, mistuning, group_ids, diag_stiff, cross_stiff, excitation):
    table = basis_table(COEF, SAMPLES)
    rel_disp = disp - jnp.roll(disp, -1, axis=0)
    rel_dir = direction - jnp.roll(direction, -1, axis=0)
    scale = 2.0 / SAMPLES

    def one_sector(items):
        rel_one, drel_one, states_one, params_one = items
        gaps = jnp.einsum('cjp,jt->ctp', rel_one, table, precision=exact_mode)
        dgaps = jnp.einsum('cjp,jt->ctp', drel_one, table, precision=exact_mode)
        traction, dtraction = contact_law(gaps, dgaps, states_one, params_one)
        load_one = jnp.einsum('ctp,jt->cjp', traction, table, precision=exact_mode) * scale
        dload_one = jnp.einsum('ctp,jt->cjp', dtraction, table, precision=exact_mode) * scale
        return (load_one, dload_one)
    loads, dloads = lax.map(one_sector, (rel_disp, rel_dir, stick_state, contact_params))
    weight = mistuning[:, None, None, None]
    force = loads - jnp.roll(loads, 1, axis=0) + weight * (disp - group_mean(disp, group_ids))
    dforce = dloads - jnp.roll(dloads, 1, axis=0) + weight * (direction - group_mean(direction, group_ids))
    stiff_diag = diag_stiff[None, :, None, :]
    stiff_cross = cross_stiff[None, :, None, :]
    disp_hat = hartley(disp)
    residual = stiff_diag * disp_hat + stiff_cross * mirror(disp_hat) + hartley(force) - excitation
    dir_hat = hartley(direction)
    jvp = stiff_diag * dir_hat + stiff_cross * mirror(dir_hat) + hartley(dforce)
    return (residual, jvp)
```

```python
import math

import jax
import jax.numpy as jnp
import numpy as np
from jax import lax
from jax.experimental import pallas as pl
from jax.experimental.pallas import tpu as pltpu
from jax.sharding import PartitionSpec as P

MESH = pl.DeviceIdType.MESH

exact_mode = lax.Precision.HIGHEST


def passed_along(value, axis, steps):
    count = lax.axis_size(axis)
    pairs = [(source, (source + steps) % count) for source in range(count)]
    return lax.ppermute(value, axis, pairs)


def from_behind(block, axis, distance):
    devices = range(lax.axis_size(axis))
    route = [(i - distance, i) for i in devices if i - distance in devices]
    return lax.ppermute(block, axis, route)


def basis_table(coefs, samples):
    coef_index = lax.broadcasted_iota(jnp.int32, (coefs, samples), 0)
    time_index = lax.broadcasted_iota(jnp.int32, (coefs, samples), 1)
    harmonic = coef_index // 2 + 1
    phase = harmonic * time_index % samples
    angle = phase.astype(jnp.float32) * (2.0 * math.pi / samples)
    return jnp.where(coef_index % 2 == 0, jnp.cos(angle), jnp.sin(angle))


def hartley_table(count):
    row_index = lax.broadcasted_iota(jnp.int32, (count, count), 0)
    col_index = lax.broadcasted_iota(jnp.int32, (count, count), 1)
    phase = row_index * col_index % count
    angle = phase.astype(jnp.float32) * (2.0 * math.pi / count)
    return (jnp.cos(angle) + jnp.sin(angle)) / math.sqrt(count)


def contact_law(gaps, dgaps, states_here, params):
    preload = params[0]
    normal_stiff = params[1]
    tangent_stiff = params[2]
    friction_coef = params[3]
    touching = (states_here != 2).astype(jnp.float32)
    sliding = states_here == 1
    normal = (preload + normal_stiff * gaps[0]) * touching
    dnormal = normal_stiff * dgaps[0] * touching
    radius = jnp.sqrt(gaps[1] * gaps[1] + gaps[2] * gaps[2] + 1.0)
    projected = (gaps[1] * dgaps[1] + gaps[2] * dgaps[2]) / (radius * radius * radius)
    tractions = [normal]
    dtractions = [dnormal]
    for channel in (1, 2):
        stuck = tangent_stiff * gaps[channel]
        dstuck = tangent_stiff * dgaps[channel]
        slipped = friction_coef * normal * gaps[channel] / radius
        dslipped = friction_coef * (
            dnormal * gaps[channel] / radius
            + normal * (dgaps[channel] / radius - gaps[channel] * projected)
        )
        tractions.append(jnp.where(sliding, slipped, stuck) * touching)
        dtractions.append(jnp.where(sliding, dslipped, dstuck) * touching)
    return (jnp.stack(tractions), jnp.stack(dtractions))


def mirror(field):
    return jnp.roll(jnp.flip(field, -1), 1, -1)


def group_flag(group_ids, own_group, other_index, sectors):
    inside = jnp.logical_and(other_index >= 0, other_index < sectors)
    safe_index = jnp.clip(other_index, 0, sectors - 1)
    other_group = lax.dynamic_slice_in_dim(group_ids, safe_index, 1)
    return jnp.logical_and(inside, other_group == own_group).astype(jnp.float32)[0]


def body_any_size(
    disp,
    direction,
    stick_state,
    contact_params,
    mistuning,
    group_ids,
    diag_stiff,
    cross_stiff,
    excitation,
):
    sectors = lax.axis_size("sector")
    sector_index = lax.axis_index("sector")
    harm_index = lax.axis_index("harm")
    local_coefs = disp.shape[2]
    samples = stick_state.shape[1]
    coefs = local_coefs * lax.axis_size("harm")
    table = basis_table(coefs, samples)
    own_table = lax.dynamic_slice_in_dim(table, harm_index * local_coefs, local_coefs, 0)
    scale = 2.0 / samples
    hartley = hartley_table(sectors)
    paired = jnp.concatenate([disp, direction], 0)
    paired_next = passed_along(paired, "sector", -1)
    relative = paired - paired_next
    gathered = lax.all_gather(relative, "harm", axis=2, tiled=True)
    params_here = contact_params[0]
    gaps = jnp.einsum("wcjp,jt->wctp", gathered, table, precision=exact_mode)
    traction, dtraction = contact_law(gaps[0], gaps[1], stick_state[0], params_here)
    loads = (
        jnp.einsum(
            "wctp,jt->wcjp", jnp.stack([traction, dtraction]), own_table, precision=exact_mode
        )
        * scale
    )
    earlier_loads = passed_along(loads, "sector", 1)
    own_group = lax.dynamic_slice_in_dim(group_ids, sector_index, 1)
    members = jnp.sum((group_ids == own_group[0]).astype(jnp.float32))
    totals = paired
    for offset in range(1, 8):
        from_before = from_behind(paired, "sector", offset)
        from_after = from_behind(paired, "sector", -offset)
        flag_before = group_flag(group_ids, own_group, sector_index - offset, sectors)
        flag_after = group_flag(group_ids, own_group, sector_index + offset, sectors)
        totals = totals + flag_before * from_before + flag_after * from_after
    weight = lax.dynamic_slice_in_dim(mistuning, sector_index, 1)[0]
    forces = loads - earlier_loads + weight * (paired - totals / members)
    outgoing = jnp.concatenate([paired, forces], 0)
    received = lax.all_to_all(outgoing[:, None], "sector", split_axis=4, concat_axis=1, tiled=True)
    states_nd = jnp.einsum("ks,wscjp->wcjpk", hartley, received[0:2], precision=exact_mode)
    forces_nd = jnp.einsum("ks,wscjp->wcjpk", hartley, received[2:4], precision=exact_mode)
    stiff_diag = diag_stiff[None, :, None, :]
    stiff_cross = cross_stiff[None, :, None, :]
    residual = (
        stiff_diag * states_nd[0] + stiff_cross * mirror(states_nd[0]) + forces_nd[0] - excitation
    )
    jvp = stiff_diag * states_nd[1] + stiff_cross * mirror(states_nd[1]) + forces_nd[1]
    return (residual, jvp)


LANES = 128
HALF = 64
ROW_HARTLEY = 0
ROW_MIRROR = 16
ROW_SPREAD = 32
ROW_LOAD = 48
ROW_SAME = 176
ROW_COEF = 304
ROW_PICK = 432
ROW_SQUARE = 560
ROW_LOADS = 576
ROW_GAPS = 704
ROWS = 960


def constant_table(sectors, coefs, samples):
    k = np.arange(sectors)
    phase = 2.0 * np.pi * (np.outer(k, k) % sectors) / sectors
    hartley = (np.cos(phase) + np.sin(phase)) / math.sqrt(sectors)
    out = np.zeros((ROWS, LANES), np.float64)
    lane_sector, lane_coef = np.arange(LANES) // 8, np.arange(LANES) % 8
    row_coef, row_k = np.arange(LANES) // sectors, np.arange(LANES) % sectors
    out[ROW_HARTLEY : ROW_HARTLEY + 16] = hartley[:, lane_sector]
    out[ROW_MIRROR : ROW_MIRROR + 16] = hartley[(-k) % sectors][:, lane_sector]
    out[ROW_SPREAD : ROW_SPREAD + 16] = k[:, None] == lane_sector[None, :]
    same = row_coef[:, None] == lane_coef[None, :]
    reaction = hartley - np.roll(hartley, -1, 1)
    out[ROW_LOAD : ROW_LOAD + 128] = same * reaction[row_k][:, lane_sector]
    out[ROW_SAME : ROW_SAME + 128] = same
    out[ROW_COEF : ROW_COEF + 128, 0:8] = row_coef[:, None] == np.arange(8)[None, :]
    out[ROW_PICK : ROW_PICK + 128, 0:16] = row_k[:, None] == k[None, :]
    out[ROW_SQUARE : ROW_SQUARE + 16, 0:16] = hartley
    c, t = np.arange(coefs), np.arange(samples)
    angle = 2.0 * np.pi * (np.outer(c // 2 + 1, t) % samples) / samples
    basis = np.where(c[:, None] % 2 == 0, np.cos(angle), np.sin(angle))
    for h in range(2):
        ordered = np.roll(basis, -h * (coefs // 2), 0)
        out[ROW_LOADS + 64 * h : ROW_LOADS + 64 * (h + 1)] = ordered * (2.0 / samples)
        out[ROW_GAPS + 128 * h : ROW_GAPS + 128 * (h + 1), 0:64] = ordered.T
    return out.astype(np.float32)


def product(a, b, precision=lax.Precision.HIGH):
    return jnp.dot(a, b, preferred_element_type=jnp.float32, precision=precision)


def kernel(
    disp,
    direction,
    states,
    params,
    mistuning,
    groups,
    diag,
    cross,
    excitation,
    table,
    residual,
    jvp,
    x_out,
    s_out,
    x_in,
    s_in,
    r_out,
    r_in,
    l_out,
    l_in,
    params8,
    tractions,
    linear,
    x_sent,
    x_got,
    s_sent,
    s_got,
    r_sent,
    r_got,
    l_sent,
    l_got,
):
    sectors = 16
    pairs = sectors // 2
    me = lax.axis_index("sector")
    h = lax.axis_index("harm")
    g0 = me // 2
    partner = (me, 1 - h)

    barrier = pltpu.get_barrier_semaphore()

    def greet(i, carry):
        pl.semaphore_signal(
            barrier, inc=1, device_id=(lax.rem(me + i, sectors), h), device_id_type=MESH
        )
        return carry

    lax.fori_loop(1, sectors, greet, 0)
    pl.semaphore_signal(barrier, inc=1, device_id=partner, device_id_type=MESH)

    def low(rows):
        return lax.broadcasted_iota(jnp.int32, (rows, LANES), 1) < HALF

    params8[0:4, :] = params[...]
    params8[4:8, :] = params[...]

    def pack(g, carry):
        lanes = pl.ds(pl.multiple_of(g * LANES, LANES), LANES)
        a, b = disp[:, lanes], direction[:, lanes]
        x_out[2 * g] = jnp.where(low(96), a, pltpu.roll(b, HALF, 1))
        x_out[2 * g + 1] = jnp.where(low(96), pltpu.roll(a, HALF, 1), b)
        z = states[:, lanes].astype(jnp.float32)
        early, late = z[0:64], z[64:128]
        s_out[2 * g, 8:72, :] = jnp.where(low(64), early, pltpu.roll(late, HALF, 1))
        s_out[2 * g + 1, 8:72, :] = jnp.where(low(64), pltpu.roll(early, HALF, 1), late)
        p = params8[:, lanes]
        turned = pltpu.roll(p, HALF, 1)
        s_out[2 * g, 0:8, :] = jnp.where(low(8), p, turned)
        s_out[2 * g + 1, 0:8, :] = jnp.where(low(8), turned, p)
        return carry

    lax.fori_loop(0, pairs, pack, 0)

    def x_copy(to, source):
        return pltpu.make_async_remote_copy(
            src_ref=x_out.at[to],
            dst_ref=x_in.at[source],
            send_sem=x_sent.at[to],
            recv_sem=x_got.at[source],
            device_id=(to, h),
            device_id_type=MESH,
        )

    def s_copy(to, source):
        return pltpu.make_async_remote_copy(
            src_ref=s_out.at[to],
            dst_ref=s_in.at[source // 2],
            send_sem=s_sent.at[to],
            recv_sem=s_got.at[source // 2],
            device_id=(to, h),
            device_id_type=MESH,
        )

    x_in[me] = x_out[me]
    mine_here = lax.rem(me, 2) == h

    @pl.when(mine_here)
    def _():
        s_in[g0] = s_out[me]

    pl.semaphore_wait(barrier, sectors)

    def send(i, carry):
        to = lax.rem(me + sectors - i, sectors)
        x_copy(to, me).start()

        @pl.when(mine_here)
        def _():
            s_copy(to, me).start()

        return carry

    lax.fori_loop(1, sectors, send, 0)

    square = table[ROW_SQUARE : ROW_SQUARE + 16, 0:16]
    row = lax.broadcasted_iota(jnp.int32, (16, 16), 0)
    col = lax.broadcasted_iota(jnp.int32, (16, 16), 1)
    group_row = jnp.broadcast_to(groups[...].astype(jnp.float32), (16, 16))
    group_col = jnp.sum(jnp.where(row == col, group_row, 0.0), axis=1, keepdims=True)
    together = (group_row == group_col).astype(jnp.float32)
    mean = together / jnp.sum(together, axis=0, keepdims=True)
    weighted = square * mistuning[...]
    exact = lax.Precision.HIGHEST
    tuned = weighted - product(weighted, mean, exact)
    tuned = product(tuned, table[ROW_SPREAD : ROW_SPREAD + 16, :], exact)
    pick = table[ROW_PICK : ROW_PICK + 128, 0:16]
    coef_rows = table[ROW_COEF : ROW_COEF + 128, 0:8]
    same = table[ROW_SAME : ROW_SAME + 128, :]
    for b in range(4):
        d = pick * product(coef_rows, diag[8 * b : 8 * b + 8, :], exact)
        c = pick * product(coef_rows, cross[8 * b : 8 * b + 8, :], exact)
        linear[b] = same * (
            product(d, table[ROW_HARTLEY : ROW_HARTLEY + 16, :], exact)
            + product(c, table[ROW_MIRROR : ROW_MIRROR + 16, :], exact)
            + product(pick, tuned, exact)
        )

    def r_copy(j):
        return pltpu.make_async_remote_copy(
            src_ref=r_out.at[j],
            dst_ref=r_in.at[j],
            send_sem=r_sent.at[j],
            recv_sem=r_got.at[j],
            device_id=partner,
            device_id_type=MESH,
        )

    def l_copy(j, sector):
        return pltpu.make_async_remote_copy(
            src_ref=l_out.at[j],
            dst_ref=l_in.at[sector],
            send_sem=l_sent.at[j],
            recv_sem=l_got.at[sector // 2],
            device_id=partner,
            device_id_type=MESH,
        )

    def arrive(sector):
        @pl.when(sector != me)
        def _():
            x_copy(me, sector).wait_recv()

    def pair(j):
        return lax.rem(g0 + j, pairs)

    def hand_over(j):
        g = pair(j)
        arrive(2 * g + 1)

        @pl.when(j < pairs - 1)
        def _():
            arrive(lax.rem(2 * g + 2, sectors))

        other = 2 * g + 1 - h
        r_out[j] = x_in[other] - x_in[lax.rem(other + 1, sectors)]
        r_copy(j).start()

    def contact(j):
        g = pair(j)
        sector = 2 * g + h
        own = x_in[sector] - x_in[lax.rem(sector + 1, sectors)]

        @pl.when(sector != me)
        def _():
            s_copy(me, sector).wait_recv()

        r_copy(j).wait_recv()
        far = r_in[j]
        rows = [jnp.concatenate([own[32 * i : 32 * i + 32], far[32 * i : 32 * i + 32]], 0) for i in range(3)]
        gaps_rows = pl.ds(pl.multiple_of(ROW_GAPS + 128 * h, 8), 128)
        moved = product(table[gaps_rows, 0:64], jnp.concatenate(rows, 1))
        law = s_in[g, 0:8, :]
        n0, kn, kt, mu = law[0:1], law[1:2], law[2:3], law[3:4]
        step = 32
        for start in range(0, 128, step):
            packed = s_in[g, 8 + start % 64 : 8 + start % 64 + step, :]
            turned = pltpu.roll(packed, HALF, 1)
            left = low(step)
            z = jnp.where(left, packed, turned) if start < 64 else jnp.where(left, turned, packed)
            raw = [moved[start : start + step, LANES * i : LANES * (i + 1)] for i in range(3)]
            swapped = [pltpu.roll(value, HALF, 1) for value in raw]
            gap = [jnp.where(left, u, v) for u, v in zip(raw, swapped)]
            dgap = [jnp.where(left, v, u) for u, v in zip(raw, swapped)]
            touching = (z < 1.5).astype(jnp.float32)
            sliding = jnp.logical_and(z > 0.5, z < 1.5)
            normal = (n0 + kn * gap[0]) * touching
            dnormal = kn * dgap[0] * touching
            inverse = lax.rsqrt(gap[1] * gap[1] + gap[2] * gap[2] + 1.0)
            along = (gap[1] * dgap[1] + gap[2] * dgap[2]) * (inverse * inverse)
            tractions[start : start + step, 0:LANES] = jnp.where(left, normal, dnormal)
            rub = mu * inverse
            for i in (1, 2):
                slipped = normal * gap[i]
                dslipped = dnormal * gap[i] + normal * (dgap[i] - gap[i] * along)
                stuck = kt * raw[i] * touching
                tractions[start : start + step, LANES * i : LANES * (i + 1)] = jnp.where(
                    sliding, rub * jnp.where(left, slipped, dslipped), stuck
                )
        loads_rows = pl.ds(pl.multiple_of(ROW_LOADS + 64 * h, 8), 64)
        loads = product(table[loads_rows, :], tractions[...])
        for i in range(3):
            l_out[j, 32 * i : 32 * i + 32, :] = loads[32:64, LANES * i : LANES * (i + 1)]
        l_copy(j, sector).start()
        for i in range(3):
            l_in[sector, 32 * i : 32 * i + 32, :] = loads[0:32, LANES * i : LANES * (i + 1)]

    arrive(2 * g0)
    hand_over(0)

    def turn(j, carry):
        @pl.when(j < pairs - 1)
        def _():
            hand_over(j + 1)

        contact(j)
        return carry

    lax.fori_loop(0, pairs, turn, 0)

    def loads_here(j, carry):
        l_copy(j, 2 * j + 1 - h).wait_recv()
        return carry

    lax.fori_loop(0, pairs, loads_here, 0)
    reaction = table[ROW_LOAD : ROW_LOAD + 128, :]
    for b in range(4):
        matrix = jnp.concatenate([linear[b], reaction], 1)
        columns = []
        for i in range(3):
            at = slice(32 * i + 8 * b, 32 * i + 8 * b + 8)
            field = [x_in[:, at, :].reshape(128, LANES), l_in[:, at, :].reshape(128, LANES)]
            columns.append(jnp.concatenate(field, 0))
        out = product(matrix, jnp.concatenate(columns, 1))
        for i in range(3):
            both = out[:, LANES * i : LANES * (i + 1)]
            first = both[:, 0:HALF].reshape(8, 16, HALF)
            second = pltpu.roll(both, HALF, 1)[:, 0:HALF].reshape(8, 16, HALF)
            residual[i, 8 * b : 8 * b + 8] = first - excitation[i, 8 * b : 8 * b + 8]
            jvp[i, 8 * b : 8 * b + 8] = second

    def sent(i, carry):
        to = lax.rem(me + sectors - i, sectors)
        x_copy(to, me).wait_send()

        @pl.when(mine_here)
        def _():
            s_copy(to, me).wait_send()

        return carry

    lax.fori_loop(1, sectors, sent, 0)

    def sent_back(j, carry):
        r_copy(j).wait_send()
        l_copy(j, 2 * pair(j) + h).wait_send()
        return carry

    lax.fori_loop(0, pairs, sent_back, 0)


def body_in_kernel(
    disp,
    direction,
    stick_state,
    contact_params,
    mistuning,
    group_ids,
    diag_stiff,
    cross_stiff,
    excitation,
):
    vmem = pl.BlockSpec(memory_space=pltpu.VMEM)
    out = jax.ShapeDtypeStruct((3, 32, 16, HALF), jnp.float32)
    dma = pltpu.SemaphoreType.DMA
    table = jnp.asarray(constant_table(16, 64, 128))
    residual, jvp = pl.pallas_call(
        kernel,
        out_shape=(out, out),
        in_specs=[vmem] * 10,
        out_specs=(vmem, vmem),
        scratch_shapes=[
            pltpu.VMEM((16, 96, LANES), jnp.float32),
            pltpu.VMEM((16, 72, LANES), jnp.float32),
            pltpu.VMEM((16, 96, LANES), jnp.float32),
            pltpu.VMEM((8, 72, LANES), jnp.float32),
            pltpu.VMEM((8, 96, LANES), jnp.float32),
            pltpu.VMEM((8, 96, LANES), jnp.float32),
            pltpu.VMEM((8, 96, LANES), jnp.float32),
            pltpu.VMEM((16, 96, LANES), jnp.float32),
            pltpu.VMEM((8, 1024), jnp.float32),
            pltpu.VMEM((128, 3 * LANES), jnp.float32),
            pltpu.VMEM((4, 128, LANES), jnp.float32),
            dma((16,)),
            dma((16,)),
            dma((16,)),
            dma((8,)),
            dma((8,)),
            dma((8,)),
            dma((8,)),
            dma((8,)),
        ],
        compiler_params=pltpu.CompilerParams(
            collective_id=0, has_side_effects=True, vmem_limit_bytes=40 * 1024 * 1024
        ),
    )(
        disp.reshape(96, 1024),
        direction.reshape(96, 1024),
        stick_state[0],
        contact_params[0],
        mistuning[None],
        group_ids[None],
        diag_stiff,
        cross_stiff,
        jnp.swapaxes(excitation, 2, 3),
        table,
    )
    return (jnp.swapaxes(residual, 2, 3), jnp.swapaxes(jvp, 2, 3))


def solution(mesh):
    in_specs = (
        P("sector", None, "harm", None),
        P("sector", None, "harm", None),
        P("sector", None, None),
        P("sector", None, None),
        P(),
        P(),
        P("harm", None),
        P("harm", None),
        P(None, "harm", "sector", None),
    )
    out_specs = (P(None, "harm", "sector", None), P(None, "harm", "sector", None))

    def body(*arrays):
        _, channels, coefs, nodes = arrays[0].shape
        sizes = (mesh.shape["sector"], mesh.shape["harm"], channels, coefs, nodes, arrays[2].shape[1])
        if sizes == (16, 2, 3, 32, 1024, 128):
            return body_in_kernel(*arrays)
        return body_any_size(*arrays)

    return jax.shard_map(body, mesh=mesh, in_specs=in_specs, out_specs=out_specs, check_vma=False)
```

```python
import math

import jax
import jax.numpy as jnp
import numpy as np
from jax import lax
from jax.experimental import pallas as pl
from jax.experimental.pallas import tpu as pltpu
from jax.sharding import PartitionSpec as P

MESH = pl.DeviceIdType.MESH

exact_mode = lax.Precision.HIGHEST


def passed_along(value, axis, steps):
    count = lax.axis_size(axis)
    pairs = [(source, (source + steps) % count) for source in range(count)]
    return lax.ppermute(value, axis, pairs)


def from_behind(block, axis, distance):
    devices = range(lax.axis_size(axis))
    route = [(i - distance, i) for i in devices if i - distance in devices]
    return lax.ppermute(block, axis, route)


def basis_table(coefs, samples):
    coef_index = lax.broadcasted_iota(jnp.int32, (coefs, samples), 0)
    time_index = lax.broadcasted_iota(jnp.int32, (coefs, samples), 1)
    harmonic = coef_index // 2 + 1
    phase = harmonic * time_index % samples
    angle = phase.astype(jnp.float32) * (2.0 * math.pi / samples)
    return jnp.where(coef_index % 2 == 0, jnp.cos(angle), jnp.sin(angle))


def hartley_table(count):
    row_index = lax.broadcasted_iota(jnp.int32, (count, count), 0)
    col_index = lax.broadcasted_iota(jnp.int32, (count, count), 1)
    phase = row_index * col_index % count
    angle = phase.astype(jnp.float32) * (2.0 * math.pi / count)
    return (jnp.cos(angle) + jnp.sin(angle)) / math.sqrt(count)


def contact_law(gaps, dgaps, states_here, params):
    preload = params[0]
    normal_stiff = params[1]
    tangent_stiff = params[2]
    friction_coef = params[3]
    touching = (states_here != 2).astype(jnp.float32)
    sliding = states_here == 1
    normal = (preload + normal_stiff * gaps[0]) * touching
    dnormal = normal_stiff * dgaps[0] * touching
    radius = jnp.sqrt(gaps[1] * gaps[1] + gaps[2] * gaps[2] + 1.0)
    projected = (gaps[1] * dgaps[1] + gaps[2] * dgaps[2]) / (radius * radius * radius)
    tractions = [normal]
    dtractions = [dnormal]
    for channel in (1, 2):
        stuck = tangent_stiff * gaps[channel]
        dstuck = tangent_stiff * dgaps[channel]
        slipped = friction_coef * normal * gaps[channel] / radius
        dslipped = friction_coef * (
            dnormal * gaps[channel] / radius
            + normal * (dgaps[channel] / radius - gaps[channel] * projected)
        )
        tractions.append(jnp.where(sliding, slipped, stuck) * touching)
        dtractions.append(jnp.where(sliding, dslipped, dstuck) * touching)
    return (jnp.stack(tractions), jnp.stack(dtractions))


def mirror(field):
    return jnp.roll(jnp.flip(field, -1), 1, -1)


def group_flag(group_ids, own_group, other_index, sectors):
    inside = jnp.logical_and(other_index >= 0, other_index < sectors)
    safe_index = jnp.clip(other_index, 0, sectors - 1)
    other_group = lax.dynamic_slice_in_dim(group_ids, safe_index, 1)
    return jnp.logical_and(inside, other_group == own_group).astype(jnp.float32)[0]


def body_any_size(
    disp,
    direction,
    stick_state,
    contact_params,
    mistuning,
    group_ids,
    diag_stiff,
    cross_stiff,
    excitation,
):
    sectors = lax.axis_size("sector")
    sector_index = lax.axis_index("sector")
    harm_index = lax.axis_index("harm")
    local_coefs = disp.shape[2]
    samples = stick_state.shape[1]
    coefs = local_coefs * lax.axis_size("harm")
    table = basis_table(coefs, samples)
    own_table = lax.dynamic_slice_in_dim(table, harm_index * local_coefs, local_coefs, 0)
    scale = 2.0 / samples
    hartley = hartley_table(sectors)
    paired = jnp.concatenate([disp, direction], 0)
    paired_next = passed_along(paired, "sector", -1)
    relative = paired - paired_next
    gathered = lax.all_gather(relative, "harm", axis=2, tiled=True)
    params_here = contact_params[0]
    gaps = jnp.einsum("wcjp,jt->wctp", gathered, table, precision=exact_mode)
    traction, dtraction = contact_law(gaps[0], gaps[1], stick_state[0], params_here)
    loads = (
        jnp.einsum(
            "wctp,jt->wcjp", jnp.stack([traction, dtraction]), own_table, precision=exact_mode
        )
        * scale
    )
    earlier_loads = passed_along(loads, "sector", 1)
    own_group = lax.dynamic_slice_in_dim(group_ids, sector_index, 1)
    members = jnp.sum((group_ids == own_group[0]).astype(jnp.float32))
    totals = paired
    for offset in range(1, 8):
        from_before = from_behind(paired, "sector", offset)
        from_after = from_behind(paired, "sector", -offset)
        flag_before = group_flag(group_ids, own_group, sector_index - offset, sectors)
        flag_after = group_flag(group_ids, own_group, sector_index + offset, sectors)
        totals = totals + flag_before * from_before + flag_after * from_after
    weight = lax.dynamic_slice_in_dim(mistuning, sector_index, 1)[0]
    forces = loads - earlier_loads + weight * (paired - totals / members)
    outgoing = jnp.concatenate([paired, forces], 0)
    received = lax.all_to_all(outgoing[:, None], "sector", split_axis=4, concat_axis=1, tiled=True)
    states_nd = jnp.einsum("ks,wscjp->wcjpk", hartley, received[0:2], precision=exact_mode)
    forces_nd = jnp.einsum("ks,wscjp->wcjpk", hartley, received[2:4], precision=exact_mode)
    stiff_diag = diag_stiff[None, :, None, :]
    stiff_cross = cross_stiff[None, :, None, :]
    residual = (
        stiff_diag * states_nd[0] + stiff_cross * mirror(states_nd[0]) + forces_nd[0] - excitation
    )
    jvp = stiff_diag * states_nd[1] + stiff_cross * mirror(states_nd[1]) + forces_nd[1]
    return (residual, jvp)


LANES = 128
HALF = 64
ROW_HARTLEY = 0
ROW_MIRROR = 16
ROW_SPREAD = 32
ROW_LOAD = 48
ROW_SAME = 176
ROW_COEF = 304
ROW_PICK = 432
ROW_SQUARE = 560
ROW_LOADS = 576
ROW_GAPS = 704
ROWS = 960


def constant_table(sectors, coefs, samples):
    k = np.arange(sectors)
    phase = 2.0 * np.pi * (np.outer(k, k) % sectors) / sectors
    hartley = (np.cos(phase) + np.sin(phase)) / math.sqrt(sectors)
    out = np.zeros((ROWS, LANES), np.float64)
    lane_sector, lane_coef = np.arange(LANES) // 8, np.arange(LANES) % 8
    row_coef, row_k = np.arange(LANES) // sectors, np.arange(LANES) % sectors
    out[ROW_HARTLEY : ROW_HARTLEY + 16] = hartley[:, lane_sector]
    out[ROW_MIRROR : ROW_MIRROR + 16] = hartley[(-k) % sectors][:, lane_sector]
    out[ROW_SPREAD : ROW_SPREAD + 16] = k[:, None] == lane_sector[None, :]
    same = row_coef[:, None] == lane_coef[None, :]
    reaction = hartley - np.roll(hartley, -1, 1)
    out[ROW_LOAD : ROW_LOAD + 128] = same * reaction[row_k][:, lane_sector]
    out[ROW_SAME : ROW_SAME + 128] = same
    out[ROW_COEF : ROW_COEF + 128, 0:8] = row_coef[:, None] == np.arange(8)[None, :]
    out[ROW_PICK : ROW_PICK + 128, 0:16] = row_k[:, None] == k[None, :]
    out[ROW_SQUARE : ROW_SQUARE + 16, 0:16] = hartley
    c, t = np.arange(coefs), np.arange(samples)
    angle = 2.0 * np.pi * (np.outer(c // 2 + 1, t) % samples) / samples
    basis = np.where(c[:, None] % 2 == 0, np.cos(angle), np.sin(angle))
    for h in range(2):
        ordered = np.roll(basis, -h * (coefs // 2), 0)
        out[ROW_LOADS + 64 * h : ROW_LOADS + 64 * (h + 1)] = ordered * (2.0 / samples)
        out[ROW_GAPS + 128 * h : ROW_GAPS + 128 * (h + 1), 0:64] = ordered.T
    return out.astype(np.float32)


def product(a, b, precision=lax.Precision.HIGH):
    return jnp.dot(a, b, preferred_element_type=jnp.float32, precision=precision)


SEND_ORDER = ((0, 2, 3, 1), (1, 0, 2, 3), (2, 3, 1, 0), (3, 1, 0, 2))
PAIR_ORDER = (
    (0, 1, 2, 6, 7, 3, 4, 5),
    (2, 6, 7, 0, 1, 3, 4, 5),
    (4, 0, 5, 6, 7, 1, 2, 3),
    (6, 4, 5, 7, 0, 1, 2, 3),
)


def seen(z, k, step):
    order = PAIR_ORDER[z]
    return int((order[k] + step) % 8 not in order[:k])


def kernel(
    disp_hbm,
    direction_hbm,
    states_hbm,
    params_hbm,
    mistuning_hbm,
    groups_hbm,
    diag_hbm,
    cross_hbm,
    excitation_hbm,
    table_hbm,
    residual,
    jvp,
    disp,
    direction,
    states,
    params,
    mistuning,
    groups,
    diag,
    cross,
    excitation,
    table,
    fetched,
    x_out,
    s_out,
    x_in,
    s_in,
    r_out,
    r_in,
    l_out,
    l_in,
    params8,
    tractions,
    linear,
    x_sent,
    x_got,
    s_sent,
    s_got,
    r_sent,
    r_got,
    l_sent,
    l_got,
):
    sectors = 16
    pairs = sectors // 2
    me = lax.axis_index("sector")
    h = lax.axis_index("harm")
    g0 = me // 2
    z0 = me // 4
    partner = (me, 1 - h)

    given = (
        disp_hbm,
        direction_hbm,
        states_hbm,
        params_hbm,
        mistuning_hbm,
        groups_hbm,
        diag_hbm,
        cross_hbm,
        excitation_hbm,
        table_hbm,
    )
    held = (disp, direction, states, params, mistuning, groups, diag, cross, excitation, table)
    fetches = [
        pltpu.make_async_copy(source, target, fetched.at[i])
        for i, (source, target) in enumerate(zip(given, held))
    ]
    for fetch in fetches:
        fetch.start()

    barrier = pltpu.get_barrier_semaphore()

    def greet(i, carry):
        pl.semaphore_signal(
            barrier, inc=1, device_id=(lax.rem(me + i, sectors), h), device_id_type=MESH
        )
        return carry

    lax.fori_loop(1, sectors, greet, 0)
    pl.semaphore_signal(barrier, inc=1, device_id=partner, device_id_type=MESH)

    def by_z(values):
        out = jnp.int32(values[3])
        for z in (2, 1, 0):
            out = jnp.where(z0 == z, values[z], out)
        return out

    def at_step(column, j):
        out = column[-1]
        for k in range(len(column) - 2, -1, -1):
            out = jnp.where(j == k, column[k], out)
        return out

    send_order = [by_z([SEND_ORDER[z][k] for z in range(4)]) for k in range(4)]
    pair_order = [by_z([PAIR_ORDER[z][k] for z in range(4)]) for k in range(8)]
    new_first = [by_z([seen(z, k, -1) for z in range(4)]) for k in range(8)]
    new_last = [by_z([seen(z, k, 1) for z in range(4)]) for k in range(8)]

    def low(rows):
        return lax.broadcasted_iota(jnp.int32, (rows, LANES), 1) < HALF

    for i in range(4):
        fetches[i].wait()
    params8[0:4, :] = params[...]
    params8[4:8, :] = params[...]

    def pack(g, carry):
        lanes = pl.ds(pl.multiple_of(g * LANES, LANES), LANES)
        a, b = disp[:, lanes], direction[:, lanes]
        x_out[2 * g] = jnp.where(low(96), a, pltpu.roll(b, HALF, 1))
        x_out[2 * g + 1] = jnp.where(low(96), pltpu.roll(a, HALF, 1), b)
        z = states[:, lanes].astype(jnp.float32)
        early, late = z[0:64], z[64:128]
        s_out[2 * g, 8:72, :] = jnp.where(low(64), early, pltpu.roll(late, HALF, 1))
        s_out[2 * g + 1, 8:72, :] = jnp.where(low(64), pltpu.roll(early, HALF, 1), late)
        p = params8[:, lanes]
        turned = pltpu.roll(p, HALF, 1)
        s_out[2 * g, 0:8, :] = jnp.where(low(8), p, turned)
        s_out[2 * g + 1, 0:8, :] = jnp.where(low(8), turned, p)
        return carry

    lax.fori_loop(0, pairs, pack, 0)

    def x_copy(to, source):
        return pltpu.make_async_remote_copy(
            src_ref=x_out.at[to],
            dst_ref=x_in.at[source],
            send_sem=x_sent.at[to],
            recv_sem=x_got.at[source],
            device_id=(to, h),
            device_id_type=MESH,
        )

    def s_copy(to, source):
        return pltpu.make_async_remote_copy(
            src_ref=s_out.at[to],
            dst_ref=s_in.at[source // 2],
            send_sem=s_sent.at[to],
            recv_sem=s_got.at[source // 2],
            device_id=(to, h),
            device_id_type=MESH,
        )

    x_in[me] = x_out[me]
    mine_here = lax.rem(me, 2) == h

    @pl.when(mine_here)
    def _():
        s_in[g0] = s_out[me]

    pl.semaphore_wait(barrier, sectors)
    core, x = lax.rem(me, 2), lax.rem(g0, 2)

    def send(i, carry):
        z = at_step(send_order, i // 4)
        q = lax.rem(i, 4)
        to = 4 * z + 2 * lax.rem(q + core, 2) + lax.rem(q // 2 + x, 2)

        @pl.when(to != me)
        def _():
            x_copy(to, me).start()

            @pl.when(mine_here)
            def _():
                s_copy(to, me).start()

        return carry

    lax.fori_loop(0, sectors, send, 0)
    for i in range(4, 10):
        fetches[i].wait()

    square = table[ROW_SQUARE : ROW_SQUARE + 16, 0:16]
    row = lax.broadcasted_iota(jnp.int32, (16, 16), 0)
    col = lax.broadcasted_iota(jnp.int32, (16, 16), 1)
    group_row = jnp.broadcast_to(groups[...].astype(jnp.float32), (16, 16))
    group_col = jnp.sum(jnp.where(row == col, group_row, 0.0), axis=1, keepdims=True)
    together = (group_row == group_col).astype(jnp.float32)
    mean = together / jnp.sum(together, axis=0, keepdims=True)
    weighted = square * mistuning[...]
    exact = lax.Precision.HIGHEST
    tuned = weighted - product(weighted, mean, exact)
    tuned = product(tuned, table[ROW_SPREAD : ROW_SPREAD + 16, :], exact)
    pick = table[ROW_PICK : ROW_PICK + 128, 0:16]
    same = table[ROW_SAME : ROW_SAME + 128, :]
    plain = product(pick, table[ROW_HARTLEY : ROW_HARTLEY + 16, :], exact)
    turned_back = product(pick, table[ROW_MIRROR : ROW_MIRROR + 16, :], exact)
    tuned = product(pick, tuned, exact)
    diag_rows = product(pick, diag[...], exact)
    cross_rows = product(pick, cross[...], exact)
    coef_here = lax.broadcasted_iota(jnp.int32, (128, 32), 0) // 16
    coef_lane = lax.broadcasted_iota(jnp.int32, (128, 32), 1)
    for b in range(4):
        chosen = coef_lane == coef_here + 8 * b
        d = jnp.sum(jnp.where(chosen, diag_rows, 0.0), axis=1, keepdims=True)
        c = jnp.sum(jnp.where(chosen, cross_rows, 0.0), axis=1, keepdims=True)
        linear[b] = same * (d * plain + c * turned_back + tuned)

    def r_copy(j):
        return pltpu.make_async_remote_copy(
            src_ref=r_out.at[j],
            dst_ref=r_in.at[j],
            send_sem=r_sent.at[j],
            recv_sem=r_got.at[j],
            device_id=partner,
            device_id_type=MESH,
        )

    def l_copy(j, sector):
        return pltpu.make_async_remote_copy(
            src_ref=l_out.at[j],
            dst_ref=l_in.at[sector],
            send_sem=l_sent.at[j],
            recv_sem=l_got.at[sector // 2],
            device_id=partner,
            device_id_type=MESH,
        )

    def arrive(sector):
        @pl.when(sector != me)
        def _():
            x_copy(me, sector).wait_recv()

    def pair(j):
        return at_step(pair_order, j)

    def hand_over(j):
        g = pair(j)
        arrive(2 * g + 1)

        @pl.when(at_step(new_first, j) == 1)
        def _():
            arrive(2 * g)

        @pl.when(at_step(new_last, j) == 1)
        def _():
            arrive(lax.rem(2 * g + 2, sectors))

        other = 2 * g + 1 - h
        r_out[j] = x_in[other] - x_in[lax.rem(other + 1, sectors)]
        r_copy(j).start()

    def contact(j):
        g = pair(j)
        sector = 2 * g + h
        own = x_in[sector] - x_in[lax.rem(sector + 1, sectors)]

        @pl.when(sector != me)
        def _():
            s_copy(me, sector).wait_recv()

        r_copy(j).wait_recv()
        far = r_in[j]
        rows = [jnp.concatenate([own[32 * i : 32 * i + 32], far[32 * i : 32 * i + 32]], 0) for i in range(3)]
        gaps_rows = pl.ds(pl.multiple_of(ROW_GAPS + 128 * h, 8), 128)
        moved = product(table[gaps_rows, 0:64], jnp.concatenate(rows, 1))
        law = s_in[g, 0:8, :]
        n0, kn, kt, mu = law[0:1], law[1:2], law[2:3], law[3:4]
        step = 32
        for start in range(0, 128, step):
            packed = s_in[g, 8 + start % 64 : 8 + start % 64 + step, :]
            turned = pltpu.roll(packed, HALF, 1)
            left = low(step)
            z = jnp.where(left, packed, turned) if start < 64 else jnp.where(left, turned, packed)
            raw = [moved[start : start + step, LANES * i : LANES * (i + 1)] for i in range(3)]
            swapped = [pltpu.roll(value, HALF, 1) for value in raw]
            gap = [jnp.where(left, u, v) for u, v in zip(raw, swapped)]
            dgap = [jnp.where(left, v, u) for u, v in zip(raw, swapped)]
            touching = (z < 1.5).astype(jnp.float32)
            sliding = jnp.logical_and(z > 0.5, z < 1.5)
            normal = (n0 + kn * gap[0]) * touching
            dnormal = kn * dgap[0] * touching
            inverse = lax.rsqrt(gap[1] * gap[1] + gap[2] * gap[2] + 1.0)
            along = (gap[1] * dgap[1] + gap[2] * dgap[2]) * (inverse * inverse)
            tractions[start : start + step, 0:LANES] = jnp.where(left, normal, dnormal)
            rub = mu * inverse
            for i in (1, 2):
                slipped = normal * gap[i]
                dslipped = dnormal * gap[i] + normal * (dgap[i] - gap[i] * along)
                stuck = kt * raw[i] * touching
                tractions[start : start + step, LANES * i : LANES * (i + 1)] = jnp.where(
                    sliding, rub * jnp.where(left, slipped, dslipped), stuck
                )
        loads_rows = pl.ds(pl.multiple_of(ROW_LOADS + 64 * h, 8), 64)
        loads = product(table[loads_rows, :], tractions[...])
        for i in range(3):
            l_out[j, 32 * i : 32 * i + 32, :] = loads[32:64, LANES * i : LANES * (i + 1)]
        l_copy(j, sector).start()
        for i in range(3):
            l_in[sector, 32 * i : 32 * i + 32, :] = loads[0:32, LANES * i : LANES * (i + 1)]

    hand_over(jnp.int32(0))

    def turn(j, carry):
        @pl.when(j < pairs - 1)
        def _():
            hand_over(j + 1)

        contact(j)
        return carry

    lax.fori_loop(0, pairs, turn, 0)

    def loads_here(j, carry):
        l_copy(j, 2 * j + 1 - h).wait_recv()
        return carry

    lax.fori_loop(0, pairs, loads_here, 0)
    reaction = table[ROW_LOAD : ROW_LOAD + 128, :]
    for b in range(4):
        matrix = jnp.concatenate([linear[b], reaction], 1)
        columns = []
        for i in range(3):
            at = slice(32 * i + 8 * b, 32 * i + 8 * b + 8)
            field = [x_in[:, at, :].reshape(128, LANES), l_in[:, at, :].reshape(128, LANES)]
            columns.append(jnp.concatenate(field, 0))
        out = product(matrix, jnp.concatenate(columns, 1))
        for i in range(3):
            both = out[:, LANES * i : LANES * (i + 1)]
            first = both[:, 0:HALF].reshape(8, 16, HALF)
            second = pltpu.roll(both, HALF, 1)[:, 0:HALF].reshape(8, 16, HALF)
            residual[i, 8 * b : 8 * b + 8] = first - excitation[i, 8 * b : 8 * b + 8]
            jvp[i, 8 * b : 8 * b + 8] = second

    def sent(i, carry):
        to = lax.rem(me + i, sectors)
        x_copy(to, me).wait_send()

        @pl.when(mine_here)
        def _():
            s_copy(to, me).wait_send()

        return carry

    lax.fori_loop(1, sectors, sent, 0)

    def sent_back(j, carry):
        r_copy(j).wait_send()
        l_copy(j, 2 * pair(j) + h).wait_send()
        return carry

    lax.fori_loop(0, pairs, sent_back, 0)


def body_in_kernel(
    disp,
    direction,
    stick_state,
    contact_params,
    mistuning,
    group_ids,
    diag_stiff,
    cross_stiff,
    excitation,
):
    vmem = pl.BlockSpec(memory_space=pltpu.VMEM)
    hbm = pl.BlockSpec(memory_space=pltpu.HBM)
    out = jax.ShapeDtypeStruct((3, 32, 16, HALF), jnp.float32)
    dma = pltpu.SemaphoreType.DMA
    table = jnp.asarray(constant_table(16, 64, 128))
    residual, jvp = pl.pallas_call(
        kernel,
        out_shape=(out, out),
        in_specs=[hbm] * 10,
        out_specs=(vmem, vmem),
        scratch_shapes=[
            pltpu.VMEM((96, 1024), jnp.float32),
            pltpu.VMEM((96, 1024), jnp.float32),
            pltpu.VMEM((128, 1024), jnp.int32),
            pltpu.VMEM((4, 1024), jnp.float32),
            pltpu.VMEM((1, 16), jnp.float32),
            pltpu.VMEM((1, 16), jnp.int32),
            pltpu.VMEM((16, 32), jnp.float32),
            pltpu.VMEM((16, 32), jnp.float32),
            pltpu.VMEM((3, 32, 16, HALF), jnp.float32),
            pltpu.VMEM((ROWS, LANES), jnp.float32),
            dma((10,)),
            pltpu.VMEM((16, 96, LANES), jnp.float32),
            pltpu.VMEM((16, 72, LANES), jnp.float32),
            pltpu.VMEM((16, 96, LANES), jnp.float32),
            pltpu.VMEM((8, 72, LANES), jnp.float32),
            pltpu.VMEM((8, 96, LANES), jnp.float32),
            pltpu.VMEM((8, 96, LANES), jnp.float32),
            pltpu.VMEM((8, 96, LANES), jnp.float32),
            pltpu.VMEM((16, 96, LANES), jnp.float32),
            pltpu.VMEM((8, 1024), jnp.float32),
            pltpu.VMEM((128, 3 * LANES), jnp.float32),
            pltpu.VMEM((4, 128, LANES), jnp.float32),
            dma((16,)),
            dma((16,)),
            dma((16,)),
            dma((8,)),
            dma((8,)),
            dma((8,)),
            dma((8,)),
            dma((8,)),
        ],
        compiler_params=pltpu.CompilerParams(
            collective_id=0, has_side_effects=True, vmem_limit_bytes=63 * 1024 * 1024
        ),
    )(
        disp.reshape(96, 1024),
        direction.reshape(96, 1024),
        stick_state[0],
        contact_params[0],
        mistuning[None],
        group_ids[None],
        diag_stiff.T,
        cross_stiff.T,
        jnp.swapaxes(excitation, 2, 3),
        table,
    )
    return (jnp.swapaxes(residual, 2, 3), jnp.swapaxes(jvp, 2, 3))


def solution(mesh):
    in_specs = (
        P("sector", None, "harm", None),
        P("sector", None, "harm", None),
        P("sector", None, None),
        P("sector", None, None),
        P(),
        P(),
        P("harm", None),
        P("harm", None),
        P(None, "harm", "sector", None),
    )
    out_specs = (P(None, "harm", "sector", None), P(None, "harm", "sector", None))

    def body(*arrays):
        _, channels, coefs, nodes = arrays[0].shape
        sizes = (mesh.shape["sector"], mesh.shape["harm"], channels, coefs, nodes, arrays[2].shape[1])
        if sizes == (16, 2, 3, 32, 1024, 128):
            return body_in_kernel(*arrays)
        return body_any_size(*arrays)

    return jax.shard_map(body, mesh=mesh, in_specs=in_specs, out_specs=out_specs, check_vma=False)
```

```python
import math

import jax
import jax.numpy as jnp
import numpy as np
from jax import lax
from jax.experimental import pallas as pl
from jax.experimental.pallas import tpu as pltpu
from jax.sharding import PartitionSpec as P

MESH = pl.DeviceIdType.MESH

exact_mode = lax.Precision.HIGHEST


def passed_along(value, axis, steps):
    count = lax.axis_size(axis)
    pairs = [(source, (source + steps) % count) for source in range(count)]
    return lax.ppermute(value, axis, pairs)


def from_behind(block, axis, distance):
    devices = range(lax.axis_size(axis))
    route = [(i - distance, i) for i in devices if i - distance in devices]
    return lax.ppermute(block, axis, route)


def basis_table(coefs, samples):
    coef_index = lax.broadcasted_iota(jnp.int32, (coefs, samples), 0)
    time_index = lax.broadcasted_iota(jnp.int32, (coefs, samples), 1)
    harmonic = coef_index // 2 + 1
    phase = harmonic * time_index % samples
    angle = phase.astype(jnp.float32) * (2.0 * math.pi / samples)
    return jnp.where(coef_index % 2 == 0, jnp.cos(angle), jnp.sin(angle))


def hartley_table(count):
    row_index = lax.broadcasted_iota(jnp.int32, (count, count), 0)
    col_index = lax.broadcasted_iota(jnp.int32, (count, count), 1)
    phase = row_index * col_index % count
    angle = phase.astype(jnp.float32) * (2.0 * math.pi / count)
    return (jnp.cos(angle) + jnp.sin(angle)) / math.sqrt(count)


def contact_law(gaps, dgaps, states_here, params):
    preload = params[0]
    normal_stiff = params[1]
    tangent_stiff = params[2]
    friction_coef = params[3]
    touching = (states_here != 2).astype(jnp.float32)
    sliding = states_here == 1
    normal = (preload + normal_stiff * gaps[0]) * touching
    dnormal = normal_stiff * dgaps[0] * touching
    radius = jnp.sqrt(gaps[1] * gaps[1] + gaps[2] * gaps[2] + 1.0)
    projected = (gaps[1] * dgaps[1] + gaps[2] * dgaps[2]) / (radius * radius * radius)
    tractions = [normal]
    dtractions = [dnormal]
    for channel in (1, 2):
        stuck = tangent_stiff * gaps[channel]
        dstuck = tangent_stiff * dgaps[channel]
        slipped = friction_coef * normal * gaps[channel] / radius
        dslipped = friction_coef * (
            dnormal * gaps[channel] / radius
            + normal * (dgaps[channel] / radius - gaps[channel] * projected)
        )
        tractions.append(jnp.where(sliding, slipped, stuck) * touching)
        dtractions.append(jnp.where(sliding, dslipped, dstuck) * touching)
    return (jnp.stack(tractions), jnp.stack(dtractions))


def mirror(field):
    return jnp.roll(jnp.flip(field, -1), 1, -1)


def group_flag(group_ids, own_group, other_index, sectors):
    inside = jnp.logical_and(other_index >= 0, other_index < sectors)
    safe_index = jnp.clip(other_index, 0, sectors - 1)
    other_group = lax.dynamic_slice_in_dim(group_ids, safe_index, 1)
    return jnp.logical_and(inside, other_group == own_group).astype(jnp.float32)[0]


def body_any_size(
    disp,
    direction,
    stick_state,
    contact_params,
    mistuning,
    group_ids,
    diag_stiff,
    cross_stiff,
    excitation,
):
    sectors = lax.axis_size("sector")
    sector_index = lax.axis_index("sector")
    harm_index = lax.axis_index("harm")
    local_coefs = disp.shape[2]
    samples = stick_state.shape[1]
    coefs = local_coefs * lax.axis_size("harm")
    table = basis_table(coefs, samples)
    own_table = lax.dynamic_slice_in_dim(table, harm_index * local_coefs, local_coefs, 0)
    scale = 2.0 / samples
    hartley = hartley_table(sectors)
    paired = jnp.concatenate([disp, direction], 0)
    paired_next = passed_along(paired, "sector", -1)
    relative = paired - paired_next
    gathered = lax.all_gather(relative, "harm", axis=2, tiled=True)
    params_here = contact_params[0]
    gaps = jnp.einsum("wcjp,jt->wctp", gathered, table, precision=exact_mode)
    traction, dtraction = contact_law(gaps[0], gaps[1], stick_state[0], params_here)
    loads = (
        jnp.einsum(
            "wctp,jt->wcjp", jnp.stack([traction, dtraction]), own_table, precision=exact_mode
        )
        * scale
    )
    earlier_loads = passed_along(loads, "sector", 1)
    own_group = lax.dynamic_slice_in_dim(group_ids, sector_index, 1)
    members = jnp.sum((group_ids == own_group[0]).astype(jnp.float32))
    totals = paired
    for offset in range(1, 8):
        from_before = from_behind(paired, "sector", offset)
        from_after = from_behind(paired, "sector", -offset)
        flag_before = group_flag(group_ids, own_group, sector_index - offset, sectors)
        flag_after = group_flag(group_ids, own_group, sector_index + offset, sectors)
        totals = totals + flag_before * from_before + flag_after * from_after
    weight = lax.dynamic_slice_in_dim(mistuning, sector_index, 1)[0]
    forces = loads - earlier_loads + weight * (paired - totals / members)
    outgoing = jnp.concatenate([paired, forces], 0)
    received = lax.all_to_all(outgoing[:, None], "sector", split_axis=4, concat_axis=1, tiled=True)
    states_nd = jnp.einsum("ks,wscjp->wcjpk", hartley, received[0:2], precision=exact_mode)
    forces_nd = jnp.einsum("ks,wscjp->wcjpk", hartley, received[2:4], precision=exact_mode)
    stiff_diag = diag_stiff[None, :, None, :]
    stiff_cross = cross_stiff[None, :, None, :]
    residual = (
        stiff_diag * states_nd[0] + stiff_cross * mirror(states_nd[0]) + forces_nd[0] - excitation
    )
    jvp = stiff_diag * states_nd[1] + stiff_cross * mirror(states_nd[1]) + forces_nd[1]
    return (residual, jvp)


LANES = 128
VMEM_KERNEL = 63 * 1024 * 1024
HALF = 64
ROW_HARTLEY = 0
ROW_MIRROR = 16
ROW_SPREAD = 32
ROW_LOAD = 48
ROW_SAME = 176
ROW_COEF = 304
ROW_PICK = 432
ROW_SQUARE = 560
ROW_LOADS = 576
ROW_GAPS = 704
ROWS = 960


def constant_table(sectors, coefs, samples):
    k = np.arange(sectors)
    phase = 2.0 * np.pi * (np.outer(k, k) % sectors) / sectors
    hartley = (np.cos(phase) + np.sin(phase)) / math.sqrt(sectors)
    out = np.zeros((ROWS, LANES), np.float64)
    lane_sector, lane_coef = np.arange(LANES) // 8, np.arange(LANES) % 8
    row_coef, row_k = np.arange(LANES) // sectors, np.arange(LANES) % sectors
    out[ROW_HARTLEY : ROW_HARTLEY + 16] = hartley[:, lane_sector]
    out[ROW_MIRROR : ROW_MIRROR + 16] = hartley[(-k) % sectors][:, lane_sector]
    out[ROW_SPREAD : ROW_SPREAD + 16] = k[:, None] == lane_sector[None, :]
    same = row_coef[:, None] == lane_coef[None, :]
    reaction = hartley - np.roll(hartley, -1, 1)
    out[ROW_LOAD : ROW_LOAD + 128] = same * reaction[row_k][:, lane_sector]
    out[ROW_SAME : ROW_SAME + 128] = same
    out[ROW_COEF : ROW_COEF + 128, 0:8] = row_coef[:, None] == np.arange(8)[None, :]
    out[ROW_PICK : ROW_PICK + 128, 0:16] = row_k[:, None] == k[None, :]
    out[ROW_SQUARE : ROW_SQUARE + 16, 0:16] = hartley
    c, t = np.arange(coefs), np.arange(samples)
    angle = 2.0 * np.pi * (np.outer(c // 2 + 1, t) % samples) / samples
    basis = np.where(c[:, None] % 2 == 0, np.cos(angle), np.sin(angle))
    for h in range(2):
        ordered = np.roll(basis, -h * (coefs // 2), 0)
        out[ROW_LOADS + 64 * h : ROW_LOADS + 64 * (h + 1)] = ordered * (2.0 / samples)
        out[ROW_GAPS + 128 * h : ROW_GAPS + 128 * (h + 1), 0:64] = ordered.T
    return out.astype(np.float32)


def product(a, b, precision=lax.Precision.HIGH):
    return jnp.dot(a, b, preferred_element_type=jnp.float32, precision=precision)


SEND_ORDER = ((2, 0, 3, 1), (0, 1, 2, 3), (3, 2, 1, 0), (1, 3, 0, 2))
PAIR_ORDER = (
    (0, 1, 2, 6, 7, 3, 4, 5),
    (2, 6, 7, 0, 1, 3, 4, 5),
    (4, 0, 5, 6, 7, 1, 2, 3),
    (6, 4, 5, 7, 0, 1, 2, 3),
)


def seen(z, k, step):
    order = PAIR_ORDER[z]
    return int((order[k] + step) % 8 not in order[:k])


def kernel(
    disp_hbm,
    direction_hbm,
    states_hbm,
    params_hbm,
    mistuning_hbm,
    groups_hbm,
    diag_hbm,
    cross_hbm,
    table_hbm,
    x_hbm,
    l_hbm,
    linear_hbm,
    disp,
    direction,
    states,
    params,
    mistuning,
    groups,
    diag,
    cross,
    table,
    fetched,
    fetched_parts,
    x_out,
    s_out,
    x_in,
    s_in,
    r_out,
    r_in,
    l_out,
    l_in,
    params8,
    tractions,
    linear,
    x_kept,
    l_kept,
    linear_kept,
    x_sent,
    x_got,
    s_sent,
    s_got,
    r_sent,
    r_got,
    l_sent,
    l_got,
):
    sectors = 16
    pairs = sectors // 2
    me = lax.axis_index("sector")
    h = lax.axis_index("harm")
    g0 = me // 2
    z0 = me // 4
    partner = (me, 1 - h)

    def by_z(values):
        out = jnp.int32(values[3])
        for z in (2, 1, 0):
            out = jnp.where(z0 == z, values[z], out)
        return out

    def at_step(column, j):
        out = column[-1]
        for k in range(len(column) - 2, -1, -1):
            out = jnp.where(j == k, column[k], out)
        return out

    send_order = [by_z([SEND_ORDER[z][k] for z in range(4)]) for k in range(4)]
    pair_order = [by_z([PAIR_ORDER[z][k] for z in range(4)]) for k in range(8)]
    new_first = [by_z([seen(z, k, -1) for z in range(4)]) for k in range(8)]
    new_last = [by_z([seen(z, k, 1) for z in range(4)]) for k in range(8)]

    def part(i, z):
        lanes = pl.ds(pl.multiple_of(z * 2 * LANES, 2 * LANES), 2 * LANES)
        source, target = ((disp_hbm, disp), (direction_hbm, direction), (states_hbm, states))[i]
        return pltpu.make_async_copy(
            source.at[:, lanes], target.at[:, lanes], fetched_parts.at[i, z]
        )

    given = (params_hbm, mistuning_hbm, groups_hbm, diag_hbm, cross_hbm, table_hbm)
    held = (params, mistuning, groups, diag, cross, table)
    fetches = [
        pltpu.make_async_copy(source, target, fetched.at[i])
        for i, (source, target) in enumerate(zip(given, held))
    ]
    for k in range(4):
        for i in range(3):
            part(i, send_order[k]).start()
        if k == 0:
            fetches[0].start()
    for fetch in fetches[1:]:
        fetch.start()

    barrier = pltpu.get_barrier_semaphore()

    def greet(i, carry):
        pl.semaphore_signal(
            barrier, inc=1, device_id=(lax.rem(me + i, sectors), h), device_id_type=MESH
        )
        return carry

    lax.fori_loop(1, sectors, greet, 0)
    pl.semaphore_signal(barrier, inc=1, device_id=partner, device_id_type=MESH)

    def low(rows):
        return lax.broadcasted_iota(jnp.int32, (rows, LANES), 1) < HALF

    def pack(g):
        lanes = pl.ds(pl.multiple_of(g * LANES, LANES), LANES)
        a, b = disp[:, lanes], direction[:, lanes]
        x_out[2 * g] = jnp.where(low(96), a, pltpu.roll(b, HALF, 1))
        x_out[2 * g + 1] = jnp.where(low(96), pltpu.roll(a, HALF, 1), b)
        z = states[:, lanes].astype(jnp.float32)
        early, late = z[0:64], z[64:128]
        s_out[2 * g, 8:72, :] = jnp.where(low(64), early, pltpu.roll(late, HALF, 1))
        s_out[2 * g + 1, 8:72, :] = jnp.where(low(64), pltpu.roll(early, HALF, 1), late)
        p = params8[:, lanes]
        turned = pltpu.roll(p, HALF, 1)
        s_out[2 * g, 0:8, :] = jnp.where(low(8), p, turned)
        s_out[2 * g + 1, 0:8, :] = jnp.where(low(8), turned, p)

    def x_copy(to, source):
        return pltpu.make_async_remote_copy(
            src_ref=x_out.at[to],
            dst_ref=x_in.at[source],
            send_sem=x_sent.at[to],
            recv_sem=x_got.at[source],
            device_id=(to, h),
            device_id_type=MESH,
        )

    def s_copy(to, source):
        return pltpu.make_async_remote_copy(
            src_ref=s_out.at[to],
            dst_ref=s_in.at[source // 2],
            send_sem=s_sent.at[to],
            recv_sem=s_got.at[source // 2],
            device_id=(to, h),
            device_id_type=MESH,
        )

    mine_here = lax.rem(me, 2) == h
    core, x = lax.rem(me, 2), lax.rem(g0, 2)

    def send(k, carry):
        z = at_step(send_order, k)
        for i in range(3):
            part(i, z).wait()

        @pl.when(k == 0)
        def _():
            fetches[0].wait()
            params8[0:4, :] = params[...]
            params8[4:8, :] = params[...]

        pack(2 * z)
        pack(2 * z + 1)

        @pl.when(k == 0)
        def _():
            pl.semaphore_wait(barrier, sectors)

        @pl.when(z == z0)
        def _():
            x_in[me] = x_out[me]

            @pl.when(mine_here)
            def _():
                s_in[g0] = s_out[me]

        for q in range(4):
            to = 4 * z + 2 * lax.rem(q + core, 2) + lax.rem(q // 2 + x, 2)

            @pl.when(to != me)
            def _():
                x_copy(to, me).start()

                @pl.when(mine_here)
                def _():
                    s_copy(to, me).start()

        return carry

    lax.fori_loop(0, 4, send, 0)
    for fetch in fetches[1:]:
        fetch.wait()

    square = table[ROW_SQUARE : ROW_SQUARE + 16, 0:16]
    row = lax.broadcasted_iota(jnp.int32, (16, 16), 0)
    col = lax.broadcasted_iota(jnp.int32, (16, 16), 1)
    group_row = jnp.broadcast_to(groups[...].astype(jnp.float32), (16, 16))
    group_col = jnp.sum(jnp.where(row == col, group_row, 0.0), axis=1, keepdims=True)
    together = (group_row == group_col).astype(jnp.float32)
    mean = together / jnp.sum(together, axis=0, keepdims=True)
    weighted = square * mistuning[...]
    exact = lax.Precision.HIGHEST
    tuned = weighted - product(weighted, mean, exact)
    tuned = product(tuned, table[ROW_SPREAD : ROW_SPREAD + 16, :], exact)
    pick = table[ROW_PICK : ROW_PICK + 128, 0:16]
    same = table[ROW_SAME : ROW_SAME + 128, :]
    plain = product(pick, table[ROW_HARTLEY : ROW_HARTLEY + 16, :], exact)
    turned_back = product(pick, table[ROW_MIRROR : ROW_MIRROR + 16, :], exact)
    tuned = product(pick, tuned, exact)
    diag_rows = product(pick, diag[...], exact)
    cross_rows = product(pick, cross[...], exact)
    coef_here = lax.broadcasted_iota(jnp.int32, (128, 32), 0) // 16
    coef_lane = lax.broadcasted_iota(jnp.int32, (128, 32), 1)
    for b in range(4):
        chosen = coef_lane == coef_here + 8 * b
        d = jnp.sum(jnp.where(chosen, diag_rows, 0.0), axis=1, keepdims=True)
        c = jnp.sum(jnp.where(chosen, cross_rows, 0.0), axis=1, keepdims=True)
        linear[b] = same * (d * plain + c * turned_back + tuned)

    linear_copy = pltpu.make_async_copy(linear, linear_hbm, linear_kept)
    linear_copy.start()
    x_keep = pltpu.make_async_copy(x_in, x_hbm, x_kept)

    def l_keep(sector):
        return pltpu.make_async_copy(l_in.at[sector], l_hbm.at[sector], l_kept.at[sector])

    def r_copy(j):
        return pltpu.make_async_remote_copy(
            src_ref=r_out.at[j],
            dst_ref=r_in.at[j],
            send_sem=r_sent.at[j],
            recv_sem=r_got.at[j],
            device_id=partner,
            device_id_type=MESH,
        )

    def l_copy(j, sector):
        return pltpu.make_async_remote_copy(
            src_ref=l_out.at[j],
            dst_ref=l_in.at[sector],
            send_sem=l_sent.at[j],
            recv_sem=l_got.at[sector // 2],
            device_id=partner,
            device_id_type=MESH,
        )

    def arrive(sector):
        @pl.when(sector != me)
        def _():
            x_copy(me, sector).wait_recv()

    def pair(j):
        return at_step(pair_order, j)

    def hand_over(j):
        g = pair(j)
        arrive(2 * g + 1)

        @pl.when(at_step(new_first, j) == 1)
        def _():
            arrive(2 * g)

        @pl.when(at_step(new_last, j) == 1)
        def _():
            arrive(lax.rem(2 * g + 2, sectors))

        other = 2 * g + 1 - h
        r_out[j] = x_in[other] - x_in[lax.rem(other + 1, sectors)]
        r_copy(j).start()

    def contact(j):
        g = pair(j)
        sector = 2 * g + h
        own = x_in[sector] - x_in[lax.rem(sector + 1, sectors)]

        @pl.when(sector != me)
        def _():
            s_copy(me, sector).wait_recv()

        r_copy(j).wait_recv()
        far = r_in[j]
        rows = [jnp.concatenate([own[32 * i : 32 * i + 32], far[32 * i : 32 * i + 32]], 0) for i in range(3)]
        gaps_rows = pl.ds(pl.multiple_of(ROW_GAPS + 128 * h, 8), 128)
        moved = product(table[gaps_rows, 0:64], jnp.concatenate(rows, 1))
        law = s_in[g, 0:8, :]
        n0, kn, kt, mu = law[0:1], law[1:2], law[2:3], law[3:4]
        step = 32
        for start in range(0, 128, step):
            packed = s_in[g, 8 + start % 64 : 8 + start % 64 + step, :]
            turned = pltpu.roll(packed, HALF, 1)
            left = low(step)
            z = jnp.where(left, packed, turned) if start < 64 else jnp.where(left, turned, packed)
            raw = [moved[start : start + step, LANES * i : LANES * (i + 1)] for i in range(3)]
            swapped = [pltpu.roll(value, HALF, 1) for value in raw]
            gap = [jnp.where(left, u, v) for u, v in zip(raw, swapped)]
            dgap = [jnp.where(left, v, u) for u, v in zip(raw, swapped)]
            touching = (z < 1.5).astype(jnp.float32)
            sliding = jnp.logical_and(z > 0.5, z < 1.5)
            normal = (n0 + kn * gap[0]) * touching
            dnormal = kn * dgap[0] * touching
            inverse = lax.rsqrt(gap[1] * gap[1] + gap[2] * gap[2] + 1.0)
            along = (gap[1] * dgap[1] + gap[2] * dgap[2]) * (inverse * inverse)
            tractions[start : start + step, 0:LANES] = jnp.where(left, normal, dnormal)
            rub = mu * inverse
            for i in (1, 2):
                slipped = normal * gap[i]
                dslipped = dnormal * gap[i] + normal * (dgap[i] - gap[i] * along)
                stuck = kt * raw[i] * touching
                tractions[start : start + step, LANES * i : LANES * (i + 1)] = jnp.where(
                    sliding, rub * jnp.where(left, slipped, dslipped), stuck
                )
        loads_rows = pl.ds(pl.multiple_of(ROW_LOADS + 64 * h, 8), 64)
        loads = product(table[loads_rows, :], tractions[...])
        for i in range(3):
            l_out[j, 32 * i : 32 * i + 32, :] = loads[32:64, LANES * i : LANES * (i + 1)]
        l_copy(j, sector).start()
        for i in range(3):
            l_in[sector, 32 * i : 32 * i + 32, :] = loads[0:32, LANES * i : LANES * (i + 1)]
        l_keep(sector).start()

    hand_over(jnp.int32(0))

    def turn(j, carry):
        @pl.when(j < pairs - 1)
        def _():
            hand_over(j + 1)

        @pl.when(j == pairs - 2)
        def _():
            x_keep.start()

        contact(j)
        return carry

    lax.fori_loop(0, pairs, turn, 0)

    def loads_here(j, carry):
        sector = 2 * pair(j) + 1 - h
        l_copy(j, sector).wait_recv()
        l_keep(sector).start()
        return carry

    lax.fori_loop(0, pairs, loads_here, 0)

    def sent(i, carry):
        to = lax.rem(me + i, sectors)
        x_copy(to, me).wait_send()

        @pl.when(mine_here)
        def _():
            s_copy(to, me).wait_send()

        return carry

    lax.fori_loop(1, sectors, sent, 0)

    def sent_back(j, carry):
        r_copy(j).wait_send()
        l_copy(j, 2 * pair(j) + h).wait_send()
        return carry

    lax.fori_loop(0, pairs, sent_back, 0)
    linear_copy.wait()
    x_keep.wait()

    def kept(i, carry):
        l_keep(i).wait()
        return carry

    lax.fori_loop(0, sectors, kept, 0)


def to_diameters(x_in, l_in, linear, reaction, excitation, residual, jvp):
    matrix = jnp.concatenate([linear[0], reaction[...]], 1)
    columns = []
    for i in range(3):
        field = [x_in[:, i].reshape(128, LANES), l_in[:, i].reshape(128, LANES)]
        columns.append(jnp.concatenate(field, 0))
    out = product(matrix, jnp.concatenate(columns, 1), lax.Precision.HIGH)
    for i in range(3):
        both = out[:, LANES * i : LANES * (i + 1)]
        first = both[:, 0:HALF].reshape(8, 16, HALF)
        second = pltpu.roll(both, HALF, 1)[:, 0:HALF].reshape(8, 16, HALF)
        residual[i] = first - excitation[i]
        jvp[i] = second


def body_in_kernel(
    disp,
    direction,
    stick_state,
    contact_params,
    mistuning,
    group_ids,
    diag_stiff,
    cross_stiff,
    excitation,
):
    hbm = pl.BlockSpec(memory_space=pltpu.HBM)
    dma = pltpu.SemaphoreType.DMA
    f32 = jnp.float32
    table = constant_table(16, 64, 128)
    x_in, l_in, linear = pl.pallas_call(
        kernel,
        out_shape=(
            jax.ShapeDtypeStruct((16, 96, LANES), f32),
            jax.ShapeDtypeStruct((16, 96, LANES), f32),
            jax.ShapeDtypeStruct((4, 128, LANES), f32),
        ),
        in_specs=[hbm] * 9,
        out_specs=(hbm, hbm, hbm),
        scratch_shapes=[
            pltpu.VMEM((96, 1024), f32),
            pltpu.VMEM((96, 1024), f32),
            pltpu.VMEM((128, 1024), jnp.int32),
            pltpu.VMEM((4, 1024), f32),
            pltpu.VMEM((1, 16), f32),
            pltpu.VMEM((1, 16), jnp.int32),
            pltpu.VMEM((16, 32), f32),
            pltpu.VMEM((16, 32), f32),
            pltpu.VMEM((ROWS, LANES), f32),
            dma((6,)),
            dma((3, 4)),
            pltpu.VMEM((16, 96, LANES), f32),
            pltpu.VMEM((16, 72, LANES), f32),
            pltpu.VMEM((16, 96, LANES), f32),
            pltpu.VMEM((8, 72, LANES), f32),
            pltpu.VMEM((8, 96, LANES), f32),
            pltpu.VMEM((8, 96, LANES), f32),
            pltpu.VMEM((8, 96, LANES), f32),
            pltpu.VMEM((16, 96, LANES), f32),
            pltpu.VMEM((8, 1024), f32),
            pltpu.VMEM((128, 3 * LANES), f32),
            pltpu.VMEM((4, 128, LANES), f32),
            dma(()),
            dma((16,)),
            dma(()),
            dma((16,)),
            dma((16,)),
            dma((16,)),
            dma((8,)),
            dma((8,)),
            dma((8,)),
            dma((8,)),
            dma((8,)),
        ],
        compiler_params=pltpu.CompilerParams(
            collective_id=0, has_side_effects=True, vmem_limit_bytes=VMEM_KERNEL
        ),
    )(
        disp.reshape(96, 1024),
        direction.reshape(96, 1024),
        stick_state[0],
        contact_params[0],
        mistuning[None],
        group_ids[None],
        diag_stiff.T,
        cross_stiff.T,
        jnp.asarray(table),
    )
    out = jax.ShapeDtypeStruct((3, 32, 16, HALF), f32)
    fields = pl.BlockSpec((16, 3, 8, LANES), lambda b: (0, 0, b, 0))
    results = pl.BlockSpec((3, 8, 16, HALF), lambda b: (0, b, 0, 0))
    residual, jvp = pl.pallas_call(
        to_diameters,
        grid=(4,),
        out_shape=(out, out),
        in_specs=[
            fields,
            fields,
            pl.BlockSpec((1, 128, LANES), lambda b: (b, 0, 0)),
            pl.BlockSpec((128, LANES), lambda b: (0, 0)),
            results,
        ],
        out_specs=(results, results),
        compiler_params=pltpu.CompilerParams(vmem_limit_bytes=VMEM_KERNEL),
    )(
        x_in.reshape(16, 3, 32, LANES),
        l_in.reshape(16, 3, 32, LANES),
        linear,
        jnp.asarray(table[ROW_LOAD : ROW_LOAD + 128]),
        jnp.swapaxes(excitation, 2, 3),
    )
    return (jnp.swapaxes(residual, 2, 3), jnp.swapaxes(jvp, 2, 3))


def solution(mesh):
    in_specs = (
        P("sector", None, "harm", None),
        P("sector", None, "harm", None),
        P("sector", None, None),
        P("sector", None, None),
        P(),
        P(),
        P("harm", None),
        P("harm", None),
        P(None, "harm", "sector", None),
    )
    out_specs = (P(None, "harm", "sector", None), P(None, "harm", "sector", None))

    def body(*arrays):
        _, channels, coefs, nodes = arrays[0].shape
        sizes = (mesh.shape["sector"], mesh.shape["harm"], channels, coefs, nodes, arrays[2].shape[1])
        if sizes == (16, 2, 3, 32, 1024, 128):
            return body_in_kernel(*arrays)
        return body_any_size(*arrays)

    return jax.shard_map(body, mesh=mesh, in_specs=in_specs, out_specs=out_specs, check_vma=False)
```

```python
import math

import jax
import jax.numpy as jnp
import numpy as np
from jax import lax
from jax.experimental import pallas as pl
from jax.experimental.pallas import tpu as pltpu
from jax.sharding import PartitionSpec as P

MESH = pl.DeviceIdType.MESH

exact_mode = lax.Precision.HIGHEST


def passed_along(value, axis, steps):
    count = lax.axis_size(axis)
    pairs = [(source, (source + steps) % count) for source in range(count)]
    return lax.ppermute(value, axis, pairs)


def from_behind(block, axis, distance):
    devices = range(lax.axis_size(axis))
    route = [(i - distance, i) for i in devices if i - distance in devices]
    return lax.ppermute(block, axis, route)


def basis_table(coefs, samples):
    coef_index = lax.broadcasted_iota(jnp.int32, (coefs, samples), 0)
    time_index = lax.broadcasted_iota(jnp.int32, (coefs, samples), 1)
    harmonic = coef_index // 2 + 1
    phase = harmonic * time_index % samples
    angle = phase.astype(jnp.float32) * (2.0 * math.pi / samples)
    return jnp.where(coef_index % 2 == 0, jnp.cos(angle), jnp.sin(angle))


def hartley_table(count):
    row_index = lax.broadcasted_iota(jnp.int32, (count, count), 0)
    col_index = lax.broadcasted_iota(jnp.int32, (count, count), 1)
    phase = row_index * col_index % count
    angle = phase.astype(jnp.float32) * (2.0 * math.pi / count)
    return (jnp.cos(angle) + jnp.sin(angle)) / math.sqrt(count)


def contact_law(gaps, dgaps, states_here, params):
    preload = params[0]
    normal_stiff = params[1]
    tangent_stiff = params[2]
    friction_coef = params[3]
    touching = (states_here != 2).astype(jnp.float32)
    sliding = states_here == 1
    normal = (preload + normal_stiff * gaps[0]) * touching
    dnormal = normal_stiff * dgaps[0] * touching
    radius = jnp.sqrt(gaps[1] * gaps[1] + gaps[2] * gaps[2] + 1.0)
    projected = (gaps[1] * dgaps[1] + gaps[2] * dgaps[2]) / (radius * radius * radius)
    tractions = [normal]
    dtractions = [dnormal]
    for channel in (1, 2):
        stuck = tangent_stiff * gaps[channel]
        dstuck = tangent_stiff * dgaps[channel]
        slipped = friction_coef * normal * gaps[channel] / radius
        dslipped = friction_coef * (
            dnormal * gaps[channel] / radius
            + normal * (dgaps[channel] / radius - gaps[channel] * projected)
        )
        tractions.append(jnp.where(sliding, slipped, stuck) * touching)
        dtractions.append(jnp.where(sliding, dslipped, dstuck) * touching)
    return (jnp.stack(tractions), jnp.stack(dtractions))


def mirror(field):
    return jnp.roll(jnp.flip(field, -1), 1, -1)


def group_flag(group_ids, own_group, other_index, sectors):
    inside = jnp.logical_and(other_index >= 0, other_index < sectors)
    safe_index = jnp.clip(other_index, 0, sectors - 1)
    other_group = lax.dynamic_slice_in_dim(group_ids, safe_index, 1)
    return jnp.logical_and(inside, other_group == own_group).astype(jnp.float32)[0]


def body_any_size(
    disp,
    direction,
    stick_state,
    contact_params,
    mistuning,
    group_ids,
    diag_stiff,
    cross_stiff,
    excitation,
):
    sectors = lax.axis_size("sector")
    sector_index = lax.axis_index("sector")
    harm_index = lax.axis_index("harm")
    local_coefs = disp.shape[2]
    samples = stick_state.shape[1]
    coefs = local_coefs * lax.axis_size("harm")
    table = basis_table(coefs, samples)
    own_table = lax.dynamic_slice_in_dim(table, harm_index * local_coefs, local_coefs, 0)
    scale = 2.0 / samples
    hartley = hartley_table(sectors)
    paired = jnp.concatenate([disp, direction], 0)
    paired_next = passed_along(paired, "sector", -1)
    relative = paired - paired_next
    gathered = lax.all_gather(relative, "harm", axis=2, tiled=True)
    params_here = contact_params[0]
    gaps = jnp.einsum("wcjp,jt->wctp", gathered, table, precision=exact_mode)
    traction, dtraction = contact_law(gaps[0], gaps[1], stick_state[0], params_here)
    loads = (
        jnp.einsum(
            "wctp,jt->wcjp", jnp.stack([traction, dtraction]), own_table, precision=exact_mode
        )
        * scale
    )
    earlier_loads = passed_along(loads, "sector", 1)
    own_group = lax.dynamic_slice_in_dim(group_ids, sector_index, 1)
    members = jnp.sum((group_ids == own_group[0]).astype(jnp.float32))
    totals = paired
    for offset in range(1, 8):
        from_before = from_behind(paired, "sector", offset)
        from_after = from_behind(paired, "sector", -offset)
        flag_before = group_flag(group_ids, own_group, sector_index - offset, sectors)
        flag_after = group_flag(group_ids, own_group, sector_index + offset, sectors)
        totals = totals + flag_before * from_before + flag_after * from_after
    weight = lax.dynamic_slice_in_dim(mistuning, sector_index, 1)[0]
    forces = loads - earlier_loads + weight * (paired - totals / members)
    outgoing = jnp.concatenate([paired, forces], 0)
    received = lax.all_to_all(outgoing[:, None], "sector", split_axis=4, concat_axis=1, tiled=True)
    states_nd = jnp.einsum("ks,wscjp->wcjpk", hartley, received[0:2], precision=exact_mode)
    forces_nd = jnp.einsum("ks,wscjp->wcjpk", hartley, received[2:4], precision=exact_mode)
    stiff_diag = diag_stiff[None, :, None, :]
    stiff_cross = cross_stiff[None, :, None, :]
    residual = (
        stiff_diag * states_nd[0] + stiff_cross * mirror(states_nd[0]) + forces_nd[0] - excitation
    )
    jvp = stiff_diag * states_nd[1] + stiff_cross * mirror(states_nd[1]) + forces_nd[1]
    return (residual, jvp)


LANES = 128
VMEM_KERNEL = 63 * 1024 * 1024
HALF = 64
ROW_HARTLEY = 0
ROW_MIRROR = 16
ROW_SPREAD = 32
ROW_LOAD = 48
ROW_SAME = 176
ROW_COEF = 304
ROW_PICK = 432
ROW_SQUARE = 560
ROW_LOADS = 576
ROW_GAPS = 704
ROWS = 960


def constant_table(sectors, coefs, samples):
    k = np.arange(sectors)
    phase = 2.0 * np.pi * (np.outer(k, k) % sectors) / sectors
    hartley = (np.cos(phase) + np.sin(phase)) / math.sqrt(sectors)
    out = np.zeros((ROWS, LANES), np.float64)
    lane_sector, lane_coef = np.arange(LANES) // 8, np.arange(LANES) % 8
    row_coef, row_k = np.arange(LANES) // sectors, np.arange(LANES) % sectors
    out[ROW_HARTLEY : ROW_HARTLEY + 16] = hartley[:, lane_sector]
    out[ROW_MIRROR : ROW_MIRROR + 16] = hartley[(-k) % sectors][:, lane_sector]
    out[ROW_SPREAD : ROW_SPREAD + 16] = k[:, None] == lane_sector[None, :]
    same = row_coef[:, None] == lane_coef[None, :]
    reaction = hartley - np.roll(hartley, -1, 1)
    out[ROW_LOAD : ROW_LOAD + 128] = same * reaction[row_k][:, lane_sector]
    out[ROW_SAME : ROW_SAME + 128] = same
    out[ROW_COEF : ROW_COEF + 128, 0:8] = row_coef[:, None] == np.arange(8)[None, :]
    out[ROW_PICK : ROW_PICK + 128, 0:16] = row_k[:, None] == k[None, :]
    out[ROW_SQUARE : ROW_SQUARE + 16, 0:16] = hartley
    c, t = np.arange(coefs), np.arange(samples)
    angle = 2.0 * np.pi * (np.outer(c // 2 + 1, t) % samples) / samples
    basis = np.where(c[:, None] % 2 == 0, np.cos(angle), np.sin(angle))
    for h in range(2):
        ordered = np.roll(basis, -h * (coefs // 2), 0)
        out[ROW_LOADS + 64 * h : ROW_LOADS + 64 * (h + 1)] = ordered * (2.0 / samples)
        out[ROW_GAPS + 128 * h : ROW_GAPS + 128 * (h + 1), 0:64] = ordered.T
    return out.astype(np.float32)


def product(a, b, precision=lax.Precision.HIGH):
    return jnp.dot(a, b, preferred_element_type=jnp.float32, precision=precision)


SEND_ORDER = ((0, 2, 3, 1), (1, 0, 2, 3), (2, 3, 1, 0), (3, 1, 0, 2))
PAIR_ORDER = (
    (0, 1, 2, 6, 7, 3, 4, 5),
    (2, 6, 3, 4, 5, 7, 0, 1),
    (4, 0, 1, 2, 3, 5, 6, 7),
    (6, 4, 5, 7, 0, 1, 2, 3),
)


def seen(z, k, step):
    order = PAIR_ORDER[z]
    return int((order[k] + step) % 8 not in order[:k])


def kernel(
    disp_hbm,
    direction_hbm,
    states_hbm,
    params_hbm,
    mistuning_hbm,
    groups_hbm,
    diag_hbm,
    cross_hbm,
    table_hbm,
    x_hbm,
    l_hbm,
    linear_hbm,
    disp,
    direction,
    states,
    params,
    mistuning,
    groups,
    diag,
    cross,
    table,
    fetched,
    fetched_parts,
    x_out,
    s_out,
    x_in,
    s_in,
    r_out,
    r_in,
    l_out,
    l_in,
    params8,
    tractions,
    linear,
    x_kept,
    l_kept,
    linear_kept,
    x_sent,
    x_got,
    s_sent,
    s_got,
    r_sent,
    r_got,
    l_sent,
    l_got,
):
    sectors = 16
    pairs = sectors // 2
    me = lax.axis_index("sector")
    h = lax.axis_index("harm")
    g0 = me // 2
    z0 = me // 4
    partner = (me, 1 - h)

    def by_z(values):
        out = jnp.int32(values[3])
        for z in (2, 1, 0):
            out = jnp.where(z0 == z, values[z], out)
        return out

    def at_step(column, j):
        out = column[-1]
        for k in range(len(column) - 2, -1, -1):
            out = jnp.where(j == k, column[k], out)
        return out

    send_order = [by_z([SEND_ORDER[z][k] for z in range(4)]) for k in range(4)]
    pair_order = [by_z([PAIR_ORDER[z][k] for z in range(4)]) for k in range(8)]
    new_first = [by_z([seen(z, k, -1) for z in range(4)]) for k in range(8)]
    new_last = [by_z([seen(z, k, 1) for z in range(4)]) for k in range(8)]

    def part(i, z):
        lanes = pl.ds(pl.multiple_of(z * 2 * LANES, 2 * LANES), 2 * LANES)
        source, target = ((disp_hbm, disp), (direction_hbm, direction), (states_hbm, states))[i]
        return pltpu.make_async_copy(
            source.at[:, lanes], target.at[:, lanes], fetched_parts.at[i, z]
        )

    given = (params_hbm, mistuning_hbm, groups_hbm, diag_hbm, cross_hbm, table_hbm)
    held = (params, mistuning, groups, diag, cross, table)
    fetches = [
        pltpu.make_async_copy(source, target, fetched.at[i])
        for i, (source, target) in enumerate(zip(given, held))
    ]
    for k in range(4):
        for i in range(3):
            part(i, send_order[k]).start()
        if k == 0:
            fetches[0].start()
    for fetch in fetches[1:]:
        fetch.start()

    barrier = pltpu.get_barrier_semaphore()

    def greet(i, carry):
        pl.semaphore_signal(
            barrier, inc=1, device_id=(lax.rem(me + i, sectors), h), device_id_type=MESH
        )
        return carry

    lax.fori_loop(1, sectors, greet, 0)
    pl.semaphore_signal(barrier, inc=1, device_id=partner, device_id_type=MESH)

    def low(rows):
        return lax.broadcasted_iota(jnp.int32, (rows, LANES), 1) < HALF

    def pack(g):
        lanes = pl.ds(pl.multiple_of(g * LANES, LANES), LANES)
        a, b = disp[:, lanes], direction[:, lanes]
        x_out[2 * g] = jnp.where(low(96), a, pltpu.roll(b, HALF, 1))
        x_out[2 * g + 1] = jnp.where(low(96), pltpu.roll(a, HALF, 1), b)
        z = states[:, lanes].astype(jnp.float32)
        early, late = z[0:64], z[64:128]
        s_out[2 * g, 8:72, :] = jnp.where(low(64), early, pltpu.roll(late, HALF, 1))
        s_out[2 * g + 1, 8:72, :] = jnp.where(low(64), pltpu.roll(early, HALF, 1), late)
        p = params8[:, lanes]
        turned = pltpu.roll(p, HALF, 1)
        s_out[2 * g, 0:8, :] = jnp.where(low(8), p, turned)
        s_out[2 * g + 1, 0:8, :] = jnp.where(low(8), turned, p)

    def x_copy(to, source):
        return pltpu.make_async_remote_copy(
            src_ref=x_out.at[to],
            dst_ref=x_in.at[source],
            send_sem=x_sent.at[to],
            recv_sem=x_got.at[source],
            device_id=(to, h),
            device_id_type=MESH,
        )

    def s_copy(to, source):
        return pltpu.make_async_remote_copy(
            src_ref=s_out.at[to],
            dst_ref=s_in.at[source // 2],
            send_sem=s_sent.at[to],
            recv_sem=s_got.at[source // 2],
            device_id=(to, h),
            device_id_type=MESH,
        )

    mine_here = lax.rem(me, 2) == h
    core, x = lax.rem(me, 2), lax.rem(g0, 2)

    def prepare(k):
        z = at_step(send_order, k)
        for i in range(3):
            part(i, z).wait()
        pack(2 * z)
        pack(2 * z + 1)

    def send(z, q):
        to = 4 * z + 2 * lax.rem(q + core, 2) + lax.rem(q // 2 + x, 2)

        @pl.when(to != me)
        def _():
            x_copy(to, me).start()

            @pl.when(mine_here)
            def _():
                s_copy(to, me).start()

    def first_sends(k, carry):
        prepare(k)

        @pl.when(k == 0)
        def _():
            x_in[me] = x_out[me]

            @pl.when(mine_here)
            def _():
                s_in[g0] = s_out[me]

            pl.semaphore_wait(barrier, sectors)

        for q in range(4):
            send(at_step(send_order, k), q)
        return carry

    fetches[0].wait()
    params8[0:4, :] = params[...]
    params8[4:8, :] = params[...]
    lax.fori_loop(0, 2, first_sends, 0)
    prepare(2)
    prepare(3)
    for fetch in fetches[1:]:
        fetch.wait()

    square = table[ROW_SQUARE : ROW_SQUARE + 16, 0:16]
    row = lax.broadcasted_iota(jnp.int32, (16, 16), 0)
    col = lax.broadcasted_iota(jnp.int32, (16, 16), 1)
    group_row = jnp.broadcast_to(groups[...].astype(jnp.float32), (16, 16))
    group_col = jnp.sum(jnp.where(row == col, group_row, 0.0), axis=1, keepdims=True)
    together = (group_row == group_col).astype(jnp.float32)
    mean = together / jnp.sum(together, axis=0, keepdims=True)
    weighted = square * mistuning[...]
    exact = lax.Precision.HIGHEST
    tuned = weighted - product(weighted, mean, exact)
    tuned = product(tuned, table[ROW_SPREAD : ROW_SPREAD + 16, :], exact)
    pick = table[ROW_PICK : ROW_PICK + 128, 0:16]
    same = table[ROW_SAME : ROW_SAME + 128, :]
    plain = product(pick, table[ROW_HARTLEY : ROW_HARTLEY + 16, :], exact)
    turned_back = product(pick, table[ROW_MIRROR : ROW_MIRROR + 16, :], exact)
    tuned = product(pick, tuned, exact)
    diag_rows = product(pick, diag[...], exact)
    cross_rows = product(pick, cross[...], exact)
    coef_here = lax.broadcasted_iota(jnp.int32, (128, 32), 0) // 16
    coef_lane = lax.broadcasted_iota(jnp.int32, (128, 32), 1)
    for b in range(4):
        chosen = coef_lane == coef_here + 8 * b
        d = jnp.sum(jnp.where(chosen, diag_rows, 0.0), axis=1, keepdims=True)
        c = jnp.sum(jnp.where(chosen, cross_rows, 0.0), axis=1, keepdims=True)
        linear[b] = same * (d * plain + c * turned_back + tuned)

    linear_copy = pltpu.make_async_copy(linear, linear_hbm, linear_kept)
    linear_copy.start()
    x_keep = pltpu.make_async_copy(x_in, x_hbm, x_kept)

    def l_keep(sector):
        return pltpu.make_async_copy(l_in.at[sector], l_hbm.at[sector], l_kept.at[sector])

    def r_copy(j):
        return pltpu.make_async_remote_copy(
            src_ref=r_out.at[j],
            dst_ref=r_in.at[j],
            send_sem=r_sent.at[j],
            recv_sem=r_got.at[j],
            device_id=partner,
            device_id_type=MESH,
        )

    def l_copy(j, sector):
        return pltpu.make_async_remote_copy(
            src_ref=l_out.at[j],
            dst_ref=l_in.at[sector],
            send_sem=l_sent.at[j],
            recv_sem=l_got.at[sector // 2],
            device_id=partner,
            device_id_type=MESH,
        )

    def arrive(sector):
        @pl.when(sector != me)
        def _():
            x_copy(me, sector).wait_recv()

    def pair(j):
        return at_step(pair_order, j)

    def hand_over(j):
        g = pair(j)
        arrive(2 * g + 1)

        @pl.when(at_step(new_first, j) == 1)
        def _():
            arrive(2 * g)

        @pl.when(at_step(new_last, j) == 1)
        def _():
            arrive(lax.rem(2 * g + 2, sectors))

        other = 2 * g + 1 - h
        r_out[j] = x_in[other] - x_in[lax.rem(other + 1, sectors)]
        r_copy(j).start()

    def contact(j):
        g = pair(j)
        sector = 2 * g + h
        own = x_in[sector] - x_in[lax.rem(sector + 1, sectors)]

        @pl.when(sector != me)
        def _():
            s_copy(me, sector).wait_recv()

        r_copy(j).wait_recv()
        far = r_in[j]
        rows = [jnp.concatenate([own[32 * i : 32 * i + 32], far[32 * i : 32 * i + 32]], 0) for i in range(3)]
        gaps_rows = pl.ds(pl.multiple_of(ROW_GAPS + 128 * h, 8), 128)
        moved = product(table[gaps_rows, 0:64], jnp.concatenate(rows, 1))
        law = s_in[g, 0:8, :]
        n0, kn, kt, mu = law[0:1], law[1:2], law[2:3], law[3:4]
        step = 32
        for start in range(0, 128, step):
            packed = s_in[g, 8 + start % 64 : 8 + start % 64 + step, :]
            turned = pltpu.roll(packed, HALF, 1)
            left = low(step)
            z = jnp.where(left, packed, turned) if start < 64 else jnp.where(left, turned, packed)
            raw = [moved[start : start + step, LANES * i : LANES * (i + 1)] for i in range(3)]
            swapped = [pltpu.roll(value, HALF, 1) for value in raw]
            gap = [jnp.where(left, u, v) for u, v in zip(raw, swapped)]
            dgap = [jnp.where(left, v, u) for u, v in zip(raw, swapped)]
            touching = (z < 1.5).astype(jnp.float32)
            sliding = jnp.logical_and(z > 0.5, z < 1.5)
            normal = (n0 + kn * gap[0]) * touching
            dnormal = kn * dgap[0] * touching
            inverse = lax.rsqrt(gap[1] * gap[1] + gap[2] * gap[2] + 1.0)
            along = (gap[1] * dgap[1] + gap[2] * dgap[2]) * (inverse * inverse)
            tractions[start : start + step, 0:LANES] = jnp.where(left, normal, dnormal)
            rub = mu * inverse
            for i in (1, 2):
                slipped = normal * gap[i]
                dslipped = dnormal * gap[i] + normal * (dgap[i] - gap[i] * along)
                stuck = kt * raw[i] * touching
                tractions[start : start + step, LANES * i : LANES * (i + 1)] = jnp.where(
                    sliding, rub * jnp.where(left, slipped, dslipped), stuck
                )
        loads_rows = pl.ds(pl.multiple_of(ROW_LOADS + 64 * h, 8), 64)
        loads = product(table[loads_rows, :], tractions[...])
        for i in range(3):
            l_out[j, 32 * i : 32 * i + 32, :] = loads[32:64, LANES * i : LANES * (i + 1)]
        l_copy(j, sector).start()
        for i in range(3):
            l_in[sector, 32 * i : 32 * i + 32, :] = loads[0:32, LANES * i : LANES * (i + 1)]
        l_keep(sector).start()

    hand_over(jnp.int32(0))

    def turn(j, carry):
        @pl.when(j < 4)
        def _():
            z = at_step(send_order, 2 + j // 2)
            for q in range(2):
                send(z, 2 * lax.rem(j, 2) + q)

        @pl.when(j < pairs - 1)
        def _():
            hand_over(j + 1)

        @pl.when(j == pairs - 2)
        def _():
            x_keep.start()

        contact(j)
        return carry

    lax.fori_loop(0, pairs, turn, 0)

    def loads_here(j, carry):
        sector = 2 * pair(j) + 1 - h
        l_copy(j, sector).wait_recv()
        l_keep(sector).start()
        return carry

    lax.fori_loop(0, pairs, loads_here, 0)

    def sent(i, carry):
        to = lax.rem(me + i, sectors)
        x_copy(to, me).wait_send()

        @pl.when(mine_here)
        def _():
            s_copy(to, me).wait_send()

        return carry

    lax.fori_loop(1, sectors, sent, 0)

    def sent_back(j, carry):
        r_copy(j).wait_send()
        l_copy(j, 2 * pair(j) + h).wait_send()
        return carry

    lax.fori_loop(0, pairs, sent_back, 0)
    linear_copy.wait()
    x_keep.wait()

    def kept(i, carry):
        l_keep(i).wait()
        return carry

    lax.fori_loop(0, sectors, kept, 0)


def to_diameters(x_in, l_in, linear, reaction, excitation, residual, jvp):
    matrix = jnp.concatenate([linear[0], reaction[...]], 1)
    columns = []
    for i in range(3):
        field = [x_in[:, i].reshape(128, LANES), l_in[:, i].reshape(128, LANES)]
        columns.append(jnp.concatenate(field, 0))
    out = product(matrix, jnp.concatenate(columns, 1), lax.Precision.HIGH)
    for i in range(3):
        both = out[:, LANES * i : LANES * (i + 1)]
        first = both[:, 0:HALF].reshape(8, 16, HALF)
        second = pltpu.roll(both, HALF, 1)[:, 0:HALF].reshape(8, 16, HALF)
        residual[i] = first - excitation[i]
        jvp[i] = second


def body_in_kernel(
    disp,
    direction,
    stick_state,
    contact_params,
    mistuning,
    group_ids,
    diag_stiff,
    cross_stiff,
    excitation,
):
    hbm = pl.BlockSpec(memory_space=pltpu.HBM)
    dma = pltpu.SemaphoreType.DMA
    f32 = jnp.float32
    table = constant_table(16, 64, 128)
    x_in, l_in, linear = pl.pallas_call(
        kernel,
        out_shape=(
            jax.ShapeDtypeStruct((16, 96, LANES), f32),
            jax.ShapeDtypeStruct((16, 96, LANES), f32),
            jax.ShapeDtypeStruct((4, 128, LANES), f32),
        ),
        in_specs=[hbm] * 9,
        out_specs=(hbm, hbm, hbm),
        scratch_shapes=[
            pltpu.VMEM((96, 1024), f32),
            pltpu.VMEM((96, 1024), f32),
            pltpu.VMEM((128, 1024), jnp.int32),
            pltpu.VMEM((4, 1024), f32),
            pltpu.VMEM((1, 16), f32),
            pltpu.VMEM((1, 16), jnp.int32),
            pltpu.VMEM((16, 32), f32),
            pltpu.VMEM((16, 32), f32),
            pltpu.VMEM((ROWS, LANES), f32),
            dma((6,)),
            dma((3, 4)),
            pltpu.VMEM((16, 96, LANES), f32),
            pltpu.VMEM((16, 72, LANES), f32),
            pltpu.VMEM((16, 96, LANES), f32),
            pltpu.VMEM((8, 72, LANES), f32),
            pltpu.VMEM((8, 96, LANES), f32),
            pltpu.VMEM((8, 96, LANES), f32),
            pltpu.VMEM((8, 96, LANES), f32),
            pltpu.VMEM((16, 96, LANES), f32),
            pltpu.VMEM((8, 1024), f32),
            pltpu.VMEM((128, 3 * LANES), f32),
            pltpu.VMEM((4, 128, LANES), f32),
            dma(()),
            dma((16,)),
            dma(()),
            dma((16,)),
            dma((16,)),
            dma((16,)),
            dma((8,)),
            dma((8,)),
            dma((8,)),
            dma((8,)),
            dma((8,)),
        ],
        compiler_params=pltpu.CompilerParams(
            collective_id=0, has_side_effects=True, vmem_limit_bytes=VMEM_KERNEL
        ),
    )(
        disp.reshape(96, 1024),
        direction.reshape(96, 1024),
        stick_state[0],
        contact_params[0],
        mistuning[None],
        group_ids[None],
        diag_stiff.T,
        cross_stiff.T,
        jnp.asarray(table),
    )
    out = jax.ShapeDtypeStruct((3, 32, 16, HALF), f32)
    fields = pl.BlockSpec((16, 3, 8, LANES), lambda b: (0, 0, b, 0))
    results = pl.BlockSpec((3, 8, 16, HALF), lambda b: (0, b, 0, 0))
    residual, jvp = pl.pallas_call(
        to_diameters,
        grid=(4,),
        out_shape=(out, out),
        in_specs=[
            fields,
            fields,
            pl.BlockSpec((1, 128, LANES), lambda b: (b, 0, 0)),
            pl.BlockSpec((128, LANES), lambda b: (0, 0)),
            results,
        ],
        out_specs=(results, results),
        compiler_params=pltpu.CompilerParams(vmem_limit_bytes=VMEM_KERNEL),
    )(
        x_in.reshape(16, 3, 32, LANES),
        l_in.reshape(16, 3, 32, LANES),
        linear,
        jnp.asarray(table[ROW_LOAD : ROW_LOAD + 128]),
        jnp.swapaxes(excitation, 2, 3),
    )
    return (jnp.swapaxes(residual, 2, 3), jnp.swapaxes(jvp, 2, 3))


def solution(mesh):
    in_specs = (
        P("sector", None, "harm", None),
        P("sector", None, "harm", None),
        P("sector", None, None),
        P("sector", None, None),
        P(),
        P(),
        P("harm", None),
        P("harm", None),
        P(None, "harm", "sector", None),
    )
    out_specs = (P(None, "harm", "sector", None), P(None, "harm", "sector", None))

    def body(*arrays):
        _, channels, coefs, nodes = arrays[0].shape
        sizes = (mesh.shape["sector"], mesh.shape["harm"], channels, coefs, nodes, arrays[2].shape[1])
        if sizes == (16, 2, 3, 32, 1024, 128):
            return body_in_kernel(*arrays)
        return body_any_size(*arrays)

    return jax.shard_map(body, mesh=mesh, in_specs=in_specs, out_specs=out_specs, check_vma=False)
```

```python
import math

import jax
import jax.numpy as jnp
import numpy as np
from jax import lax
from jax.experimental import pallas as pl
from jax.experimental.pallas import tpu as pltpu
from jax.sharding import PartitionSpec as P

MESH = pl.DeviceIdType.MESH

exact_mode = lax.Precision.HIGHEST


def passed_along(value, axis, steps):
    count = lax.axis_size(axis)
    pairs = [(source, (source + steps) % count) for source in range(count)]
    return lax.ppermute(value, axis, pairs)


def from_behind(block, axis, distance):
    devices = range(lax.axis_size(axis))
    route = [(i - distance, i) for i in devices if i - distance in devices]
    return lax.ppermute(block, axis, route)


def basis_table(coefs, samples):
    coef_index = lax.broadcasted_iota(jnp.int32, (coefs, samples), 0)
    time_index = lax.broadcasted_iota(jnp.int32, (coefs, samples), 1)
    harmonic = coef_index // 2 + 1
    phase = harmonic * time_index % samples
    angle = phase.astype(jnp.float32) * (2.0 * math.pi / samples)
    return jnp.where(coef_index % 2 == 0, jnp.cos(angle), jnp.sin(angle))


def hartley_table(count):
    row_index = lax.broadcasted_iota(jnp.int32, (count, count), 0)
    col_index = lax.broadcasted_iota(jnp.int32, (count, count), 1)
    phase = row_index * col_index % count
    angle = phase.astype(jnp.float32) * (2.0 * math.pi / count)
    return (jnp.cos(angle) + jnp.sin(angle)) / math.sqrt(count)


def contact_law(gaps, dgaps, states_here, params):
    preload = params[0]
    normal_stiff = params[1]
    tangent_stiff = params[2]
    friction_coef = params[3]
    touching = (states_here != 2).astype(jnp.float32)
    sliding = states_here == 1
    normal = (preload + normal_stiff * gaps[0]) * touching
    dnormal = normal_stiff * dgaps[0] * touching
    radius = jnp.sqrt(gaps[1] * gaps[1] + gaps[2] * gaps[2] + 1.0)
    projected = (gaps[1] * dgaps[1] + gaps[2] * dgaps[2]) / (radius * radius * radius)
    tractions = [normal]
    dtractions = [dnormal]
    for channel in (1, 2):
        stuck = tangent_stiff * gaps[channel]
        dstuck = tangent_stiff * dgaps[channel]
        slipped = friction_coef * normal * gaps[channel] / radius
        dslipped = friction_coef * (
            dnormal * gaps[channel] / radius
            + normal * (dgaps[channel] / radius - gaps[channel] * projected)
        )
        tractions.append(jnp.where(sliding, slipped, stuck) * touching)
        dtractions.append(jnp.where(sliding, dslipped, dstuck) * touching)
    return (jnp.stack(tractions), jnp.stack(dtractions))


def mirror(field):
    return jnp.roll(jnp.flip(field, -1), 1, -1)


def group_flag(group_ids, own_group, other_index, sectors):
    inside = jnp.logical_and(other_index >= 0, other_index < sectors)
    safe_index = jnp.clip(other_index, 0, sectors - 1)
    other_group = lax.dynamic_slice_in_dim(group_ids, safe_index, 1)
    return jnp.logical_and(inside, other_group == own_group).astype(jnp.float32)[0]


def body_any_size(
    disp,
    direction,
    stick_state,
    contact_params,
    mistuning,
    group_ids,
    diag_stiff,
    cross_stiff,
    excitation,
):
    sectors = lax.axis_size("sector")
    sector_index = lax.axis_index("sector")
    harm_index = lax.axis_index("harm")
    local_coefs = disp.shape[2]
    samples = stick_state.shape[1]
    coefs = local_coefs * lax.axis_size("harm")
    table = basis_table(coefs, samples)
    own_table = lax.dynamic_slice_in_dim(table, harm_index * local_coefs, local_coefs, 0)
    scale = 2.0 / samples
    hartley = hartley_table(sectors)
    paired = jnp.concatenate([disp, direction], 0)
    paired_next = passed_along(paired, "sector", -1)
    relative = paired - paired_next
    gathered = lax.all_gather(relative, "harm", axis=2, tiled=True)
    params_here = contact_params[0]
    gaps = jnp.einsum("wcjp,jt->wctp", gathered, table, precision=exact_mode)
    traction, dtraction = contact_law(gaps[0], gaps[1], stick_state[0], params_here)
    loads = (
        jnp.einsum(
            "wctp,jt->wcjp", jnp.stack([traction, dtraction]), own_table, precision=exact_mode
        )
        * scale
    )
    earlier_loads = passed_along(loads, "sector", 1)
    own_group = lax.dynamic_slice_in_dim(group_ids, sector_index, 1)
    members = jnp.sum((group_ids == own_group[0]).astype(jnp.float32))
    totals = paired
    for offset in range(1, 8):
        from_before = from_behind(paired, "sector", offset)
        from_after = from_behind(paired, "sector", -offset)
        flag_before = group_flag(group_ids, own_group, sector_index - offset, sectors)
        flag_after = group_flag(group_ids, own_group, sector_index + offset, sectors)
        totals = totals + flag_before * from_before + flag_after * from_after
    weight = lax.dynamic_slice_in_dim(mistuning, sector_index, 1)[0]
    forces = loads - earlier_loads + weight * (paired - totals / members)
    outgoing = jnp.concatenate([paired, forces], 0)
    received = lax.all_to_all(outgoing[:, None], "sector", split_axis=4, concat_axis=1, tiled=True)
    states_nd = jnp.einsum("ks,wscjp->wcjpk", hartley, received[0:2], precision=exact_mode)
    forces_nd = jnp.einsum("ks,wscjp->wcjpk", hartley, received[2:4], precision=exact_mode)
    stiff_diag = diag_stiff[None, :, None, :]
    stiff_cross = cross_stiff[None, :, None, :]
    residual = (
        stiff_diag * states_nd[0] + stiff_cross * mirror(states_nd[0]) + forces_nd[0] - excitation
    )
    jvp = stiff_diag * states_nd[1] + stiff_cross * mirror(states_nd[1]) + forces_nd[1]
    return (residual, jvp)


LANES = 128
VMEM_KERNEL = 63 * 1024 * 1024
HALF = 64
ROW_HARTLEY = 0
ROW_MIRROR = 16
ROW_SPREAD = 32
ROW_LOAD = 48
ROW_SAME = 176
ROW_COEF = 304
ROW_PICK = 432
ROW_SQUARE = 560
ROW_LOADS = 576
ROW_GAPS = 704
ROWS = 960


def constant_table(sectors, coefs, samples):
    k = np.arange(sectors)
    phase = 2.0 * np.pi * (np.outer(k, k) % sectors) / sectors
    hartley = (np.cos(phase) + np.sin(phase)) / math.sqrt(sectors)
    out = np.zeros((ROWS, LANES), np.float64)
    lane_sector, lane_coef = np.arange(LANES) // 8, np.arange(LANES) % 8
    row_coef, row_k = np.arange(LANES) // sectors, np.arange(LANES) % sectors
    out[ROW_HARTLEY : ROW_HARTLEY + 16] = hartley[:, lane_sector]
    out[ROW_MIRROR : ROW_MIRROR + 16] = hartley[(-k) % sectors][:, lane_sector]
    out[ROW_SPREAD : ROW_SPREAD + 16] = k[:, None] == lane_sector[None, :]
    same = row_coef[:, None] == lane_coef[None, :]
    reaction = hartley - np.roll(hartley, -1, 1)
    out[ROW_LOAD : ROW_LOAD + 128] = same * reaction[row_k][:, lane_sector]
    out[ROW_SAME : ROW_SAME + 128] = same
    out[ROW_COEF : ROW_COEF + 128, 0:8] = row_coef[:, None] == np.arange(8)[None, :]
    out[ROW_PICK : ROW_PICK + 128, 0:16] = row_k[:, None] == k[None, :]
    out[ROW_SQUARE : ROW_SQUARE + 16, 0:16] = hartley
    c, t = np.arange(coefs), np.arange(samples)
    angle = 2.0 * np.pi * (np.outer(c // 2 + 1, t) % samples) / samples
    basis = np.where(c[:, None] % 2 == 0, np.cos(angle), np.sin(angle))
    for h in range(2):
        ordered = np.roll(basis, -h * (coefs // 2), 0)
        out[ROW_LOADS + 64 * h : ROW_LOADS + 64 * (h + 1)] = ordered * (2.0 / samples)
        out[ROW_GAPS + 128 * h : ROW_GAPS + 128 * (h + 1), 0:64] = ordered.T
    return out.astype(np.float32)


def product(a, b, precision=lax.Precision.HIGH):
    return jnp.dot(a, b, preferred_element_type=jnp.float32, precision=precision)


SEND_ORDER = ((2, 0, 3, 1), (0, 1, 2, 3), (3, 2, 1, 0), (1, 3, 0, 2))
PAIR_ORDER = (
    (0, 1, 2, 6, 7, 3, 4, 5),
    (2, 6, 3, 4, 5, 7, 0, 1),
    (4, 0, 1, 2, 3, 5, 6, 7),
    (6, 4, 5, 7, 0, 1, 2, 3),
)


def seen(z, k, step):
    order = PAIR_ORDER[z]
    return int((order[k] + step) % 8 not in order[:k])


def kernel(
    disp_hbm,
    direction_hbm,
    states_hbm,
    params_hbm,
    mistuning_hbm,
    groups_hbm,
    diag_hbm,
    cross_hbm,
    table_hbm,
    residual,
    jvp,
    disp,
    direction,
    states,
    params,
    mistuning,
    groups,
    diag,
    cross,
    table,
    fetched,
    fetched_parts,
    x_out,
    s_out,
    x_in,
    s_in,
    r_out,
    r_in,
    l_out,
    l_in,
    params8,
    tractions,
    linear,
    x_sent,
    x_got,
    s_sent,
    s_got,
    r_sent,
    r_got,
    l_sent,
    l_got,
):
    sectors = 16
    pairs = sectors // 2
    me = lax.axis_index("sector")
    h = lax.axis_index("harm")
    g0 = me // 2
    z0 = me // 4
    partner = (me, 1 - h)
    side = lax.rem(h + lax.rem(g0, 2), 2)

    def by_z(values):
        out = jnp.int32(values[3])
        for z in (2, 1, 0):
            out = jnp.where(z0 == z, values[z], out)
        return out

    def at_step(column, j):
        out = column[-1]
        for k in range(len(column) - 2, -1, -1):
            out = jnp.where(j == k, column[k], out)
        return out

    send_order = [by_z([SEND_ORDER[z][k] for z in range(4)]) for k in range(4)]
    pair_order = [by_z([PAIR_ORDER[z][k] for z in range(4)]) for k in range(8)]
    new_first = [by_z([seen(z, k, -1) for z in range(4)]) for k in range(8)]
    new_last = [by_z([seen(z, k, 1) for z in range(4)]) for k in range(8)]

    def part(i, z):
        lanes = pl.ds(pl.multiple_of(z * 2 * LANES, 2 * LANES), 2 * LANES)
        source, target = ((disp_hbm, disp), (direction_hbm, direction), (states_hbm, states))[i]
        return pltpu.make_async_copy(
            source.at[:, lanes], target.at[:, lanes], fetched_parts.at[i, z]
        )

    given = (params_hbm, mistuning_hbm, groups_hbm, diag_hbm, cross_hbm, table_hbm)
    held = (params, mistuning, groups, diag, cross, table)
    fetches = [
        pltpu.make_async_copy(source, target, fetched.at[i])
        for i, (source, target) in enumerate(zip(given, held))
    ]
    for k in range(4):
        for i in range(3):
            part(i, send_order[k]).start()
        if k == 0:
            fetches[0].start()
    for fetch in fetches[1:]:
        fetch.start()

    barrier = pltpu.get_barrier_semaphore()

    def greet(i, carry):
        pl.semaphore_signal(
            barrier, inc=1, device_id=(lax.rem(me + i, sectors), h), device_id_type=MESH
        )
        return carry

    lax.fori_loop(1, sectors, greet, 0)
    pl.semaphore_signal(barrier, inc=1, device_id=partner, device_id_type=MESH)

    def low(rows):
        return lax.broadcasted_iota(jnp.int32, (rows, LANES), 1) < HALF

    def pack(g):
        lanes = pl.ds(pl.multiple_of(g * LANES, LANES), LANES)
        a, b = disp[:, lanes], direction[:, lanes]
        x_out[2 * g] = jnp.where(low(96), a, pltpu.roll(b, HALF, 1))
        x_out[2 * g + 1] = jnp.where(low(96), pltpu.roll(a, HALF, 1), b)
        z = states[:, lanes].astype(jnp.float32)
        early, late = z[0:64], z[64:128]
        s_out[2 * g, 8:72, :] = jnp.where(low(64), early, pltpu.roll(late, HALF, 1))
        s_out[2 * g + 1, 8:72, :] = jnp.where(low(64), pltpu.roll(early, HALF, 1), late)
        p = params8[:, lanes]
        turned = pltpu.roll(p, HALF, 1)
        s_out[2 * g, 0:8, :] = jnp.where(low(8), p, turned)
        s_out[2 * g + 1, 0:8, :] = jnp.where(low(8), turned, p)

    def x_copy(to, source):
        return pltpu.make_async_remote_copy(
            src_ref=x_out.at[to],
            dst_ref=x_in.at[source],
            send_sem=x_sent.at[to],
            recv_sem=x_got.at[source],
            device_id=(to, h),
            device_id_type=MESH,
        )

    def s_copy(to, source):
        return pltpu.make_async_remote_copy(
            src_ref=s_out.at[to],
            dst_ref=s_in.at[source // 2],
            send_sem=s_sent.at[to],
            recv_sem=s_got.at[source // 2],
            device_id=(to, h),
            device_id_type=MESH,
        )

    core, x = lax.rem(me, 2), lax.rem(g0, 2)
    mine_here = core == side

    def states_for(to):
        return core == lax.rem(h + lax.rem(to // 2, 2), 2)

    def send(k, carry):
        z = at_step(send_order, k)
        for i in range(3):
            part(i, z).wait()

        @pl.when(k == 0)
        def _():
            fetches[0].wait()
            params8[0:4, :] = params[...]
            params8[4:8, :] = params[...]

        pack(2 * z)
        pack(2 * z + 1)

        @pl.when(k == 0)
        def _():
            pl.semaphore_wait(barrier, sectors)

        @pl.when(z == z0)
        def _():
            x_in[me] = x_out[me]

            @pl.when(mine_here)
            def _():
                s_in[g0] = s_out[me]

        for q in range(4):
            to = 4 * z + 2 * lax.rem(q + core, 2) + lax.rem(q // 2 + x, 2)

            @pl.when(to != me)
            def _():
                x_copy(to, me).start()

                @pl.when(states_for(to))
                def _():
                    s_copy(to, me).start()

        return carry

    lax.fori_loop(0, 4, send, 0)
    for fetch in fetches[1:]:
        fetch.wait()

    square = table[ROW_SQUARE : ROW_SQUARE + 16, 0:16]
    row = lax.broadcasted_iota(jnp.int32, (16, 16), 0)
    col = lax.broadcasted_iota(jnp.int32, (16, 16), 1)
    group_row = jnp.broadcast_to(groups[...].astype(jnp.float32), (16, 16))
    group_col = jnp.sum(jnp.where(row == col, group_row, 0.0), axis=1, keepdims=True)
    together = (group_row == group_col).astype(jnp.float32)
    mean = together / jnp.sum(together, axis=0, keepdims=True)
    weighted = square * mistuning[...]
    exact = lax.Precision.HIGHEST
    tuned = weighted - product(weighted, mean, exact)
    tuned = product(tuned, table[ROW_SPREAD : ROW_SPREAD + 16, :], exact)
    pick = table[ROW_PICK : ROW_PICK + 128, 0:16]
    same = table[ROW_SAME : ROW_SAME + 128, :]
    plain = product(pick, table[ROW_HARTLEY : ROW_HARTLEY + 16, :], exact)
    turned_back = product(pick, table[ROW_MIRROR : ROW_MIRROR + 16, :], exact)
    tuned = product(pick, tuned, exact)
    diag_rows = product(pick, diag[...], exact)
    cross_rows = product(pick, cross[...], exact)
    coef_here = lax.broadcasted_iota(jnp.int32, (128, 32), 0) // 16
    coef_lane = lax.broadcasted_iota(jnp.int32, (128, 32), 1)
    for b in range(4):
        chosen = coef_lane == coef_here + 8 * b
        d = jnp.sum(jnp.where(chosen, diag_rows, 0.0), axis=1, keepdims=True)
        c = jnp.sum(jnp.where(chosen, cross_rows, 0.0), axis=1, keepdims=True)
        linear[b] = same * (d * plain + c * turned_back + tuned)

    def r_copy(j):
        return pltpu.make_async_remote_copy(
            src_ref=r_out.at[j],
            dst_ref=r_in.at[j],
            send_sem=r_sent.at[j],
            recv_sem=r_got.at[j],
            device_id=partner,
            device_id_type=MESH,
        )

    def l_copy(j, sector):
        return pltpu.make_async_remote_copy(
            src_ref=l_out.at[j],
            dst_ref=l_in.at[sector],
            send_sem=l_sent.at[j],
            recv_sem=l_got.at[sector // 2],
            device_id=partner,
            device_id_type=MESH,
        )

    def arrive(sector):
        @pl.when(sector != me)
        def _():
            x_copy(me, sector).wait_recv()

    def pair(j):
        return at_step(pair_order, j)

    def hand_over(j):
        g = pair(j)
        arrive(2 * g + 1)

        @pl.when(at_step(new_first, j) == 1)
        def _():
            arrive(2 * g)

        @pl.when(at_step(new_last, j) == 1)
        def _():
            arrive(lax.rem(2 * g + 2, sectors))

        other = 2 * g + 1 - side
        r_out[j] = x_in[other] - x_in[lax.rem(other + 1, sectors)]
        r_copy(j).start()

    def contact(j):
        g = pair(j)
        sector = 2 * g + side
        own = x_in[sector] - x_in[lax.rem(sector + 1, sectors)]

        @pl.when(sector != me)
        def _():
            s_copy(me, sector).wait_recv()

        r_copy(j).wait_recv()
        far = r_in[j]
        rows = [jnp.concatenate([own[32 * i : 32 * i + 32], far[32 * i : 32 * i + 32]], 0) for i in range(3)]
        gaps_rows = pl.ds(pl.multiple_of(ROW_GAPS + 128 * h, 8), 128)
        moved = product(table[gaps_rows, 0:64], jnp.concatenate(rows, 1))
        law = s_in[g, 0:8, :]
        n0, kn, kt, mu = law[0:1], law[1:2], law[2:3], law[3:4]
        step = 32
        for start in range(0, 128, step):
            packed = s_in[g, 8 + start % 64 : 8 + start % 64 + step, :]
            turned = pltpu.roll(packed, HALF, 1)
            left = low(step)
            z = jnp.where(left, packed, turned) if start < 64 else jnp.where(left, turned, packed)
            raw = [moved[start : start + step, LANES * i : LANES * (i + 1)] for i in range(3)]
            swapped = [pltpu.roll(value, HALF, 1) for value in raw]
            gap = [jnp.where(left, u, v) for u, v in zip(raw, swapped)]
            dgap = [jnp.where(left, v, u) for u, v in zip(raw, swapped)]
            touching = (z < 1.5).astype(jnp.float32)
            sliding = jnp.logical_and(z > 0.5, z < 1.5)
            normal = (n0 + kn * gap[0]) * touching
            dnormal = kn * dgap[0] * touching
            inverse = lax.rsqrt(gap[1] * gap[1] + gap[2] * gap[2] + 1.0)
            along = (gap[1] * dgap[1] + gap[2] * dgap[2]) * (inverse * inverse)
            tractions[start : start + step, 0:LANES] = jnp.where(left, normal, dnormal)
            rub = mu * inverse
            for i in (1, 2):
                slipped = normal * gap[i]
                dslipped = dnormal * gap[i] + normal * (dgap[i] - gap[i] * along)
                stuck = kt * raw[i] * touching
                tractions[start : start + step, LANES * i : LANES * (i + 1)] = jnp.where(
                    sliding, rub * jnp.where(left, slipped, dslipped), stuck
                )
        loads_rows = pl.ds(pl.multiple_of(ROW_LOADS + 64 * h, 8), 64)
        loads = product(table[loads_rows, :], tractions[...])
        for i in range(3):
            l_out[j, 32 * i : 32 * i + 32, :] = loads[32:64, LANES * i : LANES * (i + 1)]
        l_copy(j, sector).start()
        for i in range(3):
            l_in[sector, 32 * i : 32 * i + 32, :] = loads[0:32, LANES * i : LANES * (i + 1)]

    hand_over(jnp.int32(0))

    def turn(j, carry):
        @pl.when(j < pairs - 1)
        def _():
            hand_over(j + 1)

        contact(j)
        return carry

    lax.fori_loop(0, pairs, turn, 0)

    def loads_here(j, carry):
        l_copy(j, 2 * pair(j) + 1 - side).wait_recv()
        return carry

    lax.fori_loop(0, pairs, loads_here, 0)
    reaction = table[ROW_LOAD : ROW_LOAD + 128, :]
    for b in range(4):
        matrix = jnp.concatenate([linear[b], reaction], 1)
        columns = []
        for i in range(3):
            at = slice(32 * i + 8 * b, 32 * i + 8 * b + 8)
            field = [x_in[:, at, :].reshape(128, LANES), l_in[:, at, :].reshape(128, LANES)]
            columns.append(jnp.concatenate(field, 0))
        out = product(matrix, jnp.concatenate(columns, 1))
        for i in range(3):
            both = out[:, LANES * i : LANES * (i + 1)]
            residual[i, 8 * b : 8 * b + 8] = both.reshape(8, 16, LANES)
            jvp[i, 8 * b : 8 * b + 8] = pltpu.roll(both, HALF, 1).reshape(8, 16, LANES)

    def sent(i, carry):
        to = lax.rem(me + i, sectors)
        x_copy(to, me).wait_send()

        @pl.when(states_for(to))
        def _():
            s_copy(to, me).wait_send()

        return carry

    lax.fori_loop(1, sectors, sent, 0)

    def sent_back(j, carry):
        r_copy(j).wait_send()
        l_copy(j, 2 * pair(j) + side).wait_send()
        return carry

    lax.fori_loop(0, pairs, sent_back, 0)


def body_in_kernel(
    disp,
    direction,
    stick_state,
    contact_params,
    mistuning,
    group_ids,
    diag_stiff,
    cross_stiff,
    excitation,
):
    hbm = pl.BlockSpec(memory_space=pltpu.HBM)
    dma = pltpu.SemaphoreType.DMA
    f32 = jnp.float32
    table = constant_table(16, 64, 128)
    vmem = pl.BlockSpec(memory_space=pltpu.VMEM)
    out = jax.ShapeDtypeStruct((3, 32, 16, LANES), f32)
    residual, jvp = pl.pallas_call(
        kernel,
        out_shape=(out, out),
        in_specs=[hbm] * 9,
        out_specs=(vmem, vmem),
        scratch_shapes=[
            pltpu.VMEM((96, 1024), f32),
            pltpu.VMEM((96, 1024), f32),
            pltpu.VMEM((128, 1024), jnp.int32),
            pltpu.VMEM((4, 1024), f32),
            pltpu.VMEM((1, 16), f32),
            pltpu.VMEM((1, 16), jnp.int32),
            pltpu.VMEM((16, 32), f32),
            pltpu.VMEM((16, 32), f32),
            pltpu.VMEM((ROWS, LANES), f32),
            dma((6,)),
            dma((3, 4)),
            pltpu.VMEM((16, 96, LANES), f32),
            pltpu.VMEM((16, 72, LANES), f32),
            pltpu.VMEM((16, 96, LANES), f32),
            pltpu.VMEM((8, 72, LANES), f32),
            pltpu.VMEM((8, 96, LANES), f32),
            pltpu.VMEM((8, 96, LANES), f32),
            pltpu.VMEM((8, 96, LANES), f32),
            pltpu.VMEM((16, 96, LANES), f32),
            pltpu.VMEM((8, 1024), f32),
            pltpu.VMEM((128, 3 * LANES), f32),
            pltpu.VMEM((4, 128, LANES), f32),
            dma((16,)),
            dma((16,)),
            dma((16,)),
            dma((8,)),
            dma((8,)),
            dma((8,)),
            dma((8,)),
            dma((8,)),
        ],
        compiler_params=pltpu.CompilerParams(
            collective_id=0, has_side_effects=True, vmem_limit_bytes=VMEM_KERNEL
        ),
    )(
        disp.reshape(96, 1024),
        direction.reshape(96, 1024),
        stick_state[0],
        contact_params[0],
        mistuning[None],
        group_ids[None],
        diag_stiff.T,
        cross_stiff.T,
        jnp.asarray(table),
    )
    residual = residual[..., :HALF] - jnp.swapaxes(excitation, 2, 3)
    return (jnp.swapaxes(residual, 2, 3), jnp.swapaxes(jvp[..., :HALF], 2, 3))


def solution(mesh):
    in_specs = (
        P("sector", None, "harm", None),
        P("sector", None, "harm", None),
        P("sector", None, None),
        P("sector", None, None),
        P(),
        P(),
        P("harm", None),
        P("harm", None),
        P(None, "harm", "sector", None),
    )
    out_specs = (P(None, "harm", "sector", None), P(None, "harm", "sector", None))

    def body(*arrays):
        _, channels, coefs, nodes = arrays[0].shape
        sizes = (mesh.shape["sector"], mesh.shape["harm"], channels, coefs, nodes, arrays[2].shape[1])
        if sizes == (16, 2, 3, 32, 1024, 128):
            return body_in_kernel(*arrays)
        return body_any_size(*arrays)

    return jax.shard_map(body, mesh=mesh, in_specs=in_specs, out_specs=out_specs, check_vma=False)
```

```python
import math

import jax
import jax.numpy as jnp
import numpy as np
from jax import lax
from jax.experimental import pallas as pl
from jax.experimental.pallas import tpu as pltpu
from jax.sharding import PartitionSpec as P

MESH = pl.DeviceIdType.MESH

exact_mode = lax.Precision.HIGHEST


def passed_along(value, axis, steps):
    count = lax.axis_size(axis)
    pairs = [(source, (source + steps) % count) for source in range(count)]
    return lax.ppermute(value, axis, pairs)


def from_behind(block, axis, distance):
    devices = range(lax.axis_size(axis))
    route = [(i - distance, i) for i in devices if i - distance in devices]
    return lax.ppermute(block, axis, route)


def basis_table(coefs, samples):
    coef_index = lax.broadcasted_iota(jnp.int32, (coefs, samples), 0)
    time_index = lax.broadcasted_iota(jnp.int32, (coefs, samples), 1)
    harmonic = coef_index // 2 + 1
    phase = harmonic * time_index % samples
    angle = phase.astype(jnp.float32) * (2.0 * math.pi / samples)
    return jnp.where(coef_index % 2 == 0, jnp.cos(angle), jnp.sin(angle))


def hartley_table(count):
    row_index = lax.broadcasted_iota(jnp.int32, (count, count), 0)
    col_index = lax.broadcasted_iota(jnp.int32, (count, count), 1)
    phase = row_index * col_index % count
    angle = phase.astype(jnp.float32) * (2.0 * math.pi / count)
    return (jnp.cos(angle) + jnp.sin(angle)) / math.sqrt(count)


def contact_law(gaps, dgaps, states_here, params):
    preload = params[0]
    normal_stiff = params[1]
    tangent_stiff = params[2]
    friction_coef = params[3]
    touching = (states_here != 2).astype(jnp.float32)
    sliding = states_here == 1
    normal = (preload + normal_stiff * gaps[0]) * touching
    dnormal = normal_stiff * dgaps[0] * touching
    radius = jnp.sqrt(gaps[1] * gaps[1] + gaps[2] * gaps[2] + 1.0)
    projected = (gaps[1] * dgaps[1] + gaps[2] * dgaps[2]) / (radius * radius * radius)
    tractions = [normal]
    dtractions = [dnormal]
    for channel in (1, 2):
        stuck = tangent_stiff * gaps[channel]
        dstuck = tangent_stiff * dgaps[channel]
        slipped = friction_coef * normal * gaps[channel] / radius
        dslipped = friction_coef * (
            dnormal * gaps[channel] / radius
            + normal * (dgaps[channel] / radius - gaps[channel] * projected)
        )
        tractions.append(jnp.where(sliding, slipped, stuck) * touching)
        dtractions.append(jnp.where(sliding, dslipped, dstuck) * touching)
    return (jnp.stack(tractions), jnp.stack(dtractions))


def mirror(field):
    return jnp.roll(jnp.flip(field, -1), 1, -1)


def group_flag(group_ids, own_group, other_index, sectors):
    inside = jnp.logical_and(other_index >= 0, other_index < sectors)
    safe_index = jnp.clip(other_index, 0, sectors - 1)
    other_group = lax.dynamic_slice_in_dim(group_ids, safe_index, 1)
    return jnp.logical_and(inside, other_group == own_group).astype(jnp.float32)[0]


def body_any_size(
    disp,
    direction,
    stick_state,
    contact_params,
    mistuning,
    group_ids,
    diag_stiff,
    cross_stiff,
    excitation,
):
    sectors = lax.axis_size("sector")
    sector_index = lax.axis_index("sector")
    harm_index = lax.axis_index("harm")
    local_coefs = disp.shape[2]
    samples = stick_state.shape[1]
    coefs = local_coefs * lax.axis_size("harm")
    table = basis_table(coefs, samples)
    own_table = lax.dynamic_slice_in_dim(table, harm_index * local_coefs, local_coefs, 0)
    scale = 2.0 / samples
    hartley = hartley_table(sectors)
    paired = jnp.concatenate([disp, direction], 0)
    paired_next = passed_along(paired, "sector", -1)
    relative = paired - paired_next
    gathered = lax.all_gather(relative, "harm", axis=2, tiled=True)
    params_here = contact_params[0]
    gaps = jnp.einsum("wcjp,jt->wctp", gathered, table, precision=exact_mode)
    traction, dtraction = contact_law(gaps[0], gaps[1], stick_state[0], params_here)
    loads = (
        jnp.einsum(
            "wctp,jt->wcjp", jnp.stack([traction, dtraction]), own_table, precision=exact_mode
        )
        * scale
    )
    earlier_loads = passed_along(loads, "sector", 1)
    own_group = lax.dynamic_slice_in_dim(group_ids, sector_index, 1)
    members = jnp.sum((group_ids == own_group[0]).astype(jnp.float32))
    totals = paired
    for offset in range(1, 8):
        from_before = from_behind(paired, "sector", offset)
        from_after = from_behind(paired, "sector", -offset)
        flag_before = group_flag(group_ids, own_group, sector_index - offset, sectors)
        flag_after = group_flag(group_ids, own_group, sector_index + offset, sectors)
        totals = totals + flag_before * from_before + flag_after * from_after
    weight = lax.dynamic_slice_in_dim(mistuning, sector_index, 1)[0]
    forces = loads - earlier_loads + weight * (paired - totals / members)
    outgoing = jnp.concatenate([paired, forces], 0)
    received = lax.all_to_all(outgoing[:, None], "sector", split_axis=4, concat_axis=1, tiled=True)
    states_nd = jnp.einsum("ks,wscjp->wcjpk", hartley, received[0:2], precision=exact_mode)
    forces_nd = jnp.einsum("ks,wscjp->wcjpk", hartley, received[2:4], precision=exact_mode)
    stiff_diag = diag_stiff[None, :, None, :]
    stiff_cross = cross_stiff[None, :, None, :]
    residual = (
        stiff_diag * states_nd[0] + stiff_cross * mirror(states_nd[0]) + forces_nd[0] - excitation
    )
    jvp = stiff_diag * states_nd[1] + stiff_cross * mirror(states_nd[1]) + forces_nd[1]
    return (residual, jvp)


LANES = 128
VMEM_KERNEL = 63 * 1024 * 1024
HALF = 64
ROW_HARTLEY = 0
ROW_MIRROR = 16
ROW_SPREAD = 32
ROW_LOAD = 48
ROW_SAME = 176
ROW_COEF = 304
ROW_PICK = 432
ROW_SQUARE = 560
ROW_LOADS = 576
ROW_GAPS = 704
ROWS = 960


def constant_table(sectors, coefs, samples):
    k = np.arange(sectors)
    phase = 2.0 * np.pi * (np.outer(k, k) % sectors) / sectors
    hartley = (np.cos(phase) + np.sin(phase)) / math.sqrt(sectors)
    out = np.zeros((ROWS, LANES), np.float64)
    lane_sector, lane_coef = np.arange(LANES) // 8, np.arange(LANES) % 8
    row_coef, row_k = np.arange(LANES) // sectors, np.arange(LANES) % sectors
    out[ROW_HARTLEY : ROW_HARTLEY + 16] = hartley[:, lane_sector]
    out[ROW_MIRROR : ROW_MIRROR + 16] = hartley[(-k) % sectors][:, lane_sector]
    out[ROW_SPREAD : ROW_SPREAD + 16] = k[:, None] == lane_sector[None, :]
    same = row_coef[:, None] == lane_coef[None, :]
    reaction = hartley - np.roll(hartley, -1, 1)
    out[ROW_LOAD : ROW_LOAD + 128] = same * reaction[row_k][:, lane_sector]
    out[ROW_SAME : ROW_SAME + 128] = same
    out[ROW_COEF : ROW_COEF + 128, 0:8] = row_coef[:, None] == np.arange(8)[None, :]
    out[ROW_PICK : ROW_PICK + 128, 0:16] = row_k[:, None] == k[None, :]
    out[ROW_SQUARE : ROW_SQUARE + 16, 0:16] = hartley
    c, t = np.arange(coefs), np.arange(samples)
    angle = 2.0 * np.pi * (np.outer(c // 2 + 1, t) % samples) / samples
    basis = np.where(c[:, None] % 2 == 0, np.cos(angle), np.sin(angle))
    for h in range(2):
        ordered = np.roll(basis, -h * (coefs // 2), 0)
        out[ROW_LOADS + 64 * h : ROW_LOADS + 64 * (h + 1)] = ordered * (2.0 / samples)
        out[ROW_GAPS + 128 * h : ROW_GAPS + 128 * (h + 1), 0:64] = ordered.T
    return out.astype(np.float32)


def product(a, b, precision=lax.Precision.HIGH):
    return jnp.dot(a, b, preferred_element_type=jnp.float32, precision=precision)


SEND_ORDER = ((2, 0, 3, 1), (0, 1, 2, 3), (3, 2, 1, 0), (1, 3, 0, 2))
PAIR_ORDER = (
    (0, 1, 2, 6, 7, 3, 4, 5),
    (2, 6, 3, 4, 5, 7, 0, 1),
    (4, 0, 5, 6, 7, 1, 2, 3),
    (6, 4, 5, 7, 0, 1, 2, 3),
)


LATE = ((0, 2, 4), (0, 1, 4), (0, 1, 4), (0, 2, 4))


def seen(z, k, step):
    order = PAIR_ORDER[z]
    return int((order[k] + step) % 8 not in order[:k])


def kernel(
    disp_hbm,
    direction_hbm,
    states_hbm,
    params_hbm,
    mistuning_hbm,
    groups_hbm,
    diag_hbm,
    cross_hbm,
    table_hbm,
    residual,
    jvp,
    disp,
    direction,
    states,
    params,
    mistuning,
    groups,
    diag,
    cross,
    table,
    fetched,
    fetched_parts,
    x_out,
    s_out,
    x_in,
    s_in,
    r_out,
    r_in,
    l_out,
    l_in,
    params8,
    tractions,
    linear,
    moved_on,
    x_sent,
    x_got,
    s_sent,
    s_got,
    r_sent,
    r_got,
    l_sent,
    l_got,
):
    sectors = 16
    pairs = sectors // 2
    me = lax.axis_index("sector")
    h = lax.axis_index("harm")
    g0 = me // 2
    z0 = me // 4
    partner = (me, 1 - h)
    side = lax.rem(h + lax.rem(g0, 2), 2)

    def by_z(values):
        out = jnp.int32(values[3])
        for z in (2, 1, 0):
            out = jnp.where(z0 == z, values[z], out)
        return out

    def at_step(column, j):
        out = column[-1]
        for k in range(len(column) - 2, -1, -1):
            out = jnp.where(j == k, column[k], out)
        return out

    send_order = [by_z([SEND_ORDER[z][k] for z in range(4)]) for k in range(4)]
    pair_order = [by_z([PAIR_ORDER[z][k] for z in range(4)]) for k in range(8)]
    late = [by_z([int(k in LATE[z]) for z in range(4)]) for k in range(8)]
    new_first = [by_z([seen(z, k, -1) for z in range(4)]) for k in range(8)]
    new_last = [by_z([seen(z, k, 1) for z in range(4)]) for k in range(8)]

    def part(i, z):
        lanes = pl.ds(pl.multiple_of(z * 2 * LANES, 2 * LANES), 2 * LANES)
        source, target = ((disp_hbm, disp), (direction_hbm, direction), (states_hbm, states))[i]
        return pltpu.make_async_copy(
            source.at[:, lanes], target.at[:, lanes], fetched_parts.at[i, z]
        )

    given = (params_hbm, mistuning_hbm, groups_hbm, diag_hbm, cross_hbm, table_hbm)
    held = (params, mistuning, groups, diag, cross, table)
    fetches = [
        pltpu.make_async_copy(source, target, fetched.at[i])
        for i, (source, target) in enumerate(zip(given, held))
    ]
    for k in range(4):
        for i in range(3):
            part(i, send_order[k]).start()
        if k == 0:
            fetches[0].start()
    for fetch in fetches[1:]:
        fetch.start()

    barrier = pltpu.get_barrier_semaphore()

    def greet(i, carry):
        pl.semaphore_signal(
            barrier, inc=1, device_id=(lax.rem(me + i, sectors), h), device_id_type=MESH
        )
        return carry

    lax.fori_loop(1, sectors, greet, 0)
    pl.semaphore_signal(barrier, inc=1, device_id=partner, device_id_type=MESH)

    def low(rows):
        return lax.broadcasted_iota(jnp.int32, (rows, LANES), 1) < HALF

    def pack(g):
        lanes = pl.ds(pl.multiple_of(g * LANES, LANES), LANES)
        a, b = disp[:, lanes], direction[:, lanes]
        x_out[2 * g] = jnp.where(low(96), a, pltpu.roll(b, HALF, 1))
        x_out[2 * g + 1] = jnp.where(low(96), pltpu.roll(a, HALF, 1), b)
        z = states[:, lanes].astype(jnp.float32)
        early, late = z[0:64], z[64:128]
        s_out[2 * g, 8:72, :] = jnp.where(low(64), early, pltpu.roll(late, HALF, 1))
        s_out[2 * g + 1, 8:72, :] = jnp.where(low(64), pltpu.roll(early, HALF, 1), late)
        p = params8[:, lanes]
        turned = pltpu.roll(p, HALF, 1)
        s_out[2 * g, 0:8, :] = jnp.where(low(8), p, turned)
        s_out[2 * g + 1, 0:8, :] = jnp.where(low(8), turned, p)

    def x_copy(to, source):
        return pltpu.make_async_remote_copy(
            src_ref=x_out.at[to],
            dst_ref=x_in.at[source],
            send_sem=x_sent.at[to],
            recv_sem=x_got.at[source],
            device_id=(to, h),
            device_id_type=MESH,
        )

    def s_copy(to, source):
        return pltpu.make_async_remote_copy(
            src_ref=s_out.at[to],
            dst_ref=s_in.at[source // 2],
            send_sem=s_sent.at[to],
            recv_sem=s_got.at[source // 2],
            device_id=(to, h),
            device_id_type=MESH,
        )

    core, x = lax.rem(me, 2), lax.rem(g0, 2)
    mine_here = core == side

    def states_for(to):
        return core == lax.rem(h + lax.rem(to // 2, 2), 2)

    def send(k, carry):
        z = at_step(send_order, k)
        for i in range(3):
            part(i, z).wait()

        @pl.when(k == 0)
        def _():
            fetches[0].wait()
            params8[0:4, :] = params[...]
            params8[4:8, :] = params[...]

        pack(2 * z)
        pack(2 * z + 1)

        @pl.when(k == 0)
        def _():
            pl.semaphore_wait(barrier, sectors)

        @pl.when(z == z0)
        def _():
            x_in[me] = x_out[me]

            @pl.when(mine_here)
            def _():
                s_in[g0] = s_out[me]

        tos = [4 * z + 2 * lax.rem(q + core, 2) + lax.rem(q // 2 + x, 2) for q in range(4)]
        for to in tos:

            @pl.when(to != me)
            def _(to=to):
                x_copy(to, me).start()

        for to in tos:

            @pl.when(jnp.logical_and(to != me, states_for(to)))
            def _(to=to):
                s_copy(to, me).start()

        return carry

    lax.fori_loop(0, 4, send, 0)
    for fetch in fetches[1:]:
        fetch.wait()

    square = table[ROW_SQUARE : ROW_SQUARE + 16, 0:16]
    row = lax.broadcasted_iota(jnp.int32, (16, 16), 0)
    col = lax.broadcasted_iota(jnp.int32, (16, 16), 1)
    group_row = jnp.broadcast_to(groups[...].astype(jnp.float32), (16, 16))
    group_col = jnp.sum(jnp.where(row == col, group_row, 0.0), axis=1, keepdims=True)
    together = (group_row == group_col).astype(jnp.float32)
    mean = together / jnp.sum(together, axis=0, keepdims=True)
    weighted = square * mistuning[...]
    exact = lax.Precision.HIGHEST
    tuned = weighted - product(weighted, mean, exact)
    tuned = product(tuned, table[ROW_SPREAD : ROW_SPREAD + 16, :], exact)
    pick = table[ROW_PICK : ROW_PICK + 128, 0:16]
    same = table[ROW_SAME : ROW_SAME + 128, :]
    plain = product(pick, table[ROW_HARTLEY : ROW_HARTLEY + 16, :], exact)
    turned_back = product(pick, table[ROW_MIRROR : ROW_MIRROR + 16, :], exact)
    tuned = product(pick, tuned, exact)
    diag_rows = product(pick, diag[...], exact)
    cross_rows = product(pick, cross[...], exact)
    coef_here = lax.broadcasted_iota(jnp.int32, (128, 32), 0) // 16
    coef_lane = lax.broadcasted_iota(jnp.int32, (128, 32), 1)
    for b in range(4):
        chosen = coef_lane == coef_here + 8 * b
        d = jnp.sum(jnp.where(chosen, diag_rows, 0.0), axis=1, keepdims=True)
        c = jnp.sum(jnp.where(chosen, cross_rows, 0.0), axis=1, keepdims=True)
        linear[b] = same * (d * plain + c * turned_back + tuned)

    def r_copy(j):
        return pltpu.make_async_remote_copy(
            src_ref=r_out.at[j],
            dst_ref=r_in.at[j],
            send_sem=r_sent.at[j],
            recv_sem=r_got.at[j],
            device_id=partner,
            device_id_type=MESH,
        )

    def l_copy(j, sector):
        return pltpu.make_async_remote_copy(
            src_ref=l_out.at[j],
            dst_ref=l_in.at[sector],
            send_sem=l_sent.at[j],
            recv_sem=l_got.at[sector // 2],
            device_id=partner,
            device_id_type=MESH,
        )

    def arrive(sector):
        @pl.when(sector != me)
        def _():
            x_copy(me, sector).wait_recv()

    def pair(j):
        return at_step(pair_order, j)

    def hand_over(j):
        g = pair(j)
        arrive(2 * g + 1)

        @pl.when(at_step(new_first, j) == 1)
        def _():
            arrive(2 * g)

        @pl.when(at_step(new_last, j) == 1)
        def _():
            arrive(lax.rem(2 * g + 2, sectors))

        other = 2 * g + 1 - side
        r_out[j] = x_in[other] - x_in[lax.rem(other + 1, sectors)]
        r_copy(j).start()

    def contact(j):
        g = pair(j)
        sector = 2 * g + side
        own = x_in[sector] - x_in[lax.rem(sector + 1, sectors)]

        @pl.when(sector != me)
        def _():
            s_copy(me, sector).wait_recv()

        r_copy(j).wait_recv()
        far = r_in[j]
        rows = [jnp.concatenate([own[32 * i : 32 * i + 32], far[32 * i : 32 * i + 32]], 0) for i in range(3)]
        gaps_rows = pl.ds(pl.multiple_of(ROW_GAPS + 128 * h, 8), 128)
        moved = product(table[gaps_rows, 0:64], jnp.concatenate(rows, 1))
        law = s_in[g, 0:8, :]
        n0, kn, kt, mu = law[0:1], law[1:2], law[2:3], law[3:4]
        step = 32
        for start in range(0, 128, step):
            packed = s_in[g, 8 + start % 64 : 8 + start % 64 + step, :]
            turned = pltpu.roll(packed, HALF, 1)
            left = low(step)
            z = jnp.where(left, packed, turned) if start < 64 else jnp.where(left, turned, packed)
            raw = [moved[start : start + step, LANES * i : LANES * (i + 1)] for i in range(3)]
            swapped = [pltpu.roll(value, HALF, 1) for value in raw]
            gap = [jnp.where(left, u, v) for u, v in zip(raw, swapped)]
            dgap = [jnp.where(left, v, u) for u, v in zip(raw, swapped)]
            touching = (z < 1.5).astype(jnp.float32)
            sliding = jnp.logical_and(z > 0.5, z < 1.5)
            normal = (n0 + kn * gap[0]) * touching
            dnormal = kn * dgap[0] * touching
            inverse = lax.rsqrt(gap[1] * gap[1] + gap[2] * gap[2] + 1.0)
            along = (gap[1] * dgap[1] + gap[2] * dgap[2]) * (inverse * inverse)
            tractions[start : start + step, 0:LANES] = jnp.where(left, normal, dnormal)
            rub = mu * inverse
            for i in (1, 2):
                slipped = normal * gap[i]
                dslipped = dnormal * gap[i] + normal * (dgap[i] - gap[i] * along)
                stuck = kt * raw[i] * touching
                tractions[start : start + step, LANES * i : LANES * (i + 1)] = jnp.where(
                    sliding, rub * jnp.where(left, slipped, dslipped), stuck
                )
        loads_rows = pl.ds(pl.multiple_of(ROW_LOADS + 64 * h, 8), 64)
        loads = product(table[loads_rows, :], tractions[...])
        for i in range(3):
            l_out[j, 32 * i : 32 * i + 32, :] = loads[32:64, LANES * i : LANES * (i + 1)]
        l_copy(j, sector).start()
        for i in range(3):
            l_in[sector, 32 * i : 32 * i + 32, :] = loads[0:32, LANES * i : LANES * (i + 1)]

    hand_over(jnp.int32(0))

    def turn(j, carry):
        waits = at_step(late, j)

        @pl.when(jnp.logical_and(j < pairs - 1, waits == 0))
        def _():
            hand_over(j + 1)

        contact(j)

        @pl.when(jnp.logical_and(j < pairs - 1, waits == 1))
        def _():
            hand_over(j + 1)

        return carry

    lax.fori_loop(0, pairs, turn, 0)

    def columns(fields, b):
        rows = [slice(32 * i + 8 * b, 32 * i + 8 * b + 8) for i in range(3)]
        return jnp.concatenate([fields[:, at, :].reshape(128, LANES) for at in rows], 1)

    for b in range(4):
        moved_on[b] = product(linear[b], columns(x_in, b))

    def loads_here(j, carry):
        l_copy(j, 2 * pair(j) + 1 - side).wait_recv()
        return carry

    lax.fori_loop(0, pairs, loads_here, 0)
    reaction = table[ROW_LOAD : ROW_LOAD + 128, :]
    for b in range(4):
        out = moved_on[b] + product(reaction, columns(l_in, b))
        for i in range(3):
            both = out[:, LANES * i : LANES * (i + 1)]
            residual[i, 8 * b : 8 * b + 8] = both.reshape(8, 16, LANES)
            jvp[i, 8 * b : 8 * b + 8] = pltpu.roll(both, HALF, 1).reshape(8, 16, LANES)

    def sent(i, carry):
        to = lax.rem(me + i, sectors)
        x_copy(to, me).wait_send()

        @pl.when(states_for(to))
        def _():
            s_copy(to, me).wait_send()

        return carry

    lax.fori_loop(1, sectors, sent, 0)

    def sent_back(j, carry):
        r_copy(j).wait_send()
        l_copy(j, 2 * pair(j) + side).wait_send()
        return carry

    lax.fori_loop(0, pairs, sent_back, 0)


def body_in_kernel(
    disp,
    direction,
    stick_state,
    contact_params,
    mistuning,
    group_ids,
    diag_stiff,
    cross_stiff,
    excitation,
):
    hbm = pl.BlockSpec(memory_space=pltpu.HBM)
    dma = pltpu.SemaphoreType.DMA
    f32 = jnp.float32
    table = constant_table(16, 64, 128)
    vmem = pl.BlockSpec(memory_space=pltpu.VMEM)
    out = jax.ShapeDtypeStruct((3, 32, 16, LANES), f32)
    residual, jvp = pl.pallas_call(
        kernel,
        out_shape=(out, out),
        in_specs=[hbm] * 9,
        out_specs=(vmem, vmem),
        scratch_shapes=[
            pltpu.VMEM((96, 1024), f32),
            pltpu.VMEM((96, 1024), f32),
            pltpu.VMEM((128, 1024), jnp.int32),
            pltpu.VMEM((4, 1024), f32),
            pltpu.VMEM((1, 16), f32),
            pltpu.VMEM((1, 16), jnp.int32),
            pltpu.VMEM((16, 32), f32),
            pltpu.VMEM((16, 32), f32),
            pltpu.VMEM((ROWS, LANES), f32),
            dma((6,)),
            dma((3, 4)),
            pltpu.VMEM((16, 96, LANES), f32),
            pltpu.VMEM((16, 72, LANES), f32),
            pltpu.VMEM((16, 96, LANES), f32),
            pltpu.VMEM((8, 72, LANES), f32),
            pltpu.VMEM((8, 96, LANES), f32),
            pltpu.VMEM((8, 96, LANES), f32),
            pltpu.VMEM((8, 96, LANES), f32),
            pltpu.VMEM((16, 96, LANES), f32),
            pltpu.VMEM((8, 1024), f32),
            pltpu.VMEM((128, 3 * LANES), f32),
            pltpu.VMEM((4, 128, LANES), f32),
            pltpu.VMEM((4, 128, 3 * LANES), f32),
            dma((16,)),
            dma((16,)),
            dma((16,)),
            dma((8,)),
            dma((8,)),
            dma((8,)),
            dma((8,)),
            dma((8,)),
        ],
        compiler_params=pltpu.CompilerParams(
            collective_id=0, has_side_effects=True, vmem_limit_bytes=VMEM_KERNEL
        ),
    )(
        disp.reshape(96, 1024),
        direction.reshape(96, 1024),
        stick_state[0],
        contact_params[0],
        mistuning[None],
        group_ids[None],
        diag_stiff.T,
        cross_stiff.T,
        jnp.asarray(table),
    )
    residual = residual[..., :HALF] - jnp.swapaxes(excitation, 2, 3)
    return (jnp.swapaxes(residual, 2, 3), jnp.swapaxes(jvp[..., :HALF], 2, 3))


def solution(mesh):
    in_specs = (
        P("sector", None, "harm", None),
        P("sector", None, "harm", None),
        P("sector", None, None),
        P("sector", None, None),
        P(),
        P(),
        P("harm", None),
        P("harm", None),
        P(None, "harm", "sector", None),
    )
    out_specs = (P(None, "harm", "sector", None), P(None, "harm", "sector", None))

    def body(*arrays):
        _, channels, coefs, nodes = arrays[0].shape
        sizes = (mesh.shape["sector"], mesh.shape["harm"], channels, coefs, nodes, arrays[2].shape[1])
        if sizes == (16, 2, 3, 32, 1024, 128):
            return body_in_kernel(*arrays)
        return body_any_size(*arrays)

    return jax.shard_map(body, mesh=mesh, in_specs=in_specs, out_specs=out_specs, check_vma=False)
```

```python
import math

import jax
import jax.numpy as jnp
import numpy as np
from jax import lax
from jax.experimental import pallas as pl
from jax.experimental.pallas import tpu as pltpu
from jax.sharding import PartitionSpec as P

MESH = pl.DeviceIdType.MESH

exact_mode = lax.Precision.HIGHEST


def passed_along(value, axis, steps):
    count = lax.axis_size(axis)
    pairs = [(source, (source + steps) % count) for source in range(count)]
    return lax.ppermute(value, axis, pairs)


def from_behind(block, axis, distance):
    devices = range(lax.axis_size(axis))
    route = [(i - distance, i) for i in devices if i - distance in devices]
    return lax.ppermute(block, axis, route)


def basis_table(coefs, samples):
    coef_index = lax.broadcasted_iota(jnp.int32, (coefs, samples), 0)
    time_index = lax.broadcasted_iota(jnp.int32, (coefs, samples), 1)
    harmonic = coef_index // 2 + 1
    phase = harmonic * time_index % samples
    angle = phase.astype(jnp.float32) * (2.0 * math.pi / samples)
    return jnp.where(coef_index % 2 == 0, jnp.cos(angle), jnp.sin(angle))


def hartley_table(count):
    row_index = lax.broadcasted_iota(jnp.int32, (count, count), 0)
    col_index = lax.broadcasted_iota(jnp.int32, (count, count), 1)
    phase = row_index * col_index % count
    angle = phase.astype(jnp.float32) * (2.0 * math.pi / count)
    return (jnp.cos(angle) + jnp.sin(angle)) / math.sqrt(count)


def contact_law(gaps, dgaps, states_here, params):
    preload = params[0]
    normal_stiff = params[1]
    tangent_stiff = params[2]
    friction_coef = params[3]
    touching = (states_here != 2).astype(jnp.float32)
    sliding = states_here == 1
    normal = (preload + normal_stiff * gaps[0]) * touching
    dnormal = normal_stiff * dgaps[0] * touching
    radius = jnp.sqrt(gaps[1] * gaps[1] + gaps[2] * gaps[2] + 1.0)
    projected = (gaps[1] * dgaps[1] + gaps[2] * dgaps[2]) / (radius * radius * radius)
    tractions = [normal]
    dtractions = [dnormal]
    for channel in (1, 2):
        stuck = tangent_stiff * gaps[channel]
        dstuck = tangent_stiff * dgaps[channel]
        slipped = friction_coef * normal * gaps[channel] / radius
        dslipped = friction_coef * (
            dnormal * gaps[channel] / radius
            + normal * (dgaps[channel] / radius - gaps[channel] * projected)
        )
        tractions.append(jnp.where(sliding, slipped, stuck) * touching)
        dtractions.append(jnp.where(sliding, dslipped, dstuck) * touching)
    return (jnp.stack(tractions), jnp.stack(dtractions))


def mirror(field):
    return jnp.roll(jnp.flip(field, -1), 1, -1)


def group_flag(group_ids, own_group, other_index, sectors):
    inside = jnp.logical_and(other_index >= 0, other_index < sectors)
    safe_index = jnp.clip(other_index, 0, sectors - 1)
    other_group = lax.dynamic_slice_in_dim(group_ids, safe_index, 1)
    return jnp.logical_and(inside, other_group == own_group).astype(jnp.float32)[0]


def body_any_size(
    disp,
    direction,
    stick_state,
    contact_params,
    mistuning,
    group_ids,
    diag_stiff,
    cross_stiff,
    excitation,
):
    sectors = lax.axis_size("sector")
    sector_index = lax.axis_index("sector")
    harm_index = lax.axis_index("harm")
    local_coefs = disp.shape[2]
    samples = stick_state.shape[1]
    coefs = local_coefs * lax.axis_size("harm")
    table = basis_table(coefs, samples)
    own_table = lax.dynamic_slice_in_dim(table, harm_index * local_coefs, local_coefs, 0)
    scale = 2.0 / samples
    hartley = hartley_table(sectors)
    paired = jnp.concatenate([disp, direction], 0)
    paired_next = passed_along(paired, "sector", -1)
    relative = paired - paired_next
    gathered = lax.all_gather(relative, "harm", axis=2, tiled=True)
    params_here = contact_params[0]
    gaps = jnp.einsum("wcjp,jt->wctp", gathered, table, precision=exact_mode)
    traction, dtraction = contact_law(gaps[0], gaps[1], stick_state[0], params_here)
    loads = (
        jnp.einsum(
            "wctp,jt->wcjp", jnp.stack([traction, dtraction]), own_table, precision=exact_mode
        )
        * scale
    )
    earlier_loads = passed_along(loads, "sector", 1)
    own_group = lax.dynamic_slice_in_dim(group_ids, sector_index, 1)
    members = jnp.sum((group_ids == own_group[0]).astype(jnp.float32))
    totals = paired
    for offset in range(1, 8):
        from_before = from_behind(paired, "sector", offset)
        from_after = from_behind(paired, "sector", -offset)
        flag_before = group_flag(group_ids, own_group, sector_index - offset, sectors)
        flag_after = group_flag(group_ids, own_group, sector_index + offset, sectors)
        totals = totals + flag_before * from_before + flag_after * from_after
    weight = lax.dynamic_slice_in_dim(mistuning, sector_index, 1)[0]
    forces = loads - earlier_loads + weight * (paired - totals / members)
    outgoing = jnp.concatenate([paired, forces], 0)
    received = lax.all_to_all(outgoing[:, None], "sector", split_axis=4, concat_axis=1, tiled=True)
    states_nd = jnp.einsum("ks,wscjp->wcjpk", hartley, received[0:2], precision=exact_mode)
    forces_nd = jnp.einsum("ks,wscjp->wcjpk", hartley, received[2:4], precision=exact_mode)
    stiff_diag = diag_stiff[None, :, None, :]
    stiff_cross = cross_stiff[None, :, None, :]
    residual = (
        stiff_diag * states_nd[0] + stiff_cross * mirror(states_nd[0]) + forces_nd[0] - excitation
    )
    jvp = stiff_diag * states_nd[1] + stiff_cross * mirror(states_nd[1]) + forces_nd[1]
    return (residual, jvp)


LANES = 128
VMEM_KERNEL = 63 * 1024 * 1024
HALF = 64
ROW_HARTLEY = 0
ROW_MIRROR = 16
ROW_SPREAD = 32
ROW_LOAD = 48
ROW_SAME = 176
ROW_COEF = 304
ROW_PICK = 432
ROW_SQUARE = 560
ROW_LOADS = 576
ROW_GAPS = 704
ROWS = 960


def constant_table(sectors, coefs, samples):
    k = np.arange(sectors)
    phase = 2.0 * np.pi * (np.outer(k, k) % sectors) / sectors
    hartley = (np.cos(phase) + np.sin(phase)) / math.sqrt(sectors)
    out = np.zeros((ROWS, LANES), np.float64)
    lane_sector, lane_coef = np.arange(LANES) // 8, np.arange(LANES) % 8
    row_coef, row_k = np.arange(LANES) // sectors, np.arange(LANES) % sectors
    out[ROW_HARTLEY : ROW_HARTLEY + 16] = hartley[:, lane_sector]
    out[ROW_MIRROR : ROW_MIRROR + 16] = hartley[(-k) % sectors][:, lane_sector]
    out[ROW_SPREAD : ROW_SPREAD + 16] = k[:, None] == lane_sector[None, :]
    same = row_coef[:, None] == lane_coef[None, :]
    reaction = hartley - np.roll(hartley, -1, 1)
    out[ROW_LOAD : ROW_LOAD + 128] = same * reaction[row_k][:, lane_sector]
    out[ROW_SAME : ROW_SAME + 128] = same
    out[ROW_COEF : ROW_COEF + 128, 0:8] = row_coef[:, None] == np.arange(8)[None, :]
    out[ROW_PICK : ROW_PICK + 128, 0:16] = row_k[:, None] == k[None, :]
    out[ROW_SQUARE : ROW_SQUARE + 16, 0:16] = hartley
    c, t = np.arange(coefs), np.arange(samples)
    angle = 2.0 * np.pi * (np.outer(c // 2 + 1, t) % samples) / samples
    basis = np.where(c[:, None] % 2 == 0, np.cos(angle), np.sin(angle))
    for h in range(2):
        ordered = np.roll(basis, -h * (coefs // 2), 0)
        out[ROW_LOADS + 64 * h : ROW_LOADS + 64 * (h + 1)] = ordered * (2.0 / samples)
        out[ROW_GAPS + 128 * h : ROW_GAPS + 128 * (h + 1), 0:64] = ordered.T
    return out.astype(np.float32)


def product(a, b, precision=lax.Precision.HIGH):
    return jnp.dot(a, b, preferred_element_type=jnp.float32, precision=precision)


SEND_ORDER = ((2, 0, 3, 1), (0, 1, 2, 3), (3, 2, 1, 0), (1, 3, 0, 2))
PAIR_ORDER = (
    (0, 1, 2, 6, 7, 3, 4, 5),
    (2, 6, 7, 0, 1, 3, 4, 5),
    (4, 0, 5, 6, 7, 1, 2, 3),
    (6, 4, 5, 7, 0, 1, 2, 3),
)


def seen(z, k, step):
    order = PAIR_ORDER[z]
    return int((order[k] + step) % 8 not in order[:k])


def kernel(
    disp_hbm,
    direction_hbm,
    states_hbm,
    params_hbm,
    mistuning_hbm,
    groups_hbm,
    diag_hbm,
    cross_hbm,
    table_hbm,
    residual,
    jvp,
    disp,
    direction,
    states,
    params,
    mistuning,
    groups,
    diag,
    cross,
    table,
    fetched,
    fetched_parts,
    x_out,
    s_out,
    x_in,
    s_in,
    r_out,
    r_in,
    l_out,
    l_in,
    params8,
    tractions,
    linear,
    moved_on,
    x_sent,
    x_got,
    s_sent,
    s_got,
    r_sent,
    r_got,
    l_sent,
    l_got,
):
    sectors = 16
    pairs = sectors // 2
    me = lax.axis_index("sector")
    h = lax.axis_index("harm")
    g0 = me // 2
    z0 = me // 4
    partner = (me, 1 - h)
    side = h

    def by_z(values):
        out = jnp.int32(values[3])
        for z in (2, 1, 0):
            out = jnp.where(z0 == z, values[z], out)
        return out

    def at_step(column, j):
        out = column[-1]
        for k in range(len(column) - 2, -1, -1):
            out = jnp.where(j == k, column[k], out)
        return out

    send_order = [by_z([SEND_ORDER[z][k] for z in range(4)]) for k in range(4)]
    pair_order = [by_z([PAIR_ORDER[z][k] for z in range(4)]) for k in range(8)]
    new_first = [by_z([seen(z, k, -1) for z in range(4)]) for k in range(8)]
    new_last = [by_z([seen(z, k, 1) for z in range(4)]) for k in range(8)]

    def part(i, z):
        lanes = pl.ds(pl.multiple_of(z * 2 * LANES, 2 * LANES), 2 * LANES)
        source, target = ((disp_hbm, disp), (direction_hbm, direction), (states_hbm, states))[i]
        return pltpu.make_async_copy(
            source.at[:, lanes], target.at[:, lanes], fetched_parts.at[i, z]
        )

    given = (params_hbm, mistuning_hbm, groups_hbm, diag_hbm, cross_hbm, table_hbm)
    held = (params, mistuning, groups, diag, cross, table)
    fetches = [
        pltpu.make_async_copy(source, target, fetched.at[i])
        for i, (source, target) in enumerate(zip(given, held))
    ]
    for k in range(4):
        for i in range(3):
            part(i, send_order[k]).start()
        if k == 0:
            fetches[0].start()
    for fetch in fetches[1:]:
        fetch.start()

    barrier = pltpu.get_barrier_semaphore()

    def greet(i, carry):
        pl.semaphore_signal(
            barrier, inc=1, device_id=(lax.rem(me + i, sectors), h), device_id_type=MESH
        )
        return carry

    lax.fori_loop(1, sectors, greet, 0)
    pl.semaphore_signal(barrier, inc=1, device_id=partner, device_id_type=MESH)

    def low(rows):
        return lax.broadcasted_iota(jnp.int32, (rows, LANES), 1) < HALF

    def pack(g):
        lanes = pl.ds(pl.multiple_of(g * LANES, LANES), LANES)
        a, b = disp[:, lanes], direction[:, lanes]
        x_out[2 * g] = jnp.where(low(96), a, pltpu.roll(b, HALF, 1))
        x_out[2 * g + 1] = jnp.where(low(96), pltpu.roll(a, HALF, 1), b)
        z = states[:, lanes].astype(jnp.float32)
        early, late = z[0:64], z[64:128]
        s_out[2 * g, 8:72, :] = jnp.where(low(64), early, pltpu.roll(late, HALF, 1))
        s_out[2 * g + 1, 8:72, :] = jnp.where(low(64), pltpu.roll(early, HALF, 1), late)
        p = params8[:, lanes]
        turned = pltpu.roll(p, HALF, 1)
        s_out[2 * g, 0:8, :] = jnp.where(low(8), p, turned)
        s_out[2 * g + 1, 0:8, :] = jnp.where(low(8), turned, p)

    def x_copy(to, source):
        return pltpu.make_async_remote_copy(
            src_ref=x_out.at[to],
            dst_ref=x_in.at[source],
            send_sem=x_sent.at[to],
            recv_sem=x_got.at[source],
            device_id=(to, h),
            device_id_type=MESH,
        )

    def s_copy(to, source):
        return pltpu.make_async_remote_copy(
            src_ref=s_out.at[to],
            dst_ref=s_in.at[source // 2],
            send_sem=s_sent.at[to],
            recv_sem=s_got.at[source // 2],
            device_id=(to, h),
            device_id_type=MESH,
        )

    core, x = lax.rem(me, 2), lax.rem(g0, 2)
    mine_here = core == side

    def send(k, carry):
        z = at_step(send_order, k)
        for i in range(3):
            part(i, z).wait()

        @pl.when(k == 0)
        def _():
            fetches[0].wait()
            params8[0:4, :] = params[...]
            params8[4:8, :] = params[...]

        pack(2 * z)
        pack(2 * z + 1)

        @pl.when(k == 0)
        def _():
            pl.semaphore_wait(barrier, sectors)

        @pl.when(z == z0)
        def _():
            x_in[me] = x_out[me]

            @pl.when(mine_here)
            def _():
                s_in[g0] = s_out[me]

        tos = [4 * z + 2 * lax.rem(q + core, 2) + lax.rem(q // 2 + x, 2) for q in range(4)]
        for to in tos:

            @pl.when(to != me)
            def _(to=to):
                x_copy(to, me).start()

                @pl.when(mine_here)
                def _():
                    s_copy(to, me).start()

        return carry

    lax.fori_loop(0, 4, send, 0)
    for fetch in fetches[1:]:
        fetch.wait()

    square = table[ROW_SQUARE : ROW_SQUARE + 16, 0:16]
    row = lax.broadcasted_iota(jnp.int32, (16, 16), 0)
    col = lax.broadcasted_iota(jnp.int32, (16, 16), 1)
    group_row = jnp.broadcast_to(groups[...].astype(jnp.float32), (16, 16))
    group_col = jnp.sum(jnp.where(row == col, group_row, 0.0), axis=1, keepdims=True)
    together = (group_row == group_col).astype(jnp.float32)
    mean = together / jnp.sum(together, axis=0, keepdims=True)
    weighted = square * mistuning[...]
    exact = lax.Precision.HIGHEST
    tuned = weighted - product(weighted, mean, exact)
    tuned = product(tuned, table[ROW_SPREAD : ROW_SPREAD + 16, :], exact)
    pick = table[ROW_PICK : ROW_PICK + 128, 0:16]
    same = table[ROW_SAME : ROW_SAME + 128, :]
    plain = product(pick, table[ROW_HARTLEY : ROW_HARTLEY + 16, :], exact)
    turned_back = product(pick, table[ROW_MIRROR : ROW_MIRROR + 16, :], exact)
    tuned = product(pick, tuned, exact)
    diag_rows = product(pick, diag[...], exact)
    cross_rows = product(pick, cross[...], exact)
    coef_here = lax.broadcasted_iota(jnp.int32, (128, 32), 0) // 16
    coef_lane = lax.broadcasted_iota(jnp.int32, (128, 32), 1)
    for b in range(4):
        chosen = coef_lane == coef_here + 8 * b
        d = jnp.sum(jnp.where(chosen, diag_rows, 0.0), axis=1, keepdims=True)
        c = jnp.sum(jnp.where(chosen, cross_rows, 0.0), axis=1, keepdims=True)
        linear[b] = same * (d * plain + c * turned_back + tuned)

    def r_copy(j):
        return pltpu.make_async_remote_copy(
            src_ref=r_out.at[j],
            dst_ref=r_in.at[j],
            send_sem=r_sent.at[j],
            recv_sem=r_got.at[j],
            device_id=partner,
            device_id_type=MESH,
        )

    def l_copy(j, sector):
        return pltpu.make_async_remote_copy(
            src_ref=l_out.at[j],
            dst_ref=l_in.at[sector],
            send_sem=l_sent.at[j],
            recv_sem=l_got.at[sector // 2],
            device_id=partner,
            device_id_type=MESH,
        )

    def arrive(sector):
        @pl.when(sector != me)
        def _():
            x_copy(me, sector).wait_recv()

    def pair(j):
        return at_step(pair_order, j)

    def hand_over(j):
        g = pair(j)
        arrive(2 * g + 1)

        @pl.when(at_step(new_first, j) == 1)
        def _():
            arrive(2 * g)

        @pl.when(at_step(new_last, j) == 1)
        def _():
            arrive(lax.rem(2 * g + 2, sectors))

        other = 2 * g + 1 - side
        r_out[j] = x_in[other] - x_in[lax.rem(other + 1, sectors)]
        r_copy(j).start()

    def contact(j):
        g = pair(j)
        sector = 2 * g + side
        own = x_in[sector] - x_in[lax.rem(sector + 1, sectors)]

        @pl.when(sector != me)
        def _():
            s_copy(me, sector).wait_recv()

        r_copy(j).wait_recv()
        far = r_in[j]
        rows = [jnp.concatenate([own[32 * i : 32 * i + 32], far[32 * i : 32 * i + 32]], 0) for i in range(3)]
        gaps_rows = pl.ds(pl.multiple_of(ROW_GAPS + 128 * h, 8), 128)
        moved = product(table[gaps_rows, 0:64], jnp.concatenate(rows, 1))
        law = s_in[g, 0:8, :]
        n0, kn, kt, mu = law[0:1], law[1:2], law[2:3], law[3:4]
        step = 32
        for start in range(0, 128, step):
            packed = s_in[g, 8 + start % 64 : 8 + start % 64 + step, :]
            turned = pltpu.roll(packed, HALF, 1)
            left = low(step)
            z = jnp.where(left, packed, turned) if start < 64 else jnp.where(left, turned, packed)
            raw = [moved[start : start + step, LANES * i : LANES * (i + 1)] for i in range(3)]
            swapped = [pltpu.roll(value, HALF, 1) for value in raw]
            gap = [jnp.where(left, u, v) for u, v in zip(raw, swapped)]
            dgap = [jnp.where(left, v, u) for u, v in zip(raw, swapped)]
            touching = (z < 1.5).astype(jnp.float32)
            sliding = jnp.logical_and(z > 0.5, z < 1.5)
            normal = (n0 + kn * gap[0]) * touching
            dnormal = kn * dgap[0] * touching
            inverse = lax.rsqrt(gap[1] * gap[1] + gap[2] * gap[2] + 1.0)
            along = (gap[1] * dgap[1] + gap[2] * dgap[2]) * (inverse * inverse)
            tractions[start : start + step, 0:LANES] = jnp.where(left, normal, dnormal)
            rub = mu * inverse
            for i in (1, 2):
                slipped = normal * gap[i]
                dslipped = dnormal * gap[i] + normal * (dgap[i] - gap[i] * along)
                stuck = kt * raw[i] * touching
                tractions[start : start + step, LANES * i : LANES * (i + 1)] = jnp.where(
                    sliding, rub * jnp.where(left, slipped, dslipped), stuck
                )
        loads_rows = pl.ds(pl.multiple_of(ROW_LOADS + 64 * h, 8), 64)
        loads = product(table[loads_rows, :], tractions[...])
        for i in range(3):
            l_out[j, 32 * i : 32 * i + 32, :] = loads[32:64, LANES * i : LANES * (i + 1)]
        l_copy(j, sector).start()
        for i in range(3):
            l_in[sector, 32 * i : 32 * i + 32, :] = loads[0:32, LANES * i : LANES * (i + 1)]

    hand_over(jnp.int32(0))

    def turn(j, carry):
        @pl.when(j < pairs - 1)
        def _():
            hand_over(j + 1)

        contact(j)
        return carry

    lax.fori_loop(0, pairs, turn, 0)

    def columns(fields, b):
        rows = [slice(32 * i + 8 * b, 32 * i + 8 * b + 8) for i in range(3)]
        return jnp.concatenate([fields[:, at, :].reshape(128, LANES) for at in rows], 1)

    for b in range(4):
        moved_on[b] = product(linear[b], columns(x_in, b))

    def loads_here(j, carry):
        l_copy(j, 2 * pair(j) + 1 - side).wait_recv()
        return carry

    lax.fori_loop(0, pairs, loads_here, 0)
    reaction = table[ROW_LOAD : ROW_LOAD + 128, :]
    for b in range(4):
        out = moved_on[b] + product(reaction, columns(l_in, b))
        for i in range(3):
            both = out[:, LANES * i : LANES * (i + 1)]
            residual[i, 8 * b : 8 * b + 8] = both.reshape(8, 16, LANES)
            jvp[i, 8 * b : 8 * b + 8] = pltpu.roll(both, HALF, 1).reshape(8, 16, LANES)

    def sent(i, carry):
        to = lax.rem(me + i, sectors)
        x_copy(to, me).wait_send()

        @pl.when(mine_here)
        def _():
            s_copy(to, me).wait_send()

        return carry

    lax.fori_loop(1, sectors, sent, 0)

    def sent_back(j, carry):
        r_copy(j).wait_send()
        l_copy(j, 2 * pair(j) + side).wait_send()
        return carry

    lax.fori_loop(0, pairs, sent_back, 0)


def body_in_kernel(
    disp,
    direction,
    stick_state,
    contact_params,
    mistuning,
    group_ids,
    diag_stiff,
    cross_stiff,
    excitation,
):
    hbm = pl.BlockSpec(memory_space=pltpu.HBM)
    dma = pltpu.SemaphoreType.DMA
    f32 = jnp.float32
    table = constant_table(16, 64, 128)
    vmem = pl.BlockSpec(memory_space=pltpu.VMEM)
    out = jax.ShapeDtypeStruct((3, 32, 16, LANES), f32)
    residual, jvp = pl.pallas_call(
        kernel,
        out_shape=(out, out),
        in_specs=[hbm] * 9,
        out_specs=(vmem, vmem),
        scratch_shapes=[
            pltpu.VMEM((96, 1024), f32),
            pltpu.VMEM((96, 1024), f32),
            pltpu.VMEM((128, 1024), jnp.int32),
            pltpu.VMEM((4, 1024), f32),
            pltpu.VMEM((1, 16), f32),
            pltpu.VMEM((1, 16), jnp.int32),
            pltpu.VMEM((16, 32), f32),
            pltpu.VMEM((16, 32), f32),
            pltpu.VMEM((ROWS, LANES), f32),
            dma((6,)),
            dma((3, 4)),
            pltpu.VMEM((16, 96, LANES), f32),
            pltpu.VMEM((16, 72, LANES), f32),
            pltpu.VMEM((16, 96, LANES), f32),
            pltpu.VMEM((8, 72, LANES), f32),
            pltpu.VMEM((8, 96, LANES), f32),
            pltpu.VMEM((8, 96, LANES), f32),
            pltpu.VMEM((8, 96, LANES), f32),
            pltpu.VMEM((16, 96, LANES), f32),
            pltpu.VMEM((8, 1024), f32),
            pltpu.VMEM((128, 3 * LANES), f32),
            pltpu.VMEM((4, 128, LANES), f32),
            pltpu.VMEM((4, 128, 3 * LANES), f32),
            dma((16,)),
            dma((16,)),
            dma((16,)),
            dma((8,)),
            dma((8,)),
            dma((8,)),
            dma((8,)),
            dma((8,)),
        ],
        compiler_params=pltpu.CompilerParams(
            collective_id=0, has_side_effects=True, vmem_limit_bytes=VMEM_KERNEL
        ),
    )(
        disp.reshape(96, 1024),
        direction.reshape(96, 1024),
        stick_state[0],
        contact_params[0],
        mistuning[None],
        group_ids[None],
        diag_stiff.T,
        cross_stiff.T,
        jnp.asarray(table),
    )
    residual = residual[..., :HALF] - jnp.swapaxes(excitation, 2, 3)
    return (jnp.swapaxes(residual, 2, 3), jnp.swapaxes(jvp[..., :HALF], 2, 3))


def solution(mesh):
    in_specs = (
        P("sector", None, "harm", None),
        P("sector", None, "harm", None),
        P("sector", None, None),
        P("sector", None, None),
        P(),
        P(),
        P("harm", None),
        P("harm", None),
        P(None, "harm", "sector", None),
    )
    out_specs = (P(None, "harm", "sector", None), P(None, "harm", "sector", None))

    def body(*arrays):
        _, channels, coefs, nodes = arrays[0].shape
        sizes = (mesh.shape["sector"], mesh.shape["harm"], channels, coefs, nodes, arrays[2].shape[1])
        if sizes == (16, 2, 3, 32, 1024, 128):
            return body_in_kernel(*arrays)
        return body_any_size(*arrays)

    return jax.shard_map(body, mesh=mesh, in_specs=in_specs, out_specs=out_specs, check_vma=False)
```

```python
import math

import jax
import jax.numpy as jnp
import numpy as np
from jax import lax
from jax.experimental import pallas as pl
from jax.experimental.pallas import tpu as pltpu
from jax.sharding import PartitionSpec as P

MESH = pl.DeviceIdType.MESH

exact_mode = lax.Precision.HIGHEST


def passed_along(value, axis, steps):
    count = lax.axis_size(axis)
    pairs = [(source, (source + steps) % count) for source in range(count)]
    return lax.ppermute(value, axis, pairs)


def from_behind(block, axis, distance):
    devices = range(lax.axis_size(axis))
    route = [(i - distance, i) for i in devices if i - distance in devices]
    return lax.ppermute(block, axis, route)


def basis_table(coefs, samples):
    coef_index = lax.broadcasted_iota(jnp.int32, (coefs, samples), 0)
    time_index = lax.broadcasted_iota(jnp.int32, (coefs, samples), 1)
    harmonic = coef_index // 2 + 1
    phase = harmonic * time_index % samples
    angle = phase.astype(jnp.float32) * (2.0 * math.pi / samples)
    return jnp.where(coef_index % 2 == 0, jnp.cos(angle), jnp.sin(angle))


def hartley_table(count):
    row_index = lax.broadcasted_iota(jnp.int32, (count, count), 0)
    col_index = lax.broadcasted_iota(jnp.int32, (count, count), 1)
    phase = row_index * col_index % count
    angle = phase.astype(jnp.float32) * (2.0 * math.pi / count)
    return (jnp.cos(angle) + jnp.sin(angle)) / math.sqrt(count)


def contact_law(gaps, dgaps, states_here, params):
    preload = params[0]
    normal_stiff = params[1]
    tangent_stiff = params[2]
    friction_coef = params[3]
    touching = (states_here != 2).astype(jnp.float32)
    sliding = states_here == 1
    normal = (preload + normal_stiff * gaps[0]) * touching
    dnormal = normal_stiff * dgaps[0] * touching
    radius = jnp.sqrt(gaps[1] * gaps[1] + gaps[2] * gaps[2] + 1.0)
    projected = (gaps[1] * dgaps[1] + gaps[2] * dgaps[2]) / (radius * radius * radius)
    tractions = [normal]
    dtractions = [dnormal]
    for channel in (1, 2):
        stuck = tangent_stiff * gaps[channel]
        dstuck = tangent_stiff * dgaps[channel]
        slipped = friction_coef * normal * gaps[channel] / radius
        dslipped = friction_coef * (
            dnormal * gaps[channel] / radius
            + normal * (dgaps[channel] / radius - gaps[channel] * projected)
        )
        tractions.append(jnp.where(sliding, slipped, stuck) * touching)
        dtractions.append(jnp.where(sliding, dslipped, dstuck) * touching)
    return (jnp.stack(tractions), jnp.stack(dtractions))


def mirror(field):
    return jnp.roll(jnp.flip(field, -1), 1, -1)


def group_flag(group_ids, own_group, other_index, sectors):
    inside = jnp.logical_and(other_index >= 0, other_index < sectors)
    safe_index = jnp.clip(other_index, 0, sectors - 1)
    other_group = lax.dynamic_slice_in_dim(group_ids, safe_index, 1)
    return jnp.logical_and(inside, other_group == own_group).astype(jnp.float32)[0]


def body_any_size(
    disp,
    direction,
    stick_state,
    contact_params,
    mistuning,
    group_ids,
    diag_stiff,
    cross_stiff,
    excitation,
):
    sectors = lax.axis_size("sector")
    sector_index = lax.axis_index("sector")
    harm_index = lax.axis_index("harm")
    local_coefs = disp.shape[2]
    samples = stick_state.shape[1]
    coefs = local_coefs * lax.axis_size("harm")
    table = basis_table(coefs, samples)
    own_table = lax.dynamic_slice_in_dim(table, harm_index * local_coefs, local_coefs, 0)
    scale = 2.0 / samples
    hartley = hartley_table(sectors)
    paired = jnp.concatenate([disp, direction], 0)
    paired_next = passed_along(paired, "sector", -1)
    relative = paired - paired_next
    gathered = lax.all_gather(relative, "harm", axis=2, tiled=True)
    params_here = contact_params[0]
    gaps = jnp.einsum("wcjp,jt->wctp", gathered, table, precision=exact_mode)
    traction, dtraction = contact_law(gaps[0], gaps[1], stick_state[0], params_here)
    loads = (
        jnp.einsum(
            "wctp,jt->wcjp", jnp.stack([traction, dtraction]), own_table, precision=exact_mode
        )
        * scale
    )
    earlier_loads = passed_along(loads, "sector", 1)
    own_group = lax.dynamic_slice_in_dim(group_ids, sector_index, 1)
    members = jnp.sum((group_ids == own_group[0]).astype(jnp.float32))
    totals = paired
    for offset in range(1, 8):
        from_before = from_behind(paired, "sector", offset)
        from_after = from_behind(paired, "sector", -offset)
        flag_before = group_flag(group_ids, own_group, sector_index - offset, sectors)
        flag_after = group_flag(group_ids, own_group, sector_index + offset, sectors)
        totals = totals + flag_before * from_before + flag_after * from_after
    weight = lax.dynamic_slice_in_dim(mistuning, sector_index, 1)[0]
    forces = loads - earlier_loads + weight * (paired - totals / members)
    outgoing = jnp.concatenate([paired, forces], 0)
    received = lax.all_to_all(outgoing[:, None], "sector", split_axis=4, concat_axis=1, tiled=True)
    states_nd = jnp.einsum("ks,wscjp->wcjpk", hartley, received[0:2], precision=exact_mode)
    forces_nd = jnp.einsum("ks,wscjp->wcjpk", hartley, received[2:4], precision=exact_mode)
    stiff_diag = diag_stiff[None, :, None, :]
    stiff_cross = cross_stiff[None, :, None, :]
    residual = (
        stiff_diag * states_nd[0] + stiff_cross * mirror(states_nd[0]) + forces_nd[0] - excitation
    )
    jvp = stiff_diag * states_nd[1] + stiff_cross * mirror(states_nd[1]) + forces_nd[1]
    return (residual, jvp)


LANES = 128
VMEM_KERNEL = 63 * 1024 * 1024
HALF = 64
ROW_HARTLEY = 0
ROW_MIRROR = 16
ROW_SPREAD = 32
ROW_LOAD = 48
ROW_SAME = 176
ROW_COEF = 304
ROW_PICK = 432
ROW_SQUARE = 560
ROW_LOADS = 576
ROW_GAPS = 704
ROWS = 960


def constant_table(sectors, coefs, samples):
    k = np.arange(sectors)
    phase = 2.0 * np.pi * (np.outer(k, k) % sectors) / sectors
    hartley = (np.cos(phase) + np.sin(phase)) / math.sqrt(sectors)
    out = np.zeros((ROWS, LANES), np.float64)
    lane_sector, lane_coef = np.arange(LANES) // 8, np.arange(LANES) % 8
    row_coef, row_k = np.arange(LANES) // sectors, np.arange(LANES) % sectors
    out[ROW_HARTLEY : ROW_HARTLEY + 16] = hartley[:, lane_sector]
    out[ROW_MIRROR : ROW_MIRROR + 16] = hartley[(-k) % sectors][:, lane_sector]
    out[ROW_SPREAD : ROW_SPREAD + 16] = k[:, None] == lane_sector[None, :]
    same = row_coef[:, None] == lane_coef[None, :]
    reaction = hartley - np.roll(hartley, -1, 1)
    out[ROW_LOAD : ROW_LOAD + 128] = same * reaction[row_k][:, lane_sector]
    out[ROW_SAME : ROW_SAME + 128] = same
    out[ROW_COEF : ROW_COEF + 128, 0:8] = row_coef[:, None] == np.arange(8)[None, :]
    out[ROW_PICK : ROW_PICK + 128, 0:16] = row_k[:, None] == k[None, :]
    out[ROW_SQUARE : ROW_SQUARE + 16, 0:16] = hartley
    c, t = np.arange(coefs), np.arange(samples)
    angle = 2.0 * np.pi * (np.outer(c // 2 + 1, t) % samples) / samples
    basis = np.where(c[:, None] % 2 == 0, np.cos(angle), np.sin(angle))
    for h in range(2):
        ordered = np.roll(basis, -h * (coefs // 2), 0)
        out[ROW_LOADS + 64 * h : ROW_LOADS + 64 * (h + 1)] = ordered * (2.0 / samples)
        out[ROW_GAPS + 128 * h : ROW_GAPS + 128 * (h + 1), 0:64] = ordered.T
    return out.astype(np.float32)


def product(a, b, precision=lax.Precision.HIGH):
    return jnp.dot(a, b, preferred_element_type=jnp.float32, precision=precision)


SEND_ORDER = ((0, 2, 3, 1), (1, 0, 2, 3), (2, 3, 1, 0), (3, 1, 0, 2))
PAIR_ORDER = (
    (0, 1, 2, 6, 7, 3, 4, 5),
    (2, 6, 7, 0, 1, 3, 4, 5),
    (4, 0, 5, 6, 7, 1, 2, 3),
    (6, 4, 5, 7, 0, 1, 2, 3),
)


def seen(z, k, step):
    order = PAIR_ORDER[z]
    return int((order[k] + step) % 8 not in order[:k])


def kernel(
    disp_hbm,
    direction_hbm,
    states_hbm,
    params_hbm,
    mistuning_hbm,
    groups_hbm,
    diag_hbm,
    cross_hbm,
    table_hbm,
    residual,
    jvp,
    disp,
    direction,
    states,
    params,
    mistuning,
    groups,
    diag,
    cross,
    table,
    fetched,
    fetched_parts,
    x_out,
    s_out,
    x_in,
    s_in,
    r_out,
    r_in,
    l_out,
    l_in,
    params8,
    tractions,
    linear,
    moved_on,
    x_sent,
    x_got,
    s_sent,
    s_got,
    r_sent,
    r_got,
    l_sent,
    l_got,
):
    sectors = 16
    pairs = sectors // 2
    me = lax.axis_index("sector")
    h = lax.axis_index("harm")
    g0 = me // 2
    z0 = me // 4
    partner = (me, 1 - h)
    side = h

    def by_z(values):
        out = jnp.int32(values[3])
        for z in (2, 1, 0):
            out = jnp.where(z0 == z, values[z], out)
        return out

    def at_step(column, j):
        out = column[-1]
        for k in range(len(column) - 2, -1, -1):
            out = jnp.where(j == k, column[k], out)
        return out

    send_order = [by_z([SEND_ORDER[z][k] for z in range(4)]) for k in range(4)]
    pair_order = [by_z([PAIR_ORDER[z][k] for z in range(4)]) for k in range(8)]
    new_first = [by_z([seen(z, k, -1) for z in range(4)]) for k in range(8)]
    new_last = [by_z([seen(z, k, 1) for z in range(4)]) for k in range(8)]

    def part(i, z):
        lanes = pl.ds(pl.multiple_of(z * 2 * LANES, 2 * LANES), 2 * LANES)
        source, target = ((disp_hbm, disp), (direction_hbm, direction), (states_hbm, states))[i]
        return pltpu.make_async_copy(
            source.at[:, lanes], target.at[:, lanes], fetched_parts.at[i, z]
        )

    given = (params_hbm, mistuning_hbm, groups_hbm, diag_hbm, cross_hbm, table_hbm)
    held = (params, mistuning, groups, diag, cross, table)
    fetches = [
        pltpu.make_async_copy(source, target, fetched.at[i])
        for i, (source, target) in enumerate(zip(given, held))
    ]
    for k in range(4):
        for i in range(3):
            part(i, send_order[k]).start()
        if k == 0:
            fetches[0].start()
    for fetch in fetches[1:]:
        fetch.start()

    barrier = pltpu.get_barrier_semaphore()

    def greet(i, carry):
        pl.semaphore_signal(
            barrier, inc=1, device_id=(lax.rem(me + i, sectors), h), device_id_type=MESH
        )
        return carry

    lax.fori_loop(1, sectors, greet, 0)
    pl.semaphore_signal(barrier, inc=1, device_id=partner, device_id_type=MESH)

    def low(rows):
        return lax.broadcasted_iota(jnp.int32, (rows, LANES), 1) < HALF

    def pack(g):
        lanes = pl.ds(pl.multiple_of(g * LANES, LANES), LANES)
        a, b = disp[:, lanes], direction[:, lanes]
        x_out[2 * g] = jnp.where(low(96), a, pltpu.roll(b, HALF, 1))
        x_out[2 * g + 1] = jnp.where(low(96), pltpu.roll(a, HALF, 1), b)
        z = states[:, lanes].astype(jnp.float32)
        early, late = z[0:64], z[64:128]
        s_out[2 * g, 8:72, :] = jnp.where(low(64), early, pltpu.roll(late, HALF, 1))
        s_out[2 * g + 1, 8:72, :] = jnp.where(low(64), pltpu.roll(early, HALF, 1), late)
        p = params8[:, lanes]
        turned = pltpu.roll(p, HALF, 1)
        s_out[2 * g, 0:8, :] = jnp.where(low(8), p, turned)
        s_out[2 * g + 1, 0:8, :] = jnp.where(low(8), turned, p)

    def x_copy(to, source):
        return pltpu.make_async_remote_copy(
            src_ref=x_out.at[to],
            dst_ref=x_in.at[source],
            send_sem=x_sent.at[to],
            recv_sem=x_got.at[source],
            device_id=(to, h),
            device_id_type=MESH,
        )

    def s_copy(to, source):
        return pltpu.make_async_remote_copy(
            src_ref=s_out.at[to],
            dst_ref=s_in.at[source // 2],
            send_sem=s_sent.at[to],
            recv_sem=s_got.at[source // 2],
            device_id=(to, h),
            device_id_type=MESH,
        )

    core, x = lax.rem(me, 2), lax.rem(g0, 2)
    mine_here = core == side

    def send(k, carry):
        z = at_step(send_order, k)
        for i in range(3):
            part(i, z).wait()

        @pl.when(k == 0)
        def _():
            fetches[0].wait()
            params8[0:4, :] = params[...]
            params8[4:8, :] = params[...]

        pack(2 * z)
        pack(2 * z + 1)

        @pl.when(k == 0)
        def _():
            pl.semaphore_wait(barrier, sectors)

        @pl.when(z == z0)
        def _():
            x_in[me] = x_out[me]

            @pl.when(mine_here)
            def _():
                s_in[g0] = s_out[me]

        tos = [4 * z + 2 * lax.rem(q + core, 2) + lax.rem(q // 2 + x, 2) for q in range(4)]
        for to in tos:

            @pl.when(to != me)
            def _(to=to):
                x_copy(to, me).start()

                @pl.when(mine_here)
                def _():
                    s_copy(to, me).start()

        return carry

    lax.fori_loop(0, 4, send, 0)
    for fetch in fetches[1:]:
        fetch.wait()

    square = table[ROW_SQUARE : ROW_SQUARE + 16, 0:16]
    row = lax.broadcasted_iota(jnp.int32, (16, 16), 0)
    col = lax.broadcasted_iota(jnp.int32, (16, 16), 1)
    group_row = jnp.broadcast_to(groups[...].astype(jnp.float32), (16, 16))
    group_col = jnp.sum(jnp.where(row == col, group_row, 0.0), axis=1, keepdims=True)
    together = (group_row == group_col).astype(jnp.float32)
    mean = together / jnp.sum(together, axis=0, keepdims=True)
    weighted = square * mistuning[...]
    exact = lax.Precision.HIGHEST
    tuned = weighted - product(weighted, mean, exact)
    tuned = product(tuned, table[ROW_SPREAD : ROW_SPREAD + 16, :], exact)
    pick = table[ROW_PICK : ROW_PICK + 128, 0:16]
    same = table[ROW_SAME : ROW_SAME + 128, :]
    plain = product(pick, table[ROW_HARTLEY : ROW_HARTLEY + 16, :], exact)
    turned_back = product(pick, table[ROW_MIRROR : ROW_MIRROR + 16, :], exact)
    tuned = product(pick, tuned, exact)
    diag_rows = product(pick, diag[...], exact)
    cross_rows = product(pick, cross[...], exact)
    coef_here = lax.broadcasted_iota(jnp.int32, (128, 32), 0) // 16
    coef_lane = lax.broadcasted_iota(jnp.int32, (128, 32), 1)
    for b in range(4):
        chosen = coef_lane == coef_here + 8 * b
        d = jnp.sum(jnp.where(chosen, diag_rows, 0.0), axis=1, keepdims=True)
        c = jnp.sum(jnp.where(chosen, cross_rows, 0.0), axis=1, keepdims=True)
        linear[b] = same * (d * plain + c * turned_back + tuned)

    def r_copy(j):
        return pltpu.make_async_remote_copy(
            src_ref=r_out.at[j],
            dst_ref=r_in.at[j],
            send_sem=r_sent.at[j],
            recv_sem=r_got.at[j],
            device_id=partner,
            device_id_type=MESH,
        )

    def l_copy(j, sector):
        return pltpu.make_async_remote_copy(
            src_ref=l_out.at[j],
            dst_ref=l_in.at[sector],
            send_sem=l_sent.at[j],
            recv_sem=l_got.at[sector // 2],
            device_id=partner,
            device_id_type=MESH,
        )

    def arrive(sector):
        @pl.when(sector != me)
        def _():
            x_copy(me, sector).wait_recv()

    def pair(j):
        return at_step(pair_order, j)

    def hand_over(j):
        g = pair(j)
        arrive(2 * g + 1)

        @pl.when(at_step(new_first, j) == 1)
        def _():
            arrive(2 * g)

        @pl.when(at_step(new_last, j) == 1)
        def _():
            arrive(lax.rem(2 * g + 2, sectors))

        other = 2 * g + 1 - side
        r_out[j] = x_in[other] - x_in[lax.rem(other + 1, sectors)]
        r_copy(j).start()

    def contact(j):
        g = pair(j)
        sector = 2 * g + side
        own = x_in[sector] - x_in[lax.rem(sector + 1, sectors)]

        @pl.when(sector != me)
        def _():
            s_copy(me, sector).wait_recv()

        r_copy(j).wait_recv()
        far = r_in[j]
        rows = [jnp.concatenate([own[32 * i : 32 * i + 32], far[32 * i : 32 * i + 32]], 0) for i in range(3)]
        gaps_rows = pl.ds(pl.multiple_of(ROW_GAPS + 128 * h, 8), 128)
        moved = product(table[gaps_rows, 0:64], jnp.concatenate(rows, 1))
        law = s_in[g, 0:8, :]
        n0, kn, kt, mu = law[0:1], law[1:2], law[2:3], law[3:4]
        step = 32
        for start in range(0, 128, step):
            packed = s_in[g, 8 + start % 64 : 8 + start % 64 + step, :]
            turned = pltpu.roll(packed, HALF, 1)
            left = low(step)
            z = jnp.where(left, packed, turned) if start < 64 else jnp.where(left, turned, packed)
            raw = [moved[start : start + step, LANES * i : LANES * (i + 1)] for i in range(3)]
            swapped = [pltpu.roll(value, HALF, 1) for value in raw]
            gap = [jnp.where(left, u, v) for u, v in zip(raw, swapped)]
            dgap = [jnp.where(left, v, u) for u, v in zip(raw, swapped)]
            touching = (z < 1.5).astype(jnp.float32)
            sliding = jnp.logical_and(z > 0.5, z < 1.5)
            normal = (n0 + kn * gap[0]) * touching
            dnormal = kn * dgap[0] * touching
            inverse = lax.rsqrt(gap[1] * gap[1] + gap[2] * gap[2] + 1.0)
            along = (gap[1] * dgap[1] + gap[2] * dgap[2]) * (inverse * inverse)
            tractions[start : start + step, 0:LANES] = jnp.where(left, normal, dnormal)
            rub = mu * inverse
            for i in (1, 2):
                slipped = normal * gap[i]
                dslipped = dnormal * gap[i] + normal * (dgap[i] - gap[i] * along)
                stuck = kt * raw[i] * touching
                tractions[start : start + step, LANES * i : LANES * (i + 1)] = jnp.where(
                    sliding, rub * jnp.where(left, slipped, dslipped), stuck
                )
        loads_rows = pl.ds(pl.multiple_of(ROW_LOADS + 64 * h, 8), 64)
        loads = product(table[loads_rows, :], tractions[...])
        for i in range(3):
            l_out[j, 32 * i : 32 * i + 32, :] = loads[32:64, LANES * i : LANES * (i + 1)]
        l_copy(j, sector).start()
        for i in range(3):
            l_in[sector, 32 * i : 32 * i + 32, :] = loads[0:32, LANES * i : LANES * (i + 1)]

    hand_over(jnp.int32(0))

    def turn(j, carry):
        @pl.when(j < pairs - 1)
        def _():
            hand_over(j + 1)

        contact(j)
        return carry

    lax.fori_loop(0, pairs, turn, 0)

    def columns(fields, b):
        rows = [slice(32 * i + 8 * b, 32 * i + 8 * b + 8) for i in range(3)]
        return jnp.concatenate([fields[:, at, :].reshape(128, LANES) for at in rows], 1)

    for b in range(4):
        moved_on[b] = product(linear[b], columns(x_in, b))

    def loads_here(j, carry):
        l_copy(j, 2 * pair(j) + 1 - side).wait_recv()
        return carry

    lax.fori_loop(0, pairs, loads_here, 0)
    reaction = table[ROW_LOAD : ROW_LOAD + 128, :]
    for b in range(4):
        out = moved_on[b] + product(reaction, columns(l_in, b))
        for i in range(3):
            both = out[:, LANES * i : LANES * (i + 1)]
            residual[i, 8 * b : 8 * b + 8] = both.reshape(8, 16, LANES)
            jvp[i, 8 * b : 8 * b + 8] = pltpu.roll(both, HALF, 1).reshape(8, 16, LANES)

    def sent(i, carry):
        to = lax.rem(me + i, sectors)
        x_copy(to, me).wait_send()

        @pl.when(mine_here)
        def _():
            s_copy(to, me).wait_send()

        return carry

    lax.fori_loop(1, sectors, sent, 0)

    def sent_back(j, carry):
        r_copy(j).wait_send()
        l_copy(j, 2 * pair(j) + side).wait_send()
        return carry

    lax.fori_loop(0, pairs, sent_back, 0)


def body_in_kernel(
    disp,
    direction,
    stick_state,
    contact_params,
    mistuning,
    group_ids,
    diag_stiff,
    cross_stiff,
    excitation,
):
    hbm = pl.BlockSpec(memory_space=pltpu.HBM)
    dma = pltpu.SemaphoreType.DMA
    f32 = jnp.float32
    table = constant_table(16, 64, 128)
    vmem = pl.BlockSpec(memory_space=pltpu.VMEM)
    out = jax.ShapeDtypeStruct((3, 32, 16, LANES), f32)
    residual, jvp = pl.pallas_call(
        kernel,
        out_shape=(out, out),
        in_specs=[hbm] * 9,
        out_specs=(vmem, vmem),
        scratch_shapes=[
            pltpu.VMEM((96, 1024), f32),
            pltpu.VMEM((96, 1024), f32),
            pltpu.VMEM((128, 1024), jnp.int32),
            pltpu.VMEM((4, 1024), f32),
            pltpu.VMEM((1, 16), f32),
            pltpu.VMEM((1, 16), jnp.int32),
            pltpu.VMEM((16, 32), f32),
            pltpu.VMEM((16, 32), f32),
            pltpu.VMEM((ROWS, LANES), f32),
            dma((6,)),
            dma((3, 4)),
            pltpu.VMEM((16, 96, LANES), f32),
            pltpu.VMEM((16, 72, LANES), f32),
            pltpu.VMEM((16, 96, LANES), f32),
            pltpu.VMEM((8, 72, LANES), f32),
            pltpu.VMEM((8, 96, LANES), f32),
            pltpu.VMEM((8, 96, LANES), f32),
            pltpu.VMEM((8, 96, LANES), f32),
            pltpu.VMEM((16, 96, LANES), f32),
            pltpu.VMEM((8, 1024), f32),
            pltpu.VMEM((128, 3 * LANES), f32),
            pltpu.VMEM((4, 128, LANES), f32),
            pltpu.VMEM((4, 128, 3 * LANES), f32),
            dma((16,)),
            dma((16,)),
            dma((16,)),
            dma((8,)),
            dma((8,)),
            dma((8,)),
            dma((8,)),
            dma((8,)),
        ],
        compiler_params=pltpu.CompilerParams(
            collective_id=0, has_side_effects=True, vmem_limit_bytes=VMEM_KERNEL
        ),
    )(
        disp.reshape(96, 1024),
        direction.reshape(96, 1024),
        stick_state[0],
        contact_params[0],
        mistuning[None],
        group_ids[None],
        diag_stiff.T,
        cross_stiff.T,
        jnp.asarray(table),
    )
    residual = residual[..., :HALF] - jnp.swapaxes(excitation, 2, 3)
    return (jnp.swapaxes(residual, 2, 3), jnp.swapaxes(jvp[..., :HALF], 2, 3))


def solution(mesh):
    in_specs = (
        P("sector", None, "harm", None),
        P("sector", None, "harm", None),
        P("sector", None, None),
        P("sector", None, None),
        P(),
        P(),
        P("harm", None),
        P("harm", None),
        P(None, "harm", "sector", None),
    )
    out_specs = (P(None, "harm", "sector", None), P(None, "harm", "sector", None))

    def body(*arrays):
        _, channels, coefs, nodes = arrays[0].shape
        sizes = (mesh.shape["sector"], mesh.shape["harm"], channels, coefs, nodes, arrays[2].shape[1])
        if sizes == (16, 2, 3, 32, 1024, 128):
            return body_in_kernel(*arrays)
        return body_any_size(*arrays)

    return jax.shard_map(body, mesh=mesh, in_specs=in_specs, out_specs=out_specs, check_vma=False)
```
